32 devices in a mesh: shard: 8 (over y, x, core), context: 2 (over z_hi), tensor: 2 (over z_lo).
Axes of the slice: x: 2, y: 2, z: 4 (z_hi: 2, z_lo: 2; z = z_hi * 2 + z_lo), core: 2. Of those that a mesh axis runs over, the one named last changes fastest.
Arguments:
- hidden_in: bfloat16 [8192, 2048], P(('shard', 'context', 'tensor')), may hold values from -7 to 7
- cotangent: bfloat16 [8192, 2048], P(('shard', 'context', 'tensor')), may hold values from -6 to 6
- w_query: bfloat16 [2048, 2048], P('shard', ('context', 'tensor')), may hold values from -0.65 to 0.65
- w_key: bfloat16 [2048, 2048], P('shard', ('context', 'tensor')), may hold values from -0.9 to 0.9
- w_value: bfloat16 [2048, 2048], P('shard', ('context', 'tensor')), may hold values from -0.125 to 0.125
- w_out: bfloat16 [2048, 2048], P('shard', ('context', 'tensor')), may hold values from -1.42 to 1.42
- w_router: bfloat16 [2048, 16], P(('shard', 'context', 'tensor')), may hold values from -2.7 to 2.7
- norm_first: bfloat16 [2048], P(('shard', 'context', 'tensor')), may hold values from 0.25 to 1.75
- norm_second: bfloat16 [2048], P(('shard', 'context', 'tensor')), may hold values from 0.25 to 1.75
- query_gain: bfloat16 [2048], P(('shard', 'context', 'tensor')), may hold values from 0.45 to 6
- key_gain: bfloat16 [2048], P(('shard', 'context', 'tensor')), may hold values from 0.45 to 6
- w_gate: bfloat16 [16, 2048, 1024], P(('shard', 'context'), None, 'tensor'), may hold values from -0.125 to 0.125
- w_up: bfloat16 [16, 2048, 1024], P(('shard', 'context'), None, 'tensor'), may hold values from -0.125 to 0.125
- w_down: bfloat16 [16, 2048, 1024], P(('shard', 'context'), None, 'tensor'), may hold values from -2 to 2
- expert_ids: int32 [8192, 8], P(('shard', 'context', 'tensor')), may hold values from 0 to 15, all different within a row; in each aligned block of 256 rows (0 to 255, 256 to 511, ...) at most 160 rows name the same one
Outputs:
- block_output: bfloat16 [8192, 2048], P(('shard', 'context', 'tensor'))
- grad_input: float32 [8192, 2048], P(('shard', 'context', 'tensor'))
- grad_query: float32 [2048, 2048], P('shard', ('context', 'tensor'))
- grad_key: float32 [2048, 2048], P('shard', ('context', 'tensor'))
- grad_value: float32 [2048, 2048], P('shard', ('context', 'tensor'))
- grad_out: float32 [2048, 2048], P('shard', ('context', 'tensor'))
- grad_router: float32 [2048, 16], P(('shard', 'context', 'tensor'))
- grad_norm_first: float32 [2048], P(('shard', 'context', 'tensor'))
- grad_norm_second: float32 [2048], P(('shard', 'context', 'tensor'))
- grad_query_gain: float32 [2048], P(('shard', 'context', 'tensor'))
- grad_key_gain: float32 [2048], P(('shard', 'context', 'tensor'))
- grad_gate: float32 [16, 2048, 1024], P(('shard', 'context'), None, 'tensor')
- grad_up: float32 [16, 2048, 1024], P(('shard', 'context'), None, 'tensor')
- grad_down: float32 [16, 2048, 1024], P(('shard', 'context'), None, 'tensor')
The draws below stay inside these ranges and needn't reach their ends.
Inputs may be any that keep to these rules, and one draw needn't show every extreme that they name: `expert_ids`: each row names 8 different experts. Within the rows of one device no expert is named by more than 160 rows, and in some device's rows one expert is named by exactly 160.
All inputs are finite; a program needn't handle non-finite values.
Results may differ from the reference program's by a relative error of at most 0.023.
Values may be sent and summed in bfloat16 or wider, within the bound.
No kernel may reach another device: no remote copies, remote signals or barrier semaphores. Data moves between devices by JAX's collectives and lax.ppermute only.
A program may use at most 256 MiB of HBM per device.

```python
import math
import jax
import jax.numpy as jnp
import numpy as np
from jax import lax

D = 2048
HEADS = 16
HDIM = 128
FFE = 1024
TOP = 8
SEQ_LEN = 1024
TOK_DEV = 256
TOKENS = 8192
EXPERTS = 16
CAP = 160
N_SHARD = 8
N_CONTEXT = 2
N_TENSOR = 2


def column_scale():
    return 3.0 ** (jnp.arange(D, dtype=jnp.float32) / D - 0.5)


def shared_projection(key):
    base_draw = jax.random.truncated_normal(jax.random.fold_in(key, 51), -4.0, 4.0, (D, D), jnp.float32)
    return base_draw * D ** (-0.5) * column_scale()[None, :]


def draw_hidden_in(key, part):
    noise_draw = jax.random.truncated_normal(jax.random.fold_in(key, 71), -6.0, 6.0, (TOKENS, D), jnp.float32)
    return noise_draw.astype(jnp.bfloat16)


def draw_w_query(key, part):
    return shared_projection(key).astype(jnp.bfloat16)


def draw_w_key(key, part):
    own_draw = jax.random.truncated_normal(jax.random.fold_in(key, 52), -4.0, 4.0, (D, D), jnp.float32) * D ** (-0.5) * column_scale()[None, :]
    return own_draw.astype(jnp.bfloat16)


def draw_w_out(key, part):
    base_draw = jax.random.truncated_normal(jax.random.fold_in(key, 81), -4.0, 4.0, (D, D), jnp.float32) * (D // 16) ** (-0.5)
    return base_draw.astype(jnp.bfloat16)


def draw_w_router(key, part):
    noise_part = jax.random.truncated_normal(jax.random.fold_in(key, 61), -4.0, 4.0, (D, EXPERTS), jnp.float32) * 0.5 * D ** (-0.5)
    return noise_part.astype(jnp.bfloat16)


def draw_query_gain(key, part):
    values_drawn = jnp.exp(jax.random.uniform(jax.random.fold_in(key, 44), (D,), jnp.float32, math.log(0.5), math.log(2.0)))
    return values_drawn.astype(jnp.bfloat16)


def draw_key_gain(key, part):
    values_drawn = jnp.exp(jax.random.uniform(jax.random.fold_in(key, 45), (D,), jnp.float32, math.log(0.5), math.log(2.0)))
    return values_drawn.astype(jnp.bfloat16)


def levels(stream_key, extent, pieces, low, largest):
    def one(axis_at, shards_of):
        draws = jax.random.uniform(jax.random.fold_in(jax.random.fold_in(stream_key, 6), axis_at), (shards_of,), jnp.float32, low / len(pieces), largest / len(pieces))
        return jnp.repeat(jnp.exp(draws), extent[axis_at] // shards_of).reshape((-1,) + (1,) * (len(extent) - axis_at - 1))

    level = one(*pieces[0])
    for cut in pieces[1:]:
        level = level * one(*cut)
    return level


def deal_out(own_key, own, number, rows, count, top, limit, skew):
    order = jax.random.permutation(own_key, count)
    heavy_load, common = load_shares(count, rows * top, limit, skew, True), load_shares(count, rows * top, limit, skew, False)
    places = jnp.arange(count)

    def named(lengths, turn):
        used = int((lengths > 0).sum())
        fixed = max(1, used // 4)
        passed = fixed + (places - fixed + turn * (used - fixed)) % max(1, count - fixed)
        return jnp.zeros((count,), jnp.int32).at[order[jnp.where(places < fixed, places, passed)]].set(jnp.asarray(lengths, jnp.int32))

    lengths = jnp.where(number % 4 == 0, named(heavy_load, number // 4), named(common, number - number // 4 - 1))
    mixed = jax.random.permutation(jax.random.fold_in(own, 3), count)
    donor, receiver = mixed[0:count // 2 * 2:2], mixed[1:count // 2 * 2:2]
    slack = jnp.minimum(lengths[donor] - 1, limit - lengths[receiver]) // 2
    slack = jnp.where((donor == order[0]) | (receiver == order[0]) | (lengths[receiver] == 0), 0, jnp.maximum(slack, 0))
    passed = jax.random.randint(jax.random.fold_in(own, 4), (count // 2,), 0, 1 << 20) % (slack + 1)
    lengths = lengths.at[donor].add(-passed).at[receiver].add(passed)
    members = jnp.searchsorted(jnp.cumsum(lengths), jnp.arange(rows * top), side="right").astype(jnp.int32)
    grid = members.reshape(top, rows).T
    grid = grid[jax.random.permutation(jax.random.fold_in(own, 1), rows)]
    turn = jax.random.randint(jax.random.fold_in(own, 2), (rows, 1), 0, top)
    return jnp.take_along_axis(grid, (jnp.arange(top)[None, :] + turn) % top, axis=1)


def load_shares(number_of, total, most, skew, full):
    loads = [(1 << 20) // math.isqrt(standing ** skew) + 1 for standing in range(1, number_of + 1)]
    largest = most if full else min(most, max(-(-total // number_of), total * loads[0] // sum(loads)))
    least = 1 if total - largest >= number_of - 1 else 0
    holding, rest = [largest] + [least] * (number_of - 1), total - largest - least * (number_of - 1)
    while rest > 0:
        movable = [i for i in range(1, number_of) if holding[i] < largest] or [i for i in range(1, number_of) if holding[i] < most]
        whole, budget = sum([loads[i] for i in movable]), rest
        for i in movable:
            more = min(most - holding[i], max(1, budget * loads[i] // whole), rest)
            holding[i] = holding[i] + more
            rest = rest - more
    return np.array(holding)


def centred(own_key, dims, scale, most, shards=(), held_as=jnp.bfloat16):
    drawn = jax.random.normal(own_key, dims, jnp.float32) * scale
    if len(shards) > 0:
        drawn = levels(own_key, dims, shards, -0.22, 0.18) * drawn
    return jnp.clip(drawn, min=-most, max=most).astype(held_as)


def setup_inputs(seed: int = 0) -> dict:
    seeds = jax.random.split(jax.random.key(seed), 16)
    hidden_in = draw_hidden_in(jax.random.fold_in(seeds[15], 71), 0)
    cotangent = centred(seeds[1], (TOKENS, D), 1.0, 6.0, ((0, 32),))
    w_query = draw_w_query(jax.random.fold_in(seeds[15], 71), 0)
    w_key = draw_w_key(jax.random.fold_in(seeds[15], 71), 0)
    w_value = centred(seeds[4], (D, D), D ** -0.5, 0.125, ((0, 8), (1, 4)))
    w_out = draw_w_out(jax.random.fold_in(seeds[15], 71), 0)
    w_router = draw_w_router(jax.random.fold_in(seeds[15], 71), 0)
    norm_first = jnp.clip(1.0 + 0.15 * jax.random.normal(seeds[7], (D,), jnp.float32), 0.25, 1.75).astype(jnp.bfloat16)
    norm_second = jnp.clip(1.0 + 0.15 * jax.random.normal(seeds[8], (D,), jnp.float32), 0.25, 1.75).astype(jnp.bfloat16)
    query_gain = draw_query_gain(jax.random.fold_in(seeds[15], 71), 0)
    key_gain = draw_key_gain(jax.random.fold_in(seeds[15], 71), 0)
    w_gate = centred(seeds[11], (EXPERTS, D, FFE), D ** -0.5, 0.125, ((0, 16), (2, 2)))
    w_up = centred(seeds[12], (EXPERTS, D, FFE), D ** -0.5, 0.125, ((0, 16), (2, 2)))
    w_down = centred(seeds[13], (EXPERTS, D, FFE), (max(1, 2 * FFE // (EXPERTS * EXPERTS))) ** -0.5, 2.0, ((0, 16), (2, 2)))
    expert_ids_keys = jax.random.split(jax.random.fold_in(seeds[14], 1), TOKENS // TOK_DEV)
    expert_ids_turns = jax.random.permutation(jax.random.fold_in(seeds[14], 3), TOKENS // TOK_DEV)
    expert_ids = jax.vmap(lambda own, number: deal_out(jax.random.fold_in(seeds[14], 2), own, number, TOK_DEV, EXPERTS, TOP, CAP, 1))(expert_ids_keys, expert_ids_turns).reshape((TOKENS, TOP))
    return dict(hidden_in=hidden_in, cotangent=cotangent, w_query=w_query, w_key=w_key, w_value=w_value, w_out=w_out, w_router=w_router, norm_first=norm_first, norm_second=norm_second, query_gain=query_gain, key_gain=key_gain, w_gate=w_gate, w_up=w_up, w_down=w_down, expert_ids=expert_ids)


@jax.custom_vjp
def low(v):
    return lax.optimization_barrier(v.astype(jnp.bfloat16)).astype(jnp.float32)

@jax.custom_vjp
def low_back(v):
    return v

def low_keep(v):
    return (low(v), None)

def low_pass(kept, grad):
    return (grad,)

def back_keep(v):
    return (v, None)

def back_low(kept, grad):
    return (low(grad),)
low.defvjp(low_keep, low_pass)
low_back.defvjp(back_keep, back_low)
EPSILON = 1e-05
HIGHEST = lax.Precision.HIGHEST

def matmul(left, right):
    return jnp.dot(left, right, precision=HIGHEST, preferred_element_type=jnp.float32)

def contract_last(left, right):
    return lax.dot_general(left, right, (((1,), (1,)), ((), ())), precision=HIGHEST, preferred_element_type=jnp.float32)

def rms_scale(values, gain):
    return values * lax.rsqrt(lax.optimization_barrier(jnp.mean(values * values, axis=-1, keepdims=True)) + EPSILON) * gain

def rotate(values, cosine_table, sine_table):
    half_size = values.shape[-1] // 2
    first_half = values[..., :half_size]
    second_half = values[..., half_size:]
    return jnp.concatenate([first_half * cosine_table - second_half * sine_table, second_half * cosine_table + first_half * sine_table], axis=-1)

def softmax_last(scores):
    maximum = lax.optimization_barrier(jnp.max(scores, axis=-1, keepdims=True))
    weights = jnp.exp(scores - maximum)
    return weights / lax.optimization_barrier(jnp.sum(weights, axis=-1, keepdims=True))

def attend_sequence(packed):
    queries, key_vectors, value_vectors = packed
    length = queries.shape[0]
    scores = low_back(jnp.einsum('qhd,khd->hqk', queries, key_vectors, precision=HIGHEST) * HDIM ** (-0.5))
    causal = jnp.arange(length, dtype=jnp.int32)[:, None] >= jnp.arange(length, dtype=jnp.int32)[None, :]
    attn_probs = low(softmax_last(jnp.where(causal[None], scores, -1e+30)))
    return jnp.einsum('hqk,khd->qhd', attn_probs, value_vectors, precision=HIGHEST)

def slot_tables(expert_ids):
    devices = N_SHARD * N_CONTEXT * N_TENSOR
    routes = expert_ids.reshape(devices, TOK_DEV * TOP)
    onehot = (routes[:, :, None] == jnp.arange(EXPERTS, dtype=jnp.int32)[None, None, :]).astype(jnp.int32)
    before = jnp.cumsum(onehot, axis=1) - onehot
    position = lax.optimization_barrier(jnp.sum(before * onehot, axis=2))
    device = jnp.arange(devices, dtype=jnp.int32)[:, None]
    column = (device * CAP + position).reshape(-1)
    route_slot = routes.reshape(-1) * (devices * CAP) + column
    slot_table = jnp.full((EXPERTS * devices * CAP,), TOKENS, jnp.int32)
    slot_table = slot_table.at[route_slot].set(jnp.arange(TOKENS * TOP, dtype=jnp.int32) // TOP)
    return (route_slot.reshape(TOKENS, TOP), slot_table.reshape(EXPERTS, devices * CAP))

def expert_rows(packed, padded):
    index_row, gate_weight, up_weight, down_weight = packed
    rows_in = low_back(padded[index_row])
    gate_act = low_back(matmul(rows_in, gate_weight))
    up_act = low_back(matmul(rows_in, up_weight))
    hidden_act = low(gate_act * jax.nn.sigmoid(gate_act) * up_act)
    return low_back(low(contract_last(hidden_act, down_weight)))

def reference(hidden_in, cotangent, w_query, w_key, w_value, w_out, w_router, norm_first, norm_second, query_gain, key_gain, w_gate, w_up, w_down, expert_ids):
    route_slot, slot_table = slot_tables(expert_ids)
    sequences = TOKENS // SEQ_LEN
    frequency = 10000.0 ** (-2.0 * jnp.arange(HDIM // 2, dtype=jnp.float32) / HDIM)
    angles = jnp.arange(SEQ_LEN, dtype=jnp.float32)[:, None] * frequency[None, :]
    cosine_table = jnp.cos(angles)[None, :, None, :]
    sine_table = jnp.sin(angles)[None, :, None, :]
    head_shape = (sequences, SEQ_LEN, HEADS, HDIM)

    def forward(hidden, query_weight, key_weight, value_weight, out_weight, router_weight, gain_first, gain_second, gain_query, gain_key, gate_all, up_all, down_all):
        normed_first = low(rms_scale(hidden, gain_first))
        query_pre = low_back(matmul(normed_first, query_weight))
        key_pre = low_back(matmul(normed_first, key_weight))
        values = low_back(low(matmul(normed_first, value_weight)))
        queries = low_back(low(rotate(rms_scale(query_pre, gain_query).reshape(head_shape), cosine_table, sine_table)))
        key_vectors = low_back(low(rotate(rms_scale(key_pre, gain_key).reshape(head_shape), cosine_table, sine_table)))
        attended = lax.map(jax.checkpoint(attend_sequence), (queries, key_vectors, values.reshape(head_shape)))
        attended = low_back(low(attended.reshape(TOKENS, D)))
        middle = hidden + low_back(contract_last(attended, out_weight))
        normed_second = low(rms_scale(middle, gain_second))
        router_probs = softmax_last(low_back(matmul(normed_second, router_weight)))
        gate_probs = jnp.take_along_axis(router_probs, expert_ids, axis=1)
        padded = jnp.concatenate([normed_second, jnp.zeros((1, D), jnp.float32)], axis=0)

        def one_expert(packed):
            return expert_rows(packed, padded)
        produced = lax.map(jax.checkpoint(one_expert), (slot_table, gate_all, up_all, down_all))
        chosen = produced.reshape(-1, D)[route_slot]
        return middle + lax.optimization_barrier(jnp.sum(gate_probs[:, :, None] * chosen, axis=1))
    float_args = tuple((argument.astype(jnp.float32) for argument in (hidden_in, w_query, w_key, w_value, w_out, w_router, norm_first, norm_second, query_gain, key_gain, w_gate, w_up, w_down)))
    result, pullback = jax.vjp(forward, *float_args)
    gradients = pullback(cotangent.astype(jnp.float32))
    return (result.astype(jnp.bfloat16), gradients[0], gradients[1], gradients[2], gradients[3], gradients[4], gradients[5], gradients[6], gradients[7], gradients[8], gradients[9], gradients[10], gradients[11], gradients[12])
```

```python
import jax
import jax.numpy as jnp
from jax import lax
from jax.sharding import PartitionSpec as P

HDIM = 128
SEQ_LEN = 1024


EPSILON = 1e-05
MASKED = -1e30
LOW = jnp.bfloat16
WIDE = jnp.float32
SWAP = ((0, 1), (1, 0))


def rms_scale(values, gain):
    factor = lax.rsqrt(jnp.mean(values * values, axis=-1, keepdims=True) + EPSILON)
    return (values * factor * gain, factor)


def rms_back(values, factor, gain, grad_out):
    scaled = grad_out * gain
    mean_term = jnp.mean(scaled * values, axis=-1, keepdims=True)
    grad_values = factor * scaled - values * (factor * factor * factor) * mean_term
    return (grad_values, jnp.sum(grad_out * values * factor, axis=0))


def rope_tables(positions, head_size):
    half_size = head_size // 2
    frequency = 10000.0 ** (-2.0 * jnp.arange(half_size, dtype=jnp.float32) / head_size)
    angles = positions.astype(jnp.float32)[:, None] * frequency[None, :]
    return (jnp.cos(angles)[:, None, :], jnp.sin(angles)[:, None, :])


def rotate(values, cosine_table, sine_table, direction):
    half_size = values.shape[-1] // 2
    first_half = values[..., :half_size]
    second_half = values[..., half_size:]
    return jnp.concatenate(
        [
            first_half * cosine_table - direction * second_half * sine_table,
            second_half * cosine_table + direction * first_half * sine_table,
        ],
        axis=-1,
    )


def contract_last(left, right):
    return lax.dot_general(
        left, right, (((1,), (1,)), ((), ())), preferred_element_type=jnp.float32
    )


def contract_first(left, right):
    return lax.dot_general(
        left, right, (((0,), (0,)), ((), ())), preferred_element_type=jnp.float32
    )


def plain(left, right):
    return jnp.dot(left, right, preferred_element_type=jnp.float32)


def swap(values, axis):
    return lax.ppermute(values, axis, SWAP)


def hop(values, distance):
    count = lax.axis_size("shard")
    return lax.ppermute(values, "shard", tuple((i, i ^ distance) for i in range(count)))


def gather_group(block):
    near = swap(block, "tensor")
    across = swap(block, "context")
    return [block, near, across, swap(across, "tensor")]


def scatter_group(parts):
    far = swap(parts[3].astype(LOW), "tensor")
    near = swap(parts[1].astype(LOW), "tensor")
    across = swap((parts[2] + far.astype(WIDE)).astype(LOW), "context")
    return parts[0] + near.astype(WIDE) + across.astype(WIDE)


def gather_chips(block):
    count = lax.axis_size("shard")
    return [block] + [hop(block, r) for r in range(2, count, 2)]


def gather_shard(block):
    even = gather_chips(block)
    return even + [hop(piece, 1) for piece in even]


def shard_order():
    count = lax.axis_size("shard")
    return jnp.array(list(range(0, count, 2)) + list(range(1, count, 2)), jnp.int32)


def bits_of(axes):
    return [(name, 1 << b) for name in axes for b in range(lax.axis_size(name).bit_length() - 1)]


SMALL_AXES = ("tensor", "context", "shard")


def step_to(values, name, bit):
    count = lax.axis_size(name)
    return lax.ppermute(values, name, tuple((i, i ^ bit) for i in range(count)))


def gather_small(row):
    for name, bit in bits_of(SMALL_AXES):
        other = step_to(row, name, bit)
        upper = (lax.axis_index(name) & bit) > 0
        row = jnp.where(
            upper, jnp.concatenate([other, row], axis=0), jnp.concatenate([row, other], axis=0)
        )
    return row


def scatter_small(rows):
    for name, bit in reversed(bits_of(SMALL_AXES)):
        half = rows.shape[0] // 2
        upper = (lax.axis_index(name) & bit) > 0
        mine = jnp.where(upper, rows[half:], rows[:half])
        theirs = jnp.where(upper, rows[:half], rows[half:])
        rows = mine + step_to(theirs, name, bit)
    return rows


def block_scores(query_block, key_sequence, query_place, key_place):
    scores = jnp.einsum(
        "qhd,khd->hqk", query_block, key_sequence, preferred_element_type=jnp.float32
    ) * HDIM ** (-0.5)
    causal = query_place[:, None] >= key_place[None, :]
    return jnp.where(causal[None], scores, MASKED)


def attend_forward(queries, key_vectors, value_vectors, place, block_rows):
    def one_block(block_index):
        first = block_index * block_rows
        query_block = lax.dynamic_slice_in_dim(queries, first, block_rows, 0)
        query_place = lax.dynamic_slice_in_dim(place, first, block_rows, 0)
        scores = block_scores(query_block, key_vectors, query_place, place)
        maximum = jnp.max(scores, axis=-1, keepdims=True)
        weights = jnp.exp(scores - maximum)
        denominator = jnp.sum(weights, axis=-1, keepdims=True)
        attn_low = (weights / denominator).astype(jnp.bfloat16)
        output = jnp.einsum(
            "hqk,khd->qhd", attn_low, value_vectors, preferred_element_type=jnp.float32
        )
        return (output.astype(jnp.bfloat16), (maximum + jnp.log(denominator))[..., 0])

    block_total = queries.shape[0] // block_rows
    outputs, log_sums = lax.map(one_block, jnp.arange(block_total, dtype=jnp.int32))
    return (outputs.reshape(queries.shape), log_sums)


def attend_backward(queries, key_vectors, value_vectors, grad_vectors, log_sums, place, block_rows):
    score_scale = HDIM ** (-0.5)
    zero_grads = jnp.zeros(queries.shape, jnp.float32)

    def one_block(grad_carry, inputs_pair):
        grad_keys, grad_values = grad_carry
        block_index, log_sum = inputs_pair
        first = block_index * block_rows
        query_block = lax.dynamic_slice_in_dim(queries, first, block_rows, 0)
        grad_block = lax.dynamic_slice_in_dim(grad_vectors, first, block_rows, 0)
        query_place = lax.dynamic_slice_in_dim(place, first, block_rows, 0)
        scores = block_scores(query_block, key_vectors, query_place, place)
        attn_probs = jnp.exp(scores - log_sum[..., None])
        grad_probs = jnp.einsum(
            "qhd,khd->hqk", grad_block, value_vectors, preferred_element_type=jnp.float32
        )
        delta_term = jnp.sum(attn_probs * grad_probs, axis=-1, keepdims=True)
        grad_scores = (attn_probs * (grad_probs - delta_term)).astype(jnp.bfloat16)
        grad_query = (
            jnp.einsum("hqk,khd->qhd", grad_scores, key_vectors, preferred_element_type=jnp.float32)
            * score_scale
        )
        key_part = (
            jnp.einsum("hqk,qhd->khd", grad_scores, query_block, preferred_element_type=jnp.float32)
            * score_scale
        )
        value_part = jnp.einsum(
            "hqk,qhd->khd",
            attn_probs.astype(jnp.bfloat16),
            grad_block,
            preferred_element_type=jnp.float32,
        )
        return ((grad_keys + key_part, grad_values + value_part), grad_query.astype(jnp.bfloat16))

    block_total = queries.shape[0] // block_rows
    (grad_keys, grad_values), grad_queries = lax.scan(
        one_block, (zero_grads, zero_grads), (jnp.arange(block_total, dtype=jnp.int32), log_sums)
    )
    return (
        grad_queries.reshape(queries.shape),
        grad_keys.astype(jnp.bfloat16),
        grad_values.astype(jnp.bfloat16),
    )


def silu_parts(gate_act):
    sigmoid_value = jax.nn.sigmoid(gate_act)
    return (gate_act * sigmoid_value, sigmoid_value)


def expert_forward(rows, weights):
    gate_weight, up_weight, down_weight = weights
    gate_act = plain(rows, gate_weight)
    up_act = plain(rows, up_weight)
    hidden_act = (silu_parts(gate_act)[0] * up_act).astype(LOW)
    produced = contract_last(hidden_act, down_weight).astype(LOW)
    return (produced, (gate_act, up_act, hidden_act))


def expert_backward(grad_rows, kept, weights):
    gate_weight, up_weight, down_weight = weights
    gate_act, up_act, hidden_act = kept
    grad_hidden = plain(grad_rows, down_weight)
    activated, sigmoid_value = silu_parts(gate_act)
    grad_gate_act = (
        grad_hidden * up_act * sigmoid_value * (1.0 + gate_act * (1.0 - sigmoid_value))
    ).astype(LOW)
    grad_up_act = (grad_hidden * activated).astype(LOW)
    grad_route = contract_last(grad_gate_act, gate_weight) + contract_last(grad_up_act, up_weight)
    return (grad_route, grad_gate_act, grad_up_act)


def owned_weight_grad(left, right):
    half = right.shape[1] // 2
    theirs = contract_first(left, right[:, half:]).astype(LOW)
    mine = contract_first(left, right[:, :half])
    return (mine + swap(theirs, "tensor").astype(WIDE))[None]


def softmax_rows(logits):
    weights = jnp.exp(logits - jnp.max(logits, axis=-1, keepdims=True))
    return weights / jnp.sum(weights, axis=-1, keepdims=True)


def pick_rows(pick, blocks):
    chosen = jnp.einsum(
        "bst,btd->bsd", pick, jnp.stack(blocks), preferred_element_type=jnp.float32
    ).astype(LOW)
    return chosen.reshape(-1, chosen.shape[-1])


def slot_picks(ids, expert, capacity):
    routed = jnp.any(ids == expert, axis=2)
    tokens = ids.shape[1]
    line = jnp.arange(tokens, dtype=jnp.int32)
    earlier = (line[:, None] < line[None, :]).astype(LOW)
    position = plain(routed.astype(LOW), earlier).astype(jnp.int32)
    position = jnp.where(routed, position, -1)
    slots = jnp.arange(capacity, dtype=jnp.int32)
    return (position[:, None, :] == slots[None, :, None]).astype(LOW)


def return_chips(rows, picks, other_picks, capacity):
    half = rows.shape[0] // 2
    width = rows.shape[1]
    chips = half // capacity
    arrived = hop(rows[half:], 1).reshape(chips, capacity, width)
    kept = rows[:half].reshape(chips, capacity, width)
    both = jnp.concatenate([kept, arrived], axis=1)
    pick = jnp.concatenate([picks[:chips], other_picks], axis=1)
    total = None
    parts = []
    for chip in range(chips):
        part = lax.dot_general(
            pick[chip], both[chip], (((0,), (0,)), ((), ())), preferred_element_type=jnp.float32
        )
        parts.append(part)
    total = parts[0]
    for chip in range(1, chips):
        total = total + hop(parts[chip].astype(LOW), 2 * chip).astype(WIDE)
    return total


def experts_by_blocks(low_second, cot_chunks, all_ids, router, weights, capacity):
    shard, context = lax.axis_index("shard"), lax.axis_index("context")
    contexts = lax.axis_size("context")
    expert = shard * contexts + context
    other_expert = (shard ^ 1) * contexts + context
    order = shard_order()
    token_count = low_second.shape[0]
    chips = order.shape[0] // 2
    across = swap(low_second, "context")
    chunks = [gather_shard(low_second), gather_shard(across)]
    mixtures, grads, gate_grads = [], [], []
    kept_rows, kept_grads, kept_hidden, kept_gate, kept_up = [], [], [], [], []
    for turn in range(2):
        sources = (shard ^ order) * contexts + (context ^ turn)
        ids = jnp.take(all_ids, sources, axis=0)
        picks = slot_picks(ids, expert, capacity)
        other_picks = slot_picks(ids[:chips], other_expert, capacity)
        rows = pick_rows(picks, chunks[turn])
        cot_rows = pick_rows(picks, cot_chunks[turn])
        probs = softmax_rows(plain(rows, router))
        mine = jnp.arange(probs.shape[1], dtype=jnp.int32)[None, :] == expert
        gate = jnp.sum(jnp.where(mine, probs, 0.0), axis=1, keepdims=True)
        produced, kept = expert_forward(rows, weights)
        cot_wide = cot_rows.astype(WIDE)
        produced_wide = produced.astype(WIDE)
        slot_grad = jnp.sum(produced_wide * cot_wide, axis=1)
        gate_grads.append(
            jnp.sum(
                picks.astype(WIDE) * slot_grad.reshape(picks.shape[0], capacity)[:, :, None], axis=1
            )
        )
        grad_rows = (gate * cot_wide).astype(LOW)
        mixtures.append(
            return_chips((gate * produced_wide).astype(LOW), picks, other_picks, capacity)
        )
        grad_route, grad_gate_act, grad_up_act = expert_backward(grad_rows, kept, weights)
        grads.append(return_chips(grad_route.astype(LOW), picks, other_picks, capacity))
        kept_rows.append(rows)
        kept_grads.append(grad_rows)
        kept_hidden.append(kept[2])
        kept_gate.append(grad_gate_act)
        kept_up.append(grad_up_act)
    mixture = mixtures[0] + swap(mixtures[1].astype(LOW), "context").astype(WIDE)
    grad = grads[0] + swap(grads[1].astype(LOW), "context").astype(WIDE)
    lines = jnp.stack(gate_grads, axis=1)
    lines = jnp.where(context == 0, lines, lines[:, ::-1])
    places = jnp.arange(order.shape[0], dtype=jnp.int32)
    slots = jnp.where((places & 1) == 0, places // 2, chips + places // 2)
    lines = jnp.take(lines, jnp.take(slots, shard ^ places), axis=0)
    lines = lines.reshape(-1, token_count)
    by_expert = lax.all_to_all(lines, ("shard", "context"), split_axis=0, concat_axis=0, tiled=True)
    all_rows = jnp.concatenate(kept_rows, axis=0)
    weight_grads = (
        owned_weight_grad(all_rows, jnp.concatenate(kept_gate, axis=0)),
        owned_weight_grad(all_rows, jnp.concatenate(kept_up, axis=0)),
        owned_weight_grad(
            jnp.concatenate(kept_grads, axis=0), jnp.concatenate(kept_hidden, axis=0)
        ),
    )
    return (mixture, grad, by_expert.T, weight_grads)


def move_slots(buffer):
    return lax.all_to_all(buffer, ("shard", "context"), split_axis=0, concat_axis=0, tiled=True)


def experts_by_slots(low_second, cotangent, expert_ids, router_probs, weights, capacity):
    row_count, model_width = low_second.shape
    expert_count = router_probs.shape[1]
    top_count = expert_ids.shape[1]
    choose = expert_ids[:, :, None] == jnp.arange(expert_count, dtype=jnp.int32)[None, None, :]
    gate_probs = jnp.sum(jnp.where(choose, router_probs[:, None, :], 0.0), axis=2)
    route_total = row_count * top_count
    flat_ids = expert_ids.reshape(-1)
    onehot = (flat_ids[:, None] == jnp.arange(expert_count, dtype=jnp.int32)[None, :]).astype(
        jnp.int32
    )
    before = jnp.cumsum(onehot, axis=0) - onehot
    route_slot = flat_ids * capacity + jnp.sum(before * onehot, axis=1)
    route_of_slot = (
        jnp.full((expert_count * capacity,), route_total, jnp.int32)
        .at[route_slot]
        .set(jnp.arange(route_total, dtype=jnp.int32))
    )
    filled = route_of_slot < route_total
    route_clipped = jnp.minimum(route_of_slot, route_total - 1)
    token_of_slot = route_clipped // top_count
    slot_shape = (expert_count, capacity, model_width)
    flat_shape = (expert_count * capacity, model_width)
    sending = jnp.where(filled[:, None], low_second[token_of_slot], jnp.zeros((), LOW))
    rows = move_slots(sending.reshape(slot_shape)).reshape(flat_shape)
    produced, kept = expert_forward(rows, weights)
    returned = move_slots(produced.reshape(slot_shape)).reshape(flat_shape)
    chosen = returned[route_slot].reshape(row_count, top_count, model_width).astype(WIDE)
    mixture = jnp.sum(gate_probs[:, :, None] * chosen, axis=1)
    grad_top = cotangent.astype(WIDE)
    grad_gates = jnp.sum(chosen * grad_top[:, None, :], axis=2)
    slot_gate = jnp.where(filled, gate_probs.reshape(-1)[route_clipped], 0.0)
    sending_grad = (slot_gate[:, None] * grad_top[token_of_slot]).astype(LOW)
    grad_rows = move_slots(sending_grad.reshape(slot_shape)).reshape(flat_shape)
    grad_route, grad_gate_act, grad_up_act = expert_backward(grad_rows, kept, weights)
    returned_grad = move_slots(grad_route.astype(LOW).reshape(slot_shape)).reshape(flat_shape)
    grad = jnp.sum(
        returned_grad[route_slot].reshape(row_count, top_count, model_width).astype(WIDE), axis=1
    )
    by_expert = jnp.sum(jnp.where(choose, grad_gates[:, :, None], 0.0), axis=1)
    weight_grads = (
        owned_weight_grad(rows, grad_gate_act),
        owned_weight_grad(rows, grad_up_act),
        owned_weight_grad(grad_rows, kept[2]),
    )
    return (mixture, grad, by_expert, weight_grads)


def local(
    hidden_in,
    cotangent,
    w_query,
    w_key,
    w_value,
    w_out,
    w_router,
    norm_first,
    norm_second,
    query_gain,
    key_gain,
    w_gate,
    w_up,
    w_down,
    expert_ids,
):
    group_index = lax.axis_index(("context", "tensor"))
    row_count, model_width = hidden_in.shape
    column_span = w_query.shape[1]
    heads = column_span // HDIM
    expert_count = w_router.shape[1]
    top_count = expert_ids.shape[1]
    capacity = max(2, row_count * top_count * 5 // (4 * expert_count))
    by_blocks = 2 * capacity >= row_count
    block_rows = min(512, SEQ_LEN)
    device_count = model_width // norm_first.shape[0]

    router_rows = w_router.shape[0]
    small = gather_small(
        jnp.concatenate(
            [w_router.reshape(-1), norm_first, norm_second, query_gain, key_gain], axis=0
        )[None]
    )
    hidden_blocks = gather_group(hidden_in)
    packed = lax.all_gather(
        jnp.concatenate([w_query, w_key, w_value, w_out], axis=1), "shard", axis=0, tiled=True
    )
    router_size = router_rows * expert_count
    router_full = small[:, :router_size].reshape(model_width, expert_count)
    gains = [
        small[:, router_size + i * router_rows : router_size + (i + 1) * router_rows]
        .reshape(model_width)
        .astype(WIDE)
        for i in range(4)
    ]
    gain_first, gain_second, gain_query, gain_key = gains
    weights = tuple(
        jnp.concatenate([held[0], swap(held[0], "tensor")], axis=1)
        for held in (w_gate, w_up, w_down)
    )
    if by_blocks:
        all_ids = lax.all_gather(expert_ids, ("shard", "context"), axis=0, tiled=False)
        all_ids = all_ids.reshape(-1, row_count, top_count)
        cot_chunks = [gather_shard(cotangent), gather_shard(swap(cotangent, "context"))]

    qkv_cols = packed[:, : 3 * column_span]
    out_cols = packed[:, 3 * column_span :]
    inputs = hidden_in.astype(WIDE)
    factor_first = rms_scale(inputs, gain_first)[1]
    low_blocks, pre_blocks = [], []
    for block in hidden_blocks:
        low_block = rms_scale(block.astype(WIDE), gain_first)[0].astype(LOW)
        low_blocks.append(low_block)
        pre_blocks.append(plain(low_block, qkv_cols))
    low_group = jnp.concatenate(low_blocks, axis=0)
    pre = jnp.concatenate(pre_blocks, axis=0)
    group_rows = low_group.shape[0]
    query_pre = pre[:, :column_span]
    key_pre = pre[:, column_span : 2 * column_span]
    value_heads = pre[:, 2 * column_span :].astype(LOW)

    def over_group(sums):
        stacked = jnp.stack(sums).reshape(2, 4, -1)
        stacked = stacked + swap(stacked, "tensor")[:, jnp.array([1, 0, 3, 2])]
        stacked = stacked + swap(stacked, "context")[:, jnp.array([2, 3, 0, 1])]
        return stacked.reshape(2, -1)

    query_square, key_square = over_group(
        [jnp.sum(query_pre * query_pre, axis=1), jnp.sum(key_pre * key_pre, axis=1)]
    )
    query_factor = lax.rsqrt(query_square / model_width + EPSILON)[:, None]
    key_factor = lax.rsqrt(key_square / model_width + EPSILON)[:, None]
    gain_query_cols = lax.dynamic_slice_in_dim(
        gain_query, group_index * column_span, column_span, 0
    )
    gain_key_cols = lax.dynamic_slice_in_dim(gain_key, group_index * column_span, column_span, 0)
    line = jnp.arange(group_rows, dtype=jnp.int32)
    place = ((line // row_count) ^ group_index) * row_count + line % row_count
    cosine_table, sine_table = rope_tables(place, HDIM)
    head_shape = (group_rows, heads, HDIM)
    query_heads = rotate(
        (query_pre * query_factor * gain_query_cols).reshape(head_shape),
        cosine_table,
        sine_table,
        1.0,
    ).astype(LOW)
    key_heads = rotate(
        (key_pre * key_factor * gain_key_cols).reshape(head_shape), cosine_table, sine_table, 1.0
    ).astype(LOW)
    value_heads = value_heads.reshape(head_shape)
    attended_heads, log_sums = attend_forward(
        query_heads, key_heads, value_heads, place, block_rows
    )
    attended = attended_heads.reshape(group_rows, column_span)

    def block_of(values, k):
        return values[k * row_count : (k + 1) * row_count]

    middle = inputs + scatter_group(
        [contract_last(block_of(attended, k), out_cols) for k in range(4)]
    )
    normed_second, factor_second = rms_scale(middle, gain_second)
    low_second = normed_second.astype(LOW)
    router_probs = softmax_rows(plain(low_second, router_full))
    if by_blocks:
        mixture, grad_from_experts, grad_router_probs, expert_grads = experts_by_blocks(
            low_second, cot_chunks, all_ids, router_full, weights, capacity
        )
    else:
        mixture, grad_from_experts, grad_router_probs, expert_grads = experts_by_slots(
            low_second, cotangent, expert_ids, router_probs, weights, capacity
        )
    block_output = (middle + mixture).astype(LOW)
    grad_logits = (
        router_probs
        * (grad_router_probs - jnp.sum(router_probs * grad_router_probs, axis=1, keepdims=True))
    ).astype(LOW)
    grad_router_weight = contract_first(low_second, grad_logits)
    grad_second = grad_from_experts + contract_last(grad_logits, router_full)
    grad_normed_second, grad_gain_second = rms_back(middle, factor_second, gain_second, grad_second)
    grad_middle = cotangent.astype(WIDE) + grad_normed_second
    pieces = gather_group(grad_middle.astype(LOW))
    piece = jnp.concatenate(pieces, axis=0)
    out_total = contract_first(piece, attended)
    grad_rows = jnp.concatenate([plain(one, out_cols).astype(LOW) for one in pieces], axis=0)
    grad_query_heads, grad_key_heads, grad_value_heads = attend_backward(
        query_heads,
        key_heads,
        value_heads,
        grad_rows.reshape(head_shape),
        log_sums,
        place,
        block_rows,
    )
    grad_query_normed = rotate(
        grad_query_heads.astype(WIDE), cosine_table, sine_table, -1.0
    ).reshape(group_rows, column_span)
    grad_key_normed = rotate(grad_key_heads.astype(WIDE), cosine_table, sine_table, -1.0).reshape(
        group_rows, column_span
    )
    query_scaled = grad_query_normed * gain_query_cols
    key_scaled = grad_key_normed * gain_key_cols
    query_total, key_total = over_group(
        [jnp.sum(query_scaled * query_pre, axis=1), jnp.sum(key_scaled * key_pre, axis=1)]
    )
    grad_query_low = (
        query_factor * query_scaled
        - query_pre
        * (query_factor * query_factor * query_factor)
        * (query_total / model_width)[:, None]
    ).astype(LOW)
    grad_key_low = (
        key_factor * key_scaled
        - key_pre * (key_factor * key_factor * key_factor) * (key_total / model_width)[:, None]
    ).astype(LOW)
    grad_pre = jnp.concatenate(
        [grad_query_low, grad_key_low, grad_value_heads.reshape(group_rows, column_span)], axis=1
    )
    grad_first = scatter_group([contract_last(block_of(grad_pre, k), qkv_cols) for k in range(4)])
    grad_normed_first, grad_gain_first = rms_back(inputs, factor_first, gain_first, grad_first)
    grad_input = grad_middle + grad_normed_first
    packed_grads = jnp.concatenate(
        [contract_first(low_group, grad_pre).astype(LOW), out_total.astype(LOW)], axis=1
    )
    head_grads = lax.psum_scatter(packed_grads, "shard", scatter_dimension=0, tiled=True).astype(
        WIDE
    )
    zero_gain = jnp.zeros((model_width,), WIDE)
    grad_gain_query = lax.dynamic_update_slice_in_dim(
        zero_gain,
        jnp.sum(grad_query_normed * query_pre * query_factor, axis=0),
        group_index * column_span,
        0,
    )
    grad_gain_key = lax.dynamic_update_slice_in_dim(
        zero_gain,
        jnp.sum(grad_key_normed * key_pre * key_factor, axis=0),
        group_index * column_span,
        0,
    )
    by_device = [
        one.reshape(device_count, -1)
        for one in (grad_router_weight, grad_gain_second, grad_gain_query, grad_gain_key)
    ]
    early = scatter_small(jnp.concatenate(by_device, axis=1))[0]
    late = scatter_small(grad_gain_first.reshape(device_count, -1))[0]
    router_grad = early[:router_size].reshape(router_rows, expert_count)
    rest = early[router_size:].reshape(3, router_rows)
    return (
        block_output,
        grad_input,
        head_grads[:, :column_span],
        head_grads[:, column_span : 2 * column_span],
        head_grads[:, 2 * column_span : 3 * column_span],
        head_grads[:, 3 * column_span :],
        router_grad,
        late,
        rest[0],
        rest[1],
        rest[2],
        expert_grads[0],
        expert_grads[1],
        expert_grads[2],
    )


def solution(mesh):
    rows = P(("shard", "context", "tensor"), None)
    columns = P("shard", ("context", "tensor"))
    vector = P(("shard", "context", "tensor"))
    expert = P(("shard", "context"), None, "tensor")
    return jax.shard_map(
        local,
        mesh=mesh,
        in_specs=(
            (rows, rows)
            + (columns,) * 4
            + (rows,)
            + (vector,) * 4
            + (expert,) * 3
            + (rows,)
        ),
        out_specs=((rows, rows) + (columns,) * 4 + (rows,) + (vector,) * 4 + (expert,) * 3),
        check_vma=False,
    )
```

```python
import jax
import jax.numpy as jnp
from jax import lax
from jax.experimental import pallas as pl
from jax.experimental.pallas import tpu as pltpu
from jax.sharding import PartitionSpec as P

HDIM = 128


EPSILON = 1e-05
MASKED = -1e30
LOW = jnp.bfloat16
WIDE = jnp.float32
SWAP = ((0, 1), (1, 0))


def sync(*values):
    return lax.optimization_barrier(values)


def rms_scale(values, gain):
    factor = lax.rsqrt(jnp.mean(values * values, axis=-1, keepdims=True) + EPSILON)
    return (values * factor * gain, factor)


def rms_back(values, factor, gain, grad_out):
    scaled = grad_out * gain
    mean_term = jnp.mean(scaled * values, axis=-1, keepdims=True)
    grad_values = factor * scaled - values * (factor * factor * factor) * mean_term
    return (grad_values, jnp.sum(grad_out * values * factor, axis=0))


def rope_tables(positions):
    half_size = HDIM // 2
    frequency = 10000.0 ** (-2.0 * jnp.arange(half_size, dtype=WIDE) / HDIM)
    angles = positions.astype(WIDE)[:, None] * frequency[None, :]
    cosine, sine = jnp.cos(angles), jnp.sin(angles)
    return (
        jnp.concatenate([cosine, cosine], axis=1),
        jnp.concatenate([-sine, sine], axis=1),
    )


def contract_last(left, right):
    return lax.dot_general(
        left, right, (((1,), (1,)), ((), ())), preferred_element_type=jnp.float32
    )


def contract_first(left, right):
    return lax.dot_general(
        left, right, (((0,), (0,)), ((), ())), preferred_element_type=jnp.float32
    )


def plain(left, right):
    return jnp.dot(left, right, preferred_element_type=jnp.float32)


def swap(values, axis):
    return lax.ppermute(values, axis, SWAP)


def hop(values, distance):
    count = lax.axis_size("shard")
    return lax.ppermute(values, "shard", tuple((i, i ^ distance) for i in range(count)))


def gather_group(block):
    near = swap(block, "tensor")
    across = swap(block, "context")
    return [block, near, across, swap(across, "tensor")]


def scatter_group(parts):
    far, near = sync(swap(parts[3].astype(LOW), "tensor"), parts[1].astype(LOW))
    across = swap((parts[2] + far.astype(WIDE)).astype(LOW), "context")
    return parts[0] + swap(near, "tensor").astype(WIDE) + across.astype(WIDE)


def over_chips(blocks):
    count = lax.axis_size("shard")
    groups = [list(range(core, count, 2)) for core in range(2)]
    return lax.all_to_all(
        blocks, "shard", split_axis=0, concat_axis=0, axis_index_groups=groups, tiled=True
    )


def gather_chips(block):
    chips = lax.axis_size("shard") // 2
    return over_chips(jnp.broadcast_to(block[None], (chips,) + block.shape))


DEVICES = ("shard", "context", "tensor")


def deal(rows):
    return lax.all_to_all(rows, DEVICES, split_axis=0, concat_axis=0, tiled=True)


def device_total():
    return lax.axis_size("shard") * lax.axis_size("context") * lax.axis_size("tensor")


def gather_small(row):
    return deal(jnp.broadcast_to(row[None], (device_total(), row.shape[0])))


def scatter_small(rows):
    return jnp.sum(deal(rows), axis=0)


def params():
    return pltpu.CompilerParams(vmem_limit_bytes=48 * 1024 * 1024)


def as_column(row, width):
    return jnp.broadcast_to(row, (width, row.shape[1])).T


def turn(values, cosine, sine):
    return values * cosine + pltpu.roll(values, HDIM // 2, 1) * sine


def norm_factors(squares_ref, width):
    factors = lax.rsqrt(squares_ref[...] / width + EPSILON)
    return as_column(factors[0:1], HDIM), as_column(factors[1:2], HDIM)


def prepare_kernel(width, pre_ref, squares_ref, gain_ref, cos_ref, sin_ref, q_ref, k_ref, v_ref):
    span = q_ref.shape[1]
    cosine, sine = cos_ref[...], sin_ref[...]
    factors = norm_factors(squares_ref, width)
    for which, out_ref in ((0, q_ref), (1, k_ref)):
        for first in range(0, span, HDIM):
            cols = slice(which * span + first, which * span + first + HDIM)
            gain = gain_ref[which : which + 1, first : first + HDIM]
            normed = pre_ref[:, cols] * factors[which] * gain
            out_ref[:, first : first + HDIM] = turn(normed, cosine, sine).astype(LOW)
    v_ref[...] = pre_ref[:, 2 * span :].astype(LOW)


def prepare(pre, squares, gain_cols, cosine, sine, width, block):
    rows, total = pre.shape
    span = total // 3
    row_block = lambda cols: pl.BlockSpec((block, cols), lambda i: (i, 0))
    return pl.pallas_call(
        lambda *refs: prepare_kernel(width, *refs),
        grid=(rows // block,),
        in_specs=[
            row_block(total),
            pl.BlockSpec((2, block), lambda i: (0, i)),
            pl.BlockSpec((2, span), lambda i: (0, 0)),
            row_block(HDIM),
            row_block(HDIM),
        ],
        out_specs=[row_block(span)] * 3,
        out_shape=[jax.ShapeDtypeStruct((rows, span), LOW)] * 3,
        compiler_params=params(),
        cost_estimate=pl.CostEstimate(
            flops=10 * rows * total, bytes_accessed=6 * rows * total, transcendentals=0
        ),
    )(pre, squares, gain_cols, cosine, sine)


def visible(group, which, keys, queries):
    line = lax.broadcasted_iota(jnp.int32, (keys, queries), 0)
    key_place = ((line // queries) ^ group) * queries + line % queries
    query_place = (which ^ group) * queries + lax.broadcasted_iota(
        jnp.int32, (keys, queries), 1
    )
    return query_place >= key_place


def dot_last(left, right):
    return lax.dot_general(left, right, (((1,), (1,)), ((), ())), preferred_element_type=WIDE)


def dot_first(left, right):
    return lax.dot_general(left, right, (((0,), (0,)), ((), ())), preferred_element_type=WIDE)


def attend_kernel(which, group_ref, q_ref, k_ref, v_ref, out_ref, log_ref):
    keys, queries = k_ref.shape[0], q_ref.shape[0]
    scores = dot_last(k_ref[...], q_ref[...]) * HDIM ** (-0.5)
    scores = jnp.where(visible(group_ref[0], which, keys, queries), scores, MASKED)
    maximum = jnp.max(scores, axis=0, keepdims=True)
    weights = jnp.exp(scores - maximum)
    total = jnp.sum(weights, axis=0, keepdims=True)
    attn_low = (weights * (1.0 / total)).astype(LOW)
    out_ref[...] = dot_first(v_ref[...], attn_low).T.astype(LOW)
    log_ref[...] = (maximum + jnp.log(total))[None]


def attend_block(which, group, queries, keys, values, block):
    rows, span = queries.shape
    heads = span // HDIM
    whole = pl.BlockSpec((rows, HDIM), lambda h, g: (0, h))
    return pl.pallas_call(
        lambda *refs: attend_kernel(which, *refs),
        grid_spec=pltpu.PrefetchScalarGridSpec(
            num_scalar_prefetch=1,
            grid=(heads,),
            in_specs=[pl.BlockSpec((block, HDIM), lambda h, g: (which, h)), whole, whole],
            out_specs=[
                pl.BlockSpec((block, HDIM), lambda h, g: (0, h)),
                pl.BlockSpec((1, 1, block), lambda h, g: (h, 0, 0)),
            ],
        ),
        out_shape=[
            jax.ShapeDtypeStruct((block, span), LOW),
            jax.ShapeDtypeStruct((heads, 1, block), WIDE),
        ],
        compiler_params=params(),
        cost_estimate=pl.CostEstimate(
            flops=4 * block * rows * span,
            bytes_accessed=4 * rows * span,
            transcendentals=block * rows * heads,
        ),
    )(group, queries, keys, values)


def attend_back_kernel(which, first, group_ref, q_ref, k_ref, v_ref, grad_ref, log_ref, *refs):
    keys, queries = k_ref.shape[0], q_ref.shape[0]
    grad_q_ref, grad_k_ref, grad_v_ref = refs[-3:]
    scores = dot_last(k_ref[...], q_ref[...]) * HDIM ** (-0.5)
    probs = jnp.exp(scores - log_ref[0])
    probs = jnp.where(visible(group_ref[0], which, keys, queries), probs, 0.0)
    grad_probs = dot_last(v_ref[...], grad_ref[...])
    delta = jnp.sum(probs * grad_probs, axis=0, keepdims=True)
    grad_scores = (probs * (grad_probs - delta)).astype(LOW)
    grad_q_ref[...] = (dot_first(k_ref[...], grad_scores).T * HDIM ** (-0.5)).astype(LOW)
    key_part = plain(grad_scores, q_ref[...]) * HDIM ** (-0.5)
    value_part = plain(probs.astype(LOW), grad_ref[...])
    grad_k_ref[...] = key_part if first else refs[0][...] + key_part
    grad_v_ref[...] = value_part if first else refs[1][...] + value_part


def attend_block_back(which, group, queries, keys, values, grad, logs, sums, block):
    rows, span = queries.shape
    heads = span // HDIM
    whole = pl.BlockSpec((rows, HDIM), lambda h, g: (0, h))
    own = pl.BlockSpec((block, HDIM), lambda h, g: (0, h))
    carried = [] if sums is None else list(sums)
    return pl.pallas_call(
        lambda *refs: attend_back_kernel(which, sums is None, *refs),
        grid_spec=pltpu.PrefetchScalarGridSpec(
            num_scalar_prefetch=1,
            grid=(heads,),
            in_specs=[
                pl.BlockSpec((block, HDIM), lambda h, g: (which, h)),
                whole,
                whole,
                own,
                pl.BlockSpec((1, 1, block), lambda h, g: (h, 0, 0)),
            ]
            + [whole] * len(carried),
            out_specs=[own, whole, whole],
        ),
        out_shape=[
            jax.ShapeDtypeStruct((block, span), LOW),
            jax.ShapeDtypeStruct((rows, span), WIDE),
            jax.ShapeDtypeStruct((rows, span), WIDE),
        ],
        compiler_params=params(),
        cost_estimate=pl.CostEstimate(
            flops=10 * block * rows * span,
            bytes_accessed=20 * rows * span,
            transcendentals=block * rows * heads,
        ),
    )(group, queries, keys, values, grad, logs, *carried)


def turned_back(which, first, grads, cosine, sine):
    values = grads[which][:, first : first + HDIM].astype(WIDE)
    return turn(values, cosine, -sine)


def norm_sums_kernel(
    width, gq_ref, gk_ref, pre_ref, squares_ref, gain_ref, cos_ref, sin_ref, total_ref, col_ref
):
    span = gq_ref.shape[1]
    cosine, sine = cos_ref[...], sin_ref[...]
    factors = norm_factors(squares_ref, width)

    @pl.when(pl.program_id(0) == 0)
    def _():
        col_ref[...] = jnp.zeros_like(col_ref)

    for which in range(2):
        total = jnp.zeros(cosine.shape, WIDE)
        for first in range(0, span, HDIM):
            grad = turned_back(which, first, (gq_ref, gk_ref), cosine, sine)
            cols = slice(which * span + first, which * span + first + HDIM)
            product = grad * pre_ref[:, cols]
            total = total + product * gain_ref[which : which + 1, first : first + HDIM]
            col_ref[which : which + 1, first : first + HDIM] += jnp.sum(
                product * factors[which], axis=0, keepdims=True
            )
        total_ref[which : which + 1, :] = jnp.sum(total.T, axis=0, keepdims=True)


def norm_grads_kernel(
    width,
    gq_ref,
    gk_ref,
    gv_ref,
    pre_ref,
    squares_ref,
    total_ref,
    gain_ref,
    cos_ref,
    sin_ref,
    out_ref,
):
    span = gq_ref.shape[1]
    cosine, sine = cos_ref[...], sin_ref[...]
    factors = norm_factors(squares_ref, width)
    for which in range(2):
        factor = factors[which]
        mean = as_column(total_ref[which : which + 1] / width, HDIM)
        pull = factor * factor * factor * mean
        for first in range(0, span, HDIM):
            grad = turned_back(which, first, (gq_ref, gk_ref), cosine, sine)
            cols = slice(which * span + first, which * span + first + HDIM)
            scaled = grad * gain_ref[which : which + 1, first : first + HDIM]
            out_ref[:, cols] = (factor * scaled - pre_ref[:, cols] * pull).astype(LOW)
    out_ref[:, 2 * span :] = gv_ref[...].astype(LOW)


def norm_call(body, operands, kinds, outs, width, block):
    def spec(shape, kind):
        if kind == "rows":
            return pl.BlockSpec((block, shape[1]), lambda i: (i, 0))
        if kind == "line":
            return pl.BlockSpec((shape[0], block), lambda i: (0, i))
        return pl.BlockSpec(shape, lambda i: (0, 0))

    size = sum(o.size * o.dtype.itemsize for o in operands)
    return pl.pallas_call(
        lambda *refs: body(width, *refs),
        grid=(operands[0].shape[0] // block,),
        in_specs=[spec(o.shape, kind) for o, kind in zip(operands, kinds)],
        out_specs=[spec(shape, kind) for shape, _, kind in outs],
        out_shape=[jax.ShapeDtypeStruct(shape, dtype) for shape, dtype, _ in outs],
        compiler_params=params(),
        cost_estimate=pl.CostEstimate(flops=4 * size, bytes_accessed=size, transcendentals=0),
    )(*operands)


def silu_parts(gate_act):
    sigmoid_value = jax.nn.sigmoid(gate_act)
    return (gate_act * sigmoid_value, sigmoid_value)


def expert_hidden(rows, weights):
    gate_act = plain(rows, weights[0])
    up_act = plain(rows, weights[1])
    return (gate_act, up_act, (silu_parts(gate_act)[0] * up_act).astype(LOW))


def expert_produce(hidden_act, weights):
    return contract_last(hidden_act, weights[2]).astype(LOW)


def expert_forward(rows, weights):
    kept = expert_hidden(rows, weights)
    return (expert_produce(kept[2], weights), kept)


def expert_backward(grad_rows, kept, weights):
    gate_weight, up_weight, down_weight = weights
    gate_act, up_act, hidden_act = kept
    grad_hidden = plain(grad_rows, down_weight)
    activated, sigmoid_value = silu_parts(gate_act)
    grad_gate_act = (
        grad_hidden * up_act * sigmoid_value * (1.0 + gate_act * (1.0 - sigmoid_value))
    ).astype(LOW)
    grad_up_act = (grad_hidden * activated).astype(LOW)
    grad_route = contract_last(grad_gate_act, gate_weight) + contract_last(grad_up_act, up_weight)
    return (grad_route, grad_gate_act, grad_up_act)


def their_grad(left, right):
    return contract_first(left, right[:, right.shape[1] // 2 :]).astype(LOW)


def own_grad(left, right, arrived):
    mine = contract_first(left, right[:, : right.shape[1] // 2])
    return (mine + arrived.astype(WIDE))[None]


def halves(values):
    half = values.shape[0] // 2
    return (values[:half], values[half:])


def with_partner(held):
    return jnp.concatenate([held, swap(held, "tensor")], axis=1)


def softmax_rows(logits):
    weights = jnp.exp(logits - jnp.max(logits, axis=-1, keepdims=True))
    return weights / jnp.sum(weights, axis=-1, keepdims=True)


def pick_rows(picks, other_picks, blocks):
    pick = jnp.concatenate([picks, other_picks], axis=1)
    chosen = jnp.einsum("bst,btd->bsd", pick, blocks, preferred_element_type=jnp.float32)
    chosen = chosen.astype(LOW)
    capacity, width = picks.shape[1], blocks.shape[2]
    kept = chosen[:, :capacity].reshape(-1, width)
    arrived = hop(chosen[:, capacity:].reshape(-1, width), 1)
    return jnp.concatenate([kept, arrived], axis=0)


def slot_picks(ids, expert, capacity):
    routed = jnp.any(ids == expert, axis=1)
    tokens = ids.shape[2]
    line = jnp.arange(tokens, dtype=jnp.int32)
    earlier = (line[:, None] < line[None, :]).astype(LOW)
    position = plain(routed.astype(LOW), earlier).astype(jnp.int32)
    position = jnp.where(routed, position, -1)
    slots = jnp.arange(capacity, dtype=jnp.int32)
    return (position[:, None, :] == slots[None, :, None]).astype(LOW)


def chip_parts(rows, picks, other_picks):
    half = rows.shape[0] // 2
    return combine(rows[:half], hop(rows[half:], 1), picks, other_picks)


def combine(kept, arrived, picks, other_picks):
    shape = picks.shape[:2] + kept.shape[1:]
    both = jnp.concatenate([kept.reshape(shape), arrived.reshape(shape)], axis=1)
    pick = jnp.concatenate([picks, other_picks], axis=1)
    parts = jnp.einsum("bst,bsd->btd", pick, both, preferred_element_type=jnp.float32)
    return parts.astype(LOW)


def sum_chips(parts):
    return jnp.sum(over_chips(parts).astype(WIDE), axis=0)


def experts_by_blocks(
    low_second, cot_near, cot_far, all_ids, router, gate_weight, w_up, w_down, capacity
):
    shard, context = lax.axis_index("shard"), lax.axis_index("context")
    contexts = lax.axis_size("context")
    expert = shard * contexts + context
    other_expert = (shard ^ 1) * contexts + context
    token_count = low_second.shape[0]
    chips = lax.axis_size("shard") // 2
    same_core = 2 * jnp.arange(chips, dtype=jnp.int32) + (shard & 1)
    picks = []
    for turn in range(2):
        ids = jnp.take(all_ids, same_core * contexts + (context ^ turn), axis=0)
        far_ids = jnp.take(all_ids, (same_core ^ 1) * contexts + (context ^ turn), axis=0)
        picks.append(
            (
                slot_picks(ids, expert, capacity),
                slot_picks(ids, other_expert, capacity),
                slot_picks(far_ids, expert, capacity),
            )
        )

    def arrive(turn, rows):
        probs = softmax_rows(plain(rows, router))
        mine = jnp.arange(probs.shape[1], dtype=jnp.int32)[None, :] == expert
        return jnp.sum(jnp.where(mine, probs, 0.0), axis=1, keepdims=True)

    def leave(turn, produced, cot_rows, gate):
        cot_wide = cot_rows.astype(WIDE)
        produced_wide = produced.astype(WIDE)
        slot_grad = jnp.sum(produced_wide * cot_wide, axis=1)
        all_picks = jnp.concatenate([picks[turn][0], picks[turn][2]], axis=0).astype(WIDE)
        gate_grad = jnp.sum(all_picks * slot_grad.reshape(2 * chips, capacity)[:, :, None], axis=1)
        return (gate_grad, (gate * cot_wide).astype(LOW), (gate * produced_wide).astype(LOW))

    up_halves = halves(w_up)
    near_chunk, across, up_first, up_late = sync(
        gather_chips(low_second),
        swap(low_second, "context"),
        swap(up_halves[0], "tensor"),
        up_halves[1],
    )
    near_rows = pick_rows(*picks[0][:2], near_chunk)
    near_rows, up_second, w_down, cot_near = sync(
        near_rows, swap(up_late, "tensor"), w_down, cot_near
    )
    up_arrived = jnp.concatenate([up_first, up_second], axis=0)
    weights = (
        gate_weight,
        jnp.concatenate([w_up, up_arrived], axis=1),
        with_partner(w_down),
    )
    near_kept = expert_hidden(near_rows, weights)
    near_hidden, far_chunk = sync(near_kept[2], gather_chips(across))
    near_kept = near_kept[:2] + (near_hidden,)
    far_rows = pick_rows(*picks[1][:2], far_chunk)
    far_kept = expert_hidden(far_rows, weights)
    near_cot, far_cot = pick_rows(*picks[0][:2], cot_near), pick_rows(*picks[1][:2], cot_far)
    gate = arrive(0, near_rows)
    produced = expert_produce(near_hidden, weights)
    near_gate_grad, near_grad_rows, weighted = leave(0, produced, near_cot, gate)
    mixture_parts = chip_parts(weighted, *picks[0][:2])
    gate = arrive(1, far_rows)
    produced = expert_produce(far_kept[2], weights)
    far_gate_grad, far_grad_rows, far_weighted = leave(1, produced, far_cot, gate)
    gate_grads = [near_gate_grad, far_gate_grad]
    rest_parts = chip_parts(far_weighted, *picks[1][:2])
    far_grad_rows, mixture_parts = sync(far_grad_rows, mixture_parts)
    mixture = sum_chips(mixture_parts)

    def both(near, far):
        return jnp.concatenate([near, far], axis=0)

    far_route, far_gate_act, far_up_act = expert_backward(far_grad_rows, far_kept, weights)
    down_pair = (both(near_grad_rows, far_grad_rows), both(near_kept[2], far_kept[2]))
    down_theirs = their_grad(*down_pair)
    far_parts = chip_parts(far_route.astype(LOW), *picks[1][:2])
    near_grad_rows, far_parts, down_theirs, mixture, rest_parts = sync(
        near_grad_rows, far_parts, down_theirs, mixture, rest_parts
    )
    near_route, near_gate_act, near_up_act = expert_backward(near_grad_rows, near_kept, weights)
    near_route = near_route.astype(LOW)
    near_half = near_route.shape[0] // 2
    near_swapped, far_grad = sync(
        hop(near_route[near_half:], 1), sum_chips(far_parts).astype(LOW)
    )
    near_parts = combine(near_route[:near_half], near_swapped, *picks[0][:2])
    all_rows = both(near_rows, far_rows)
    gate_pair = (all_rows, both(near_gate_act, far_gate_act))
    up_pair = (all_rows, both(near_up_act, far_up_act))
    gate_theirs = their_grad(*gate_pair)
    far_arrived = swap(far_grad, "context")
    grad, rest_parts, gate_theirs, down_arrived = sync(
        sum_chips(near_parts) + far_arrived.astype(WIDE),
        rest_parts,
        gate_theirs,
        swap(down_theirs, "tensor"),
    )
    up_theirs = their_grad(*up_pair)
    lines = jnp.stack(gate_grads, axis=1)
    lines = jnp.where(context == 0, lines, lines[:, ::-1])
    mine, far = lines[:chips], lines[chips:]
    low_core = (shard & 1) == 0
    lines = jnp.stack([jnp.where(low_core, mine, far), jnp.where(low_core, far, mine)], axis=1)
    lines = lines.reshape(-1, token_count)
    by_expert = lax.all_to_all(lines, ("shard", "context"), split_axis=0, concat_axis=0, tiled=True)
    later = (mixture, rest_parts, gate_theirs, up_theirs, gate_pair, up_pair, down_pair, down_arrived)
    return (grad, by_expert.T, later)


def move_slots(buffer):
    return lax.all_to_all(buffer, ("shard", "context"), split_axis=0, concat_axis=0, tiled=True)


def experts_by_slots(low_second, cotangent, expert_ids, router_probs, weights, capacity):
    row_count, model_width = low_second.shape
    expert_count = router_probs.shape[1]
    top_count = expert_ids.shape[1]
    choose = expert_ids[:, :, None] == jnp.arange(expert_count, dtype=jnp.int32)[None, None, :]
    gate_probs = jnp.sum(jnp.where(choose, router_probs[:, None, :], 0.0), axis=2)
    route_total = row_count * top_count
    flat_ids = expert_ids.reshape(-1)
    onehot = (flat_ids[:, None] == jnp.arange(expert_count, dtype=jnp.int32)[None, :]).astype(
        jnp.int32
    )
    before = jnp.cumsum(onehot, axis=0) - onehot
    route_slot = flat_ids * capacity + jnp.sum(before * onehot, axis=1)
    route_of_slot = (
        jnp.full((expert_count * capacity,), route_total, jnp.int32)
        .at[route_slot]
        .set(jnp.arange(route_total, dtype=jnp.int32))
    )
    filled = route_of_slot < route_total
    route_clipped = jnp.minimum(route_of_slot, route_total - 1)
    token_of_slot = route_clipped // top_count
    slot_shape = (expert_count, capacity, model_width)
    flat_shape = (expert_count * capacity, model_width)
    sending = jnp.where(filled[:, None], low_second[token_of_slot], jnp.zeros((), LOW))
    rows = move_slots(sending.reshape(slot_shape)).reshape(flat_shape)
    produced, kept = expert_forward(rows, weights)
    returned = move_slots(produced.reshape(slot_shape)).reshape(flat_shape)
    chosen = returned[route_slot].reshape(row_count, top_count, model_width).astype(WIDE)
    mixture = jnp.sum(gate_probs[:, :, None] * chosen, axis=1)
    grad_top = cotangent.astype(WIDE)
    grad_gates = jnp.sum(chosen * grad_top[:, None, :], axis=2)
    slot_gate = jnp.where(filled, gate_probs.reshape(-1)[route_clipped], 0.0)
    sending_grad = (slot_gate[:, None] * grad_top[token_of_slot]).astype(LOW)
    grad_rows = move_slots(sending_grad.reshape(slot_shape)).reshape(flat_shape)
    grad_route, grad_gate_act, grad_up_act = expert_backward(grad_rows, kept, weights)
    returned_grad = move_slots(grad_route.astype(LOW).reshape(slot_shape)).reshape(flat_shape)
    grad = jnp.sum(
        returned_grad[route_slot].reshape(row_count, top_count, model_width).astype(WIDE), axis=1
    )
    by_expert = jnp.sum(jnp.where(choose, grad_gates[:, :, None], 0.0), axis=1)
    pairs = [(rows, grad_gate_act), (rows, grad_up_act), (grad_rows, kept[2])]
    grads = tuple(own_grad(*pair, swap(their_grad(*pair), "tensor")) for pair in pairs)
    return (grad, by_expert, mixture, grads)


def local(
    hidden_in,
    cotangent,
    w_query,
    w_key,
    w_value,
    w_out,
    w_router,
    norm_first,
    norm_second,
    query_gain,
    key_gain,
    w_gate,
    w_up,
    w_down,
    expert_ids,
):
    group_index = lax.axis_index(("context", "tensor"))
    row_count, model_width = hidden_in.shape
    column_span = w_query.shape[1]
    expert_count = w_router.shape[1]
    top_count = expert_ids.shape[1]
    capacity = max(2, row_count * top_count * 5 // (4 * expert_count))
    by_blocks = 2 * capacity >= row_count
    device_count = model_width // norm_first.shape[0]

    router_rows = w_router.shape[0]
    small = gather_small(
        jnp.concatenate(
            [
                w_router.reshape(-1),
                norm_first,
                norm_second,
                query_gain,
                key_gain,
                expert_ids.T.reshape(-1).astype(LOW),
            ],
            axis=0,
        )
    )
    hidden_blocks = gather_group(hidden_in)
    hidden_blocks[3], gate_early = sync(hidden_blocks[3], w_gate[0, : model_width // 2])
    packed = lax.all_gather(
        jnp.concatenate([w_query, w_key, w_value, w_out], axis=1), "shard", axis=0, tiled=True
    )
    router_size = router_rows * expert_count
    router_full = small[:, :router_size].reshape(model_width, expert_count)
    gains = [
        small[:, router_size + i * router_rows : router_size + (i + 1) * router_rows]
        .reshape(model_width)
        .astype(WIDE)
        for i in range(4)
    ]
    gain_first, gain_second, gain_query, gain_key = gains
    if by_blocks:
        tensors = lax.axis_size("tensor")
        all_ids = small[:, router_size + 4 * router_rows :].astype(jnp.int32)
        all_ids = all_ids.reshape(-1, tensors, top_count, row_count)
        all_ids = lax.dynamic_index_in_dim(all_ids, lax.axis_index("tensor"), 1, False)

    qkv_cols = packed[:, : 3 * column_span]
    out_cols = packed[:, 3 * column_span :]
    inputs = hidden_in.astype(WIDE)
    factor_first = rms_scale(inputs, gain_first)[1]
    low_blocks, pre_blocks = [], []
    for block in hidden_blocks:
        low_block = rms_scale(block.astype(WIDE), gain_first)[0].astype(LOW)
        low_blocks.append(low_block)
        pre_blocks.append(plain(low_block, qkv_cols))
    low_group = jnp.concatenate(low_blocks, axis=0)
    pre = jnp.concatenate(pre_blocks, axis=0)
    group_rows = low_group.shape[0]
    line = jnp.arange(group_rows, dtype=jnp.int32)
    place = ((line // row_count) ^ group_index) * row_count + line % row_count
    cosine, sine = rope_tables(place)
    gain_cols = jnp.stack(
        [
            lax.dynamic_slice_in_dim(gain, group_index * column_span, column_span, 0)
            for gain in (gain_query, gain_key)
        ]
    )

    def over_group(stacked):
        stacked = stacked.reshape(2, 4, -1)
        stacked = stacked + swap(stacked, "tensor")[:, jnp.array([1, 0, 3, 2])]
        stacked = stacked + swap(stacked, "context")[:, jnp.array([2, 3, 0, 1])]
        return stacked.reshape(2, -1)

    half_rows = model_width // 2
    gate_first = swap(gate_early, "tensor")
    own_squares, gate_first, early_cot = sync(
        jnp.stack(
            [
                jnp.sum(jnp.square(pre[:, i * column_span : (i + 1) * column_span]), axis=1)
                for i in range(2)
            ]
        ),
        gate_first,
        cotangent,
    )
    if by_blocks:
        cot_near = gather_chips(early_cot)
        cot_across = swap(early_cot, "context")
    squares, gate_late = sync(over_group(own_squares), w_gate[0, half_rows:])
    gate_second = swap(gate_late, "tensor")
    query_heads, key_heads, value_heads = prepare(
        pre, squares, gain_cols, cosine, sine, model_width, row_count
    )
    group = group_index[None].astype(jnp.int32)
    blocks, logs = [None] * 4, [None] * 4
    for k in (3, 2, 1, 0):
        blocks[k], logs[k] = attend_block(
            k, group, query_heads, key_heads, value_heads, row_count
        )
    parts = [contract_last(block, out_cols) for block in blocks]
    far_part, gate_second = sync(parts[3].astype(LOW), gate_second)
    gate_weight = jnp.concatenate(
        [w_gate[0], jnp.concatenate([gate_first, gate_second], axis=0)], axis=1
    )
    far = swap(far_part, "tensor")
    far, near_part, part = sync(far, parts[1].astype(LOW), parts[2])
    if by_blocks:
        far, cot_near, cot_across = sync(far, cot_near, cot_across)
    across = swap((part + far.astype(WIDE)).astype(LOW), "context")
    near = swap(near_part, "tensor")
    if by_blocks:
        across, cot_far, gate_weight = sync(across, gather_chips(cot_across), gate_weight)
    middle = inputs + parts[0] + near.astype(WIDE) + across.astype(WIDE)
    normed_second, factor_second = rms_scale(middle, gain_second)
    low_second = normed_second.astype(LOW)
    router_probs = softmax_rows(plain(low_second, router_full))
    low_second, late_up, late_down = sync(low_second, w_up[0], w_down[0])
    if by_blocks:
        grad_from_experts, grad_router_probs, later = experts_by_blocks(
            low_second,
            cot_near,
            cot_far,
            all_ids,
            router_full,
            gate_weight,
            late_up,
            late_down,
            capacity,
        )
        mixture, rest_parts, gate_theirs, up_theirs, gate_pair, up_pair, down_pair, arrived = later
    else:
        weights = (gate_weight, with_partner(late_up), with_partner(late_down))
        grad_from_experts, grad_router_probs, mixture, expert_grads = experts_by_slots(
            low_second, cotangent, expert_ids, router_probs, weights, capacity
        )
    grad_logits = (
        router_probs
        * (grad_router_probs - jnp.sum(router_probs * grad_router_probs, axis=1, keepdims=True))
    ).astype(LOW)
    grad_router_weight = contract_first(low_second, grad_logits)
    grad_second = grad_from_experts + contract_last(grad_logits, router_full)
    grad_normed_second, grad_gain_second = rms_back(middle, factor_second, gain_second, grad_second)
    grad_middle = cotangent.astype(WIDE) + grad_normed_second
    grad_branch = grad_middle.astype(LOW)
    near_piece, across = swap(grad_branch, "tensor"), swap(grad_branch, "context")

    def piece_back(k, piece, sums):
        grad_queries, *sums = attend_block_back(
            k,
            group,
            query_heads,
            key_heads,
            value_heads,
            plain(piece, out_cols).astype(LOW),
            logs[k],
            sums,
            row_count,
        )
        return (grad_queries, tuple(sums))

    own_query, own_sums = piece_back(0, grad_branch, None)
    if by_blocks:
        down_grad = own_grad(*down_pair, arrived)
        rest = sum_chips(rest_parts).astype(LOW)
    near_query, near_sums = piece_back(1, near_piece, own_sums)
    if by_blocks:
        across, near_sums, down_grad, rest, up_theirs = sync(
            across, near_sums, down_grad, rest, up_theirs
        )
        rest_arrived = swap(rest, "context")
    last = swap(across, "tensor")
    across_query, across_sums = piece_back(2, across, near_sums)
    if by_blocks:
        gate_halves = halves(gate_theirs)
        last, across_sums, gate_early = sync(last, across_sums, gate_halves[0])
    pieces = [grad_branch, near_piece, across, last]
    last_query, sums = piece_back(3, last, across_sums)
    grad_queries = [own_query, near_query, across_query, last_query]
    grad_query_heads = jnp.concatenate(grad_queries, axis=0)
    out_total = contract_first(pieces[0], blocks[0])
    for k in range(1, 4):
        out_total = out_total + contract_first(pieces[k], blocks[k])
    out_grad = lax.psum_scatter(out_total.astype(LOW), "shard", scatter_dimension=0, tiled=True)
    totals, gain_grads = norm_call(
        norm_sums_kernel,
        (grad_query_heads, sums[0], pre, squares, gain_cols, cosine, sine),
        ("rows", "rows", "rows", "line", "whole", "rows", "rows"),
        (((2, group_rows), WIDE, "line"), ((2, column_span), WIDE, "whole")),
        model_width,
        row_count,
    )
    if by_blocks:
        totals, rest_arrived, gate_first, gate_late = sync(
            totals, rest_arrived, swap(gate_early, "tensor"), gate_halves[1]
        )
        mixture = mixture + rest_arrived.astype(WIDE)
    block_output = (middle + mixture).astype(LOW)
    totals = over_group(totals)
    if by_blocks:
        totals, gate_late = sync(totals, gate_late)
    (grad_pre,) = norm_call(
        norm_grads_kernel,
        (grad_query_heads, *sums, pre, squares, totals, gain_cols, cosine, sine),
        ("rows", "rows", "rows", "rows", "line", "line", "whole", "rows", "rows"),
        (((group_rows, 3 * column_span), LOW, "rows"),),
        model_width,
        row_count,
    )

    def block_of(values, k):
        return values[k * row_count : (k + 1) * row_count]

    far_part = contract_last(block_of(grad_pre, 3), qkv_cols).astype(LOW)
    if by_blocks:
        far_part, grad_pre, gate_second = sync(far_part, grad_pre, swap(gate_late, "tensor"))
    far = swap(far_part, "tensor")
    head_total = contract_first(low_group, grad_pre).astype(LOW)
    parts = [contract_last(block_of(grad_pre, k), qkv_cols) for k in range(3)]
    far, head_total, parts[1], parts[2] = sync(far, head_total, parts[1].astype(LOW), parts[2])
    across = swap((parts[2] + far.astype(WIDE)).astype(LOW), "context")
    near = swap(parts[1], "tensor")
    head_grads = lax.psum_scatter(head_total, "shard", scatter_dimension=0, tiled=True).astype(WIDE)
    if by_blocks:
        near, across, gain_grads, up_theirs = sync(near, across, gain_grads, up_theirs)
        up_arrived = swap(up_theirs, "tensor")
        gate_arrived = jnp.concatenate([gate_first, gate_second], axis=0)
        expert_grads = (
            own_grad(*gate_pair, gate_arrived),
            own_grad(*up_pair, up_arrived),
            down_grad,
        )
    grad_first = parts[0] + near.astype(WIDE) + across.astype(WIDE)
    grad_normed_first, grad_gain_first = rms_back(inputs, factor_first, gain_first, grad_first)
    grad_input = grad_middle + grad_normed_first
    zero_gain = jnp.zeros((2, model_width), WIDE)
    grad_gains = lax.dynamic_update_slice(zero_gain, gain_grads, (0, group_index * column_span))
    by_device = [
        one.reshape(device_count, -1)
        for one in (grad_router_weight, grad_gain_second, grad_gains[0], grad_gains[1])
    ]
    early = scatter_small(jnp.concatenate(by_device, axis=1))
    late = scatter_small(grad_gain_first.reshape(device_count, -1))
    router_grad = early[:router_size].reshape(router_rows, expert_count)
    rest = early[router_size:].reshape(3, router_rows)
    return (
        block_output,
        grad_input,
        head_grads[:, :column_span],
        head_grads[:, column_span : 2 * column_span],
        head_grads[:, 2 * column_span : 3 * column_span],
        out_grad.astype(WIDE),
        router_grad,
        late,
        rest[0],
        rest[1],
        rest[2],
        expert_grads[0],
        expert_grads[1],
        expert_grads[2],
    )


def solution(mesh):
    rows = P(("shard", "context", "tensor"), None)
    columns = P("shard", ("context", "tensor"))
    vector = P(("shard", "context", "tensor"))
    expert = P(("shard", "context"), None, "tensor")
    return jax.shard_map(
        local,
        mesh=mesh,
        in_specs=(
            (rows, rows)
            + (columns,) * 4
            + (rows,)
            + (vector,) * 4
            + (expert,) * 3
            + (rows,)
        ),
        out_specs=((rows, rows) + (columns,) * 4 + (rows,) + (vector,) * 4 + (expert,) * 3),
        check_vma=False,
    )
```

```python
import jax
import jax.numpy as jnp
from jax import lax
from jax.experimental import pallas as pl
from jax.experimental.pallas import tpu as pltpu
from jax.sharding import PartitionSpec as P

HDIM = 128


EPSILON = 1e-05
MASKED = -1e30
LOW = jnp.bfloat16
WIDE = jnp.float32
SWAP = ((0, 1), (1, 0))


def sync(*values):
    return lax.optimization_barrier(values)


def rms_scale(values, gain):
    factor = lax.rsqrt(jnp.mean(values * values, axis=-1, keepdims=True) + EPSILON)
    return (values * factor * gain, factor)


def rms_back(values, factor, gain, grad_out):
    scaled = grad_out * gain
    mean_term = jnp.mean(scaled * values, axis=-1, keepdims=True)
    grad_values = factor * scaled - values * (factor * factor * factor) * mean_term
    return (grad_values, jnp.sum(grad_out * values * factor, axis=0))


def rope_tables(positions):
    half_size = HDIM // 2
    frequency = 10000.0 ** (-2.0 * jnp.arange(half_size, dtype=WIDE) / HDIM)
    angles = positions.astype(WIDE)[:, None] * frequency[None, :]
    cosine, sine = jnp.cos(angles), jnp.sin(angles)
    return (
        jnp.concatenate([cosine, cosine], axis=1),
        jnp.concatenate([-sine, sine], axis=1),
    )


def contract_last(left, right):
    return lax.dot_general(
        left, right, (((1,), (1,)), ((), ())), preferred_element_type=jnp.float32
    )


def contract_first(left, right):
    return lax.dot_general(
        left, right, (((0,), (0,)), ((), ())), preferred_element_type=jnp.float32
    )


def plain(left, right):
    return jnp.dot(left, right, preferred_element_type=jnp.float32)


def swap(values, axis):
    return lax.ppermute(values, axis, SWAP)


def hop(values, distance):
    count = lax.axis_size("shard")
    return lax.ppermute(values, "shard", tuple((i, i ^ distance) for i in range(count)))


def gather_group(block):
    near = swap(block, "tensor")
    across = swap(block, "context")
    return [block, near, across, swap(across, "tensor")]


def scatter_group(parts):
    far, near = sync(swap(parts[3].astype(LOW), "tensor"), parts[1].astype(LOW))
    across = swap((parts[2] + far.astype(WIDE)).astype(LOW), "context")
    return parts[0] + swap(near, "tensor").astype(WIDE) + across.astype(WIDE)


def over_chips(blocks):
    count = lax.axis_size("shard")
    groups = [list(range(core, count, 2)) for core in range(2)]
    return lax.all_to_all(
        blocks, "shard", split_axis=0, concat_axis=0, axis_index_groups=groups, tiled=True
    )


def gather_chips(block):
    chips = lax.axis_size("shard") // 2
    return over_chips(jnp.broadcast_to(block[None], (chips,) + block.shape))


DEVICES = ("shard", "context", "tensor")


def deal(rows):
    return lax.all_to_all(rows, DEVICES, split_axis=0, concat_axis=0, tiled=True)


def device_total():
    return lax.axis_size("shard") * lax.axis_size("context") * lax.axis_size("tensor")


def gather_small(row):
    return deal(jnp.broadcast_to(row[None], (device_total(), row.shape[0])))


def scatter_small(rows):
    return jnp.sum(deal(rows), axis=0)


def params():
    return pltpu.CompilerParams(vmem_limit_bytes=48 * 1024 * 1024)


def as_column(row, width):
    return jnp.broadcast_to(row, (width, row.shape[1])).T


def turn(values, cosine, sine):
    return values * cosine + pltpu.roll(values, HDIM // 2, 1) * sine


def norm_factors(squares_ref, width):
    factors = lax.rsqrt(squares_ref[...] / width + EPSILON)
    return as_column(factors[0:1], HDIM), as_column(factors[1:2], HDIM)


def prepare_kernel(width, pre_ref, squares_ref, gain_ref, cos_ref, sin_ref, q_ref, k_ref, v_ref):
    span = q_ref.shape[1]
    cosine, sine = cos_ref[...], sin_ref[...]
    factors = norm_factors(squares_ref, width)
    for which, out_ref in ((0, q_ref), (1, k_ref)):
        for first in range(0, span, HDIM):
            cols = slice(which * span + first, which * span + first + HDIM)
            gain = gain_ref[which : which + 1, first : first + HDIM]
            normed = pre_ref[:, cols] * factors[which] * gain
            out_ref[:, first : first + HDIM] = turn(normed, cosine, sine).astype(LOW)
    v_ref[...] = pre_ref[:, 2 * span :].astype(LOW)


def prepare(pre, squares, gain_cols, cosine, sine, width, block):
    rows, total = pre.shape
    span = total // 3
    row_block = lambda cols: pl.BlockSpec((block, cols), lambda i: (i, 0))
    return pl.pallas_call(
        lambda *refs: prepare_kernel(width, *refs),
        grid=(rows // block,),
        in_specs=[
            row_block(total),
            pl.BlockSpec((2, block), lambda i: (0, i)),
            pl.BlockSpec((2, span), lambda i: (0, 0)),
            row_block(HDIM),
            row_block(HDIM),
        ],
        out_specs=[row_block(span)] * 3,
        out_shape=[jax.ShapeDtypeStruct((rows, span), LOW)] * 3,
        compiler_params=params(),
        cost_estimate=pl.CostEstimate(
            flops=10 * rows * total, bytes_accessed=6 * rows * total, transcendentals=0
        ),
    )(pre, squares, gain_cols, cosine, sine)


def visible(group, which, keys, queries):
    line = lax.broadcasted_iota(jnp.int32, (keys, queries), 0)
    key_place = ((line // queries) ^ group) * queries + line % queries
    query_place = (which ^ group) * queries + lax.broadcasted_iota(
        jnp.int32, (keys, queries), 1
    )
    return query_place >= key_place


def dot_last(left, right):
    return lax.dot_general(left, right, (((1,), (1,)), ((), ())), preferred_element_type=WIDE)


def dot_first(left, right):
    return lax.dot_general(left, right, (((0,), (0,)), ((), ())), preferred_element_type=WIDE)


def attend_kernel(which, group_ref, q_ref, k_ref, v_ref, out_ref, log_ref):
    keys, queries = k_ref.shape[0], q_ref.shape[0]
    scores = dot_last(k_ref[...], q_ref[...]) * HDIM ** (-0.5)
    scores = jnp.where(visible(group_ref[0], which, keys, queries), scores, MASKED)
    maximum = jnp.max(scores, axis=0, keepdims=True)
    weights = jnp.exp(scores - maximum)
    total = jnp.sum(weights, axis=0, keepdims=True)
    attn_low = (weights * (1.0 / total)).astype(LOW)
    out_ref[...] = dot_first(v_ref[...], attn_low).T.astype(LOW)
    log_ref[...] = (maximum + jnp.log(total))[None]


def attend_block(which, group, queries, keys, values, block):
    rows, span = queries.shape
    heads = span // HDIM
    whole = pl.BlockSpec((rows, HDIM), lambda h, g: (0, h))
    return pl.pallas_call(
        lambda *refs: attend_kernel(which, *refs),
        grid_spec=pltpu.PrefetchScalarGridSpec(
            num_scalar_prefetch=1,
            grid=(heads,),
            in_specs=[pl.BlockSpec((block, HDIM), lambda h, g: (which, h)), whole, whole],
            out_specs=[
                pl.BlockSpec((block, HDIM), lambda h, g: (0, h)),
                pl.BlockSpec((1, 1, block), lambda h, g: (h, 0, 0)),
            ],
        ),
        out_shape=[
            jax.ShapeDtypeStruct((block, span), LOW),
            jax.ShapeDtypeStruct((heads, 1, block), WIDE),
        ],
        compiler_params=params(),
        cost_estimate=pl.CostEstimate(
            flops=4 * block * rows * span,
            bytes_accessed=4 * rows * span,
            transcendentals=block * rows * heads,
        ),
    )(group, queries, keys, values)


def attend_back_kernel(which, first, group_ref, q_ref, k_ref, v_ref, grad_ref, log_ref, *refs):
    keys, queries = k_ref.shape[0], q_ref.shape[0]
    grad_q_ref, grad_k_ref, grad_v_ref = refs[-3:]
    scores = dot_last(k_ref[...], q_ref[...]) * HDIM ** (-0.5)
    probs = jnp.exp(scores - log_ref[0])
    probs = jnp.where(visible(group_ref[0], which, keys, queries), probs, 0.0)
    grad_probs = dot_last(v_ref[...], grad_ref[...])
    delta = jnp.sum(probs * grad_probs, axis=0, keepdims=True)
    grad_scores = (probs * (grad_probs - delta)).astype(LOW)
    grad_q_ref[...] = (dot_first(k_ref[...], grad_scores).T * HDIM ** (-0.5)).astype(LOW)
    key_part = plain(grad_scores, q_ref[...]) * HDIM ** (-0.5)
    value_part = plain(probs.astype(LOW), grad_ref[...])
    grad_k_ref[...] = key_part if first else refs[0][...] + key_part
    grad_v_ref[...] = value_part if first else refs[1][...] + value_part


def attend_block_back(which, group, queries, keys, values, grad, logs, sums, block):
    rows, span = queries.shape
    heads = span // HDIM
    whole = pl.BlockSpec((rows, HDIM), lambda h, g: (0, h))
    own = pl.BlockSpec((block, HDIM), lambda h, g: (0, h))
    carried = [] if sums is None else list(sums)
    return pl.pallas_call(
        lambda *refs: attend_back_kernel(which, sums is None, *refs),
        grid_spec=pltpu.PrefetchScalarGridSpec(
            num_scalar_prefetch=1,
            grid=(heads,),
            in_specs=[
                pl.BlockSpec((block, HDIM), lambda h, g: (which, h)),
                whole,
                whole,
                own,
                pl.BlockSpec((1, 1, block), lambda h, g: (h, 0, 0)),
            ]
            + [whole] * len(carried),
            out_specs=[own, whole, whole],
        ),
        out_shape=[
            jax.ShapeDtypeStruct((block, span), LOW),
            jax.ShapeDtypeStruct((rows, span), WIDE),
            jax.ShapeDtypeStruct((rows, span), WIDE),
        ],
        compiler_params=params(),
        cost_estimate=pl.CostEstimate(
            flops=10 * block * rows * span,
            bytes_accessed=20 * rows * span,
            transcendentals=block * rows * heads,
        ),
    )(group, queries, keys, values, grad, logs, *carried)


def turned_back(which, first, grads, cosine, sine):
    values = grads[which][:, first : first + HDIM].astype(WIDE)
    return turn(values, cosine, -sine)


def norm_sums_kernel(
    width, gq_ref, gk_ref, pre_ref, squares_ref, gain_ref, cos_ref, sin_ref, total_ref, col_ref
):
    span = gq_ref.shape[1]
    cosine, sine = cos_ref[...], sin_ref[...]
    factors = norm_factors(squares_ref, width)

    @pl.when(pl.program_id(0) == 0)
    def _():
        col_ref[...] = jnp.zeros_like(col_ref)

    for which in range(2):
        total = jnp.zeros(cosine.shape, WIDE)
        for first in range(0, span, HDIM):
            grad = turned_back(which, first, (gq_ref, gk_ref), cosine, sine)
            cols = slice(which * span + first, which * span + first + HDIM)
            product = grad * pre_ref[:, cols]
            total = total + product * gain_ref[which : which + 1, first : first + HDIM]
            col_ref[which : which + 1, first : first + HDIM] += jnp.sum(
                product * factors[which], axis=0, keepdims=True
            )
        total_ref[which : which + 1, :] = jnp.sum(total.T, axis=0, keepdims=True)


def norm_grads_kernel(
    width,
    gq_ref,
    gk_ref,
    gv_ref,
    pre_ref,
    squares_ref,
    total_ref,
    gain_ref,
    cos_ref,
    sin_ref,
    out_ref,
):
    span = gq_ref.shape[1]
    cosine, sine = cos_ref[...], sin_ref[...]
    factors = norm_factors(squares_ref, width)
    for which in range(2):
        factor = factors[which]
        mean = as_column(total_ref[which : which + 1] / width, HDIM)
        pull = factor * factor * factor * mean
        for first in range(0, span, HDIM):
            grad = turned_back(which, first, (gq_ref, gk_ref), cosine, sine)
            cols = slice(which * span + first, which * span + first + HDIM)
            scaled = grad * gain_ref[which : which + 1, first : first + HDIM]
            out_ref[:, cols] = (factor * scaled - pre_ref[:, cols] * pull).astype(LOW)
    out_ref[:, 2 * span :] = gv_ref[...].astype(LOW)


def norm_call(body, operands, kinds, outs, width, block):
    def spec(shape, kind):
        if kind == "rows":
            return pl.BlockSpec((block, shape[1]), lambda i: (i, 0))
        if kind == "line":
            return pl.BlockSpec((shape[0], block), lambda i: (0, i))
        return pl.BlockSpec(shape, lambda i: (0, 0))

    size = sum(o.size * o.dtype.itemsize for o in operands)
    return pl.pallas_call(
        lambda *refs: body(width, *refs),
        grid=(operands[0].shape[0] // block,),
        in_specs=[spec(o.shape, kind) for o, kind in zip(operands, kinds)],
        out_specs=[spec(shape, kind) for shape, _, kind in outs],
        out_shape=[jax.ShapeDtypeStruct(shape, dtype) for shape, dtype, _ in outs],
        compiler_params=params(),
        cost_estimate=pl.CostEstimate(flops=4 * size, bytes_accessed=size, transcendentals=0),
    )(*operands)


def silu_parts(gate_act):
    sigmoid_value = jax.nn.sigmoid(gate_act)
    return (gate_act * sigmoid_value, sigmoid_value)


def expert_hidden(rows, weights):
    gate_act = plain(rows, weights[0])
    up_act = plain(rows, weights[1])
    return (gate_act, up_act, (silu_parts(gate_act)[0] * up_act).astype(LOW))


def expert_produce(hidden_act, weights):
    return contract_last(hidden_act, weights[2]).astype(LOW)


def expert_forward(rows, weights):
    kept = expert_hidden(rows, weights)
    return (expert_produce(kept[2], weights), kept)


def expert_backward(grad_rows, kept, weights):
    gate_weight, up_weight, down_weight = weights
    gate_act, up_act, hidden_act = kept
    grad_hidden = plain(grad_rows, down_weight)
    activated, sigmoid_value = silu_parts(gate_act)
    grad_gate_act = (
        grad_hidden * up_act * sigmoid_value * (1.0 + gate_act * (1.0 - sigmoid_value))
    ).astype(LOW)
    grad_up_act = (grad_hidden * activated).astype(LOW)
    grad_route = contract_last(grad_gate_act, gate_weight) + contract_last(grad_up_act, up_weight)
    return (grad_route, grad_gate_act, grad_up_act)


def weight_total(left, right):
    return contract_first(left, right).astype(LOW)


def columns_of(values, tensor):
    half = values.shape[1] // 2
    return lax.dynamic_slice_in_dim(values, tensor * half, half, 1)


def their_grad(left, right):
    return contract_first(left, columns_of(right, 1 - lax.axis_index("tensor"))).astype(LOW)


def own_grad(left, right, arrived):
    mine = contract_first(left, columns_of(right, lax.axis_index("tensor")))
    return mine + arrived.astype(WIDE)


def owned_grad(total):
    return lax.psum_scatter(total, "tensor", scatter_dimension=1, tiled=True)


def halves(values):
    half = values.shape[0] // 2
    return (values[:half], values[half:])


def whole_weight(held):
    return lax.all_gather(held, "tensor", axis=1, tiled=True)


def softmax_rows(logits):
    weights = jnp.exp(logits - jnp.max(logits, axis=-1, keepdims=True))
    return weights / jnp.sum(weights, axis=-1, keepdims=True)


def pick_rows(picks, other_picks, blocks):
    pick = jnp.concatenate([picks, other_picks], axis=1)
    chosen = jnp.einsum("bst,btd->bsd", pick, blocks, preferred_element_type=jnp.float32)
    chosen = chosen.astype(LOW)
    capacity, width = picks.shape[1], blocks.shape[2]
    kept = chosen[:, :capacity].reshape(-1, width)
    arrived = hop(chosen[:, capacity:].reshape(-1, width), 1)
    return jnp.concatenate([kept, arrived], axis=0)


def slot_picks(ids, expert, capacity):
    routed = jnp.any(ids == expert, axis=1)
    tokens = ids.shape[2]
    line = jnp.arange(tokens, dtype=jnp.int32)
    earlier = (line[:, None] < line[None, :]).astype(LOW)
    position = plain(routed.astype(LOW), earlier).astype(jnp.int32)
    position = jnp.where(routed, position, -1)
    slots = jnp.arange(capacity, dtype=jnp.int32)
    return (position[:, None, :] == slots[None, :, None]).astype(LOW)


def chip_parts(rows, picks, other_picks):
    half = rows.shape[0] // 2
    return combine(rows[:half], hop(rows[half:], 1), picks, other_picks)


def combine(kept, arrived, picks, other_picks):
    shape = picks.shape[:2] + kept.shape[1:]
    both = jnp.concatenate([kept.reshape(shape), arrived.reshape(shape)], axis=1)
    pick = jnp.concatenate([picks, other_picks], axis=1)
    parts = jnp.einsum("bst,bsd->btd", pick, both, preferred_element_type=jnp.float32)
    return parts.astype(LOW)


def sum_chips(parts):
    return jnp.sum(over_chips(parts).astype(WIDE), axis=0)


def experts_by_blocks(
    low_second, cot_near, cotangent, all_ids, router, gate_weight, w_up, w_down, capacity
):
    shard, context = lax.axis_index("shard"), lax.axis_index("context")
    contexts = lax.axis_size("context")
    expert = shard * contexts + context
    other_expert = (shard ^ 1) * contexts + context
    token_count = low_second.shape[0]
    chips = lax.axis_size("shard") // 2
    same_core = 2 * jnp.arange(chips, dtype=jnp.int32) + (shard & 1)
    picks = []
    for turn in range(2):
        ids = jnp.take(all_ids, same_core * contexts + (context ^ turn), axis=0)
        far_ids = jnp.take(all_ids, (same_core ^ 1) * contexts + (context ^ turn), axis=0)
        picks.append(
            (
                slot_picks(ids, expert, capacity),
                slot_picks(ids, other_expert, capacity),
                slot_picks(far_ids, expert, capacity),
            )
        )

    def arrive(turn, rows):
        probs = softmax_rows(plain(rows, router))
        mine = jnp.arange(probs.shape[1], dtype=jnp.int32)[None, :] == expert
        return jnp.sum(jnp.where(mine, probs, 0.0), axis=1, keepdims=True)

    def leave(turn, produced, cot_rows, gate):
        cot_wide = cot_rows.astype(WIDE)
        produced_wide = produced.astype(WIDE)
        slot_grad = jnp.sum(produced_wide * cot_wide, axis=1)
        all_picks = jnp.concatenate([picks[turn][0], picks[turn][2]], axis=0).astype(WIDE)
        gate_grad = jnp.sum(all_picks * slot_grad.reshape(2 * chips, capacity)[:, :, None], axis=1)
        return (gate_grad, (gate * cot_wide).astype(LOW), (gate * produced_wide).astype(LOW))

    up_weight = whole_weight(w_up)
    near_chunk, across, w_down, cot_near, cotangent = sync(
        gather_chips(low_second), swap(low_second, "context"), w_down, cot_near, cotangent
    )
    cot_across = swap(cotangent, "context")
    near_rows = pick_rows(*picks[0][:2], near_chunk)
    down_weight = whole_weight(w_down)
    weights = (gate_weight, up_weight, down_weight)
    near_kept = expert_hidden(near_rows, weights)
    near_hidden, far_chunk, cot_across = sync(near_kept[2], gather_chips(across), cot_across)
    near_kept = near_kept[:2] + (near_hidden,)
    cot_far = gather_chips(cot_across)
    far_rows = pick_rows(*picks[1][:2], far_chunk)
    far_rows, down_weight = sync(far_rows, down_weight)
    weights = (gate_weight, up_weight, down_weight)
    far_kept = expert_hidden(far_rows, weights)
    near_cot, far_cot = pick_rows(*picks[0][:2], cot_near), pick_rows(*picks[1][:2], cot_far)
    gate = arrive(0, near_rows)
    produced = expert_produce(near_hidden, weights)
    near_gate_grad, near_grad_rows, weighted = leave(0, produced, near_cot, gate)
    mixture_parts = chip_parts(weighted, *picks[0][:2])
    gate = arrive(1, far_rows)
    produced = expert_produce(far_kept[2], weights)
    far_gate_grad, far_grad_rows, far_weighted = leave(1, produced, far_cot, gate)
    rest_parts = chip_parts(far_weighted, *picks[1][:2])
    lines = jnp.stack([near_gate_grad, far_gate_grad], axis=1)
    lines = jnp.where(context == 0, lines, lines[:, ::-1])
    mine, far = lines[:chips], lines[chips:]
    low_core = (shard & 1) == 0
    lines = jnp.stack([jnp.where(low_core, mine, far), jnp.where(low_core, far, mine)], axis=1)
    lines = lines.reshape(-1, token_count)
    by_expert = lax.all_to_all(lines, ("shard", "context"), split_axis=0, concat_axis=0, tiled=True)

    def both(near, far):
        return jnp.concatenate([near, far], axis=0)

    far_route, far_gate_act, far_up_act = expert_backward(far_grad_rows, far_kept, weights)
    far_route, near_grad_rows, far_grad_rows = sync(far_route, near_grad_rows, far_grad_rows)
    down_pair = (both(near_grad_rows, far_grad_rows), both(near_kept[2], far_kept[2]))
    down_total = weight_total(*down_pair)
    far_parts = chip_parts(far_route.astype(LOW), *picks[1][:2])
    near_grad_rows, far_parts, by_expert, down_total = sync(
        near_grad_rows, far_parts, by_expert, down_total
    )
    down_grad = owned_grad(down_total)
    near_route, near_gate_act, near_up_act = expert_backward(near_grad_rows, near_kept, weights)
    near_route = near_route.astype(LOW)
    near_half = near_route.shape[0] // 2
    near_swapped = hop(near_route[near_half:], 1)
    near_route, near_gate_act = sync(near_route, near_gate_act)
    all_rows = both(near_rows, far_rows)
    near_swapped, far_grad, near_up_act, gate_total = sync(
        near_swapped,
        sum_chips(far_parts).astype(LOW),
        near_up_act,
        weight_total(all_rows, both(near_gate_act, far_gate_act)),
    )
    gate_grad = owned_grad(gate_total)
    near_parts = combine(near_route[:near_half], near_swapped, *picks[0][:2])
    up_pair = (all_rows, both(near_up_act, far_up_act))
    far_arrived = swap(far_grad, "context")
    grad, mixture_parts, rest_parts, up_theirs, down_grad = sync(
        sum_chips(near_parts) + far_arrived.astype(WIDE),
        mixture_parts,
        rest_parts,
        their_grad(*up_pair),
        down_grad,
    )
    later = (mixture_parts, rest_parts, gate_grad, down_grad, up_theirs, up_pair)
    return (grad, by_expert.T, later)


def move_slots(buffer):
    return lax.all_to_all(buffer, ("shard", "context"), split_axis=0, concat_axis=0, tiled=True)


def experts_by_slots(low_second, cotangent, expert_ids, router_probs, weights, capacity):
    row_count, model_width = low_second.shape
    expert_count = router_probs.shape[1]
    top_count = expert_ids.shape[1]
    choose = expert_ids[:, :, None] == jnp.arange(expert_count, dtype=jnp.int32)[None, None, :]
    gate_probs = jnp.sum(jnp.where(choose, router_probs[:, None, :], 0.0), axis=2)
    route_total = row_count * top_count
    flat_ids = expert_ids.reshape(-1)
    onehot = (flat_ids[:, None] == jnp.arange(expert_count, dtype=jnp.int32)[None, :]).astype(
        jnp.int32
    )
    before = jnp.cumsum(onehot, axis=0) - onehot
    route_slot = flat_ids * capacity + jnp.sum(before * onehot, axis=1)
    route_of_slot = (
        jnp.full((expert_count * capacity,), route_total, jnp.int32)
        .at[route_slot]
        .set(jnp.arange(route_total, dtype=jnp.int32))
    )
    filled = route_of_slot < route_total
    route_clipped = jnp.minimum(route_of_slot, route_total - 1)
    token_of_slot = route_clipped // top_count
    slot_shape = (expert_count, capacity, model_width)
    flat_shape = (expert_count * capacity, model_width)
    sending = jnp.where(filled[:, None], low_second[token_of_slot], jnp.zeros((), LOW))
    rows = move_slots(sending.reshape(slot_shape)).reshape(flat_shape)
    produced, kept = expert_forward(rows, weights)
    returned = move_slots(produced.reshape(slot_shape)).reshape(flat_shape)
    chosen = returned[route_slot].reshape(row_count, top_count, model_width).astype(WIDE)
    mixture = jnp.sum(gate_probs[:, :, None] * chosen, axis=1)
    grad_top = cotangent.astype(WIDE)
    grad_gates = jnp.sum(chosen * grad_top[:, None, :], axis=2)
    slot_gate = jnp.where(filled, gate_probs.reshape(-1)[route_clipped], 0.0)
    sending_grad = (slot_gate[:, None] * grad_top[token_of_slot]).astype(LOW)
    grad_rows = move_slots(sending_grad.reshape(slot_shape)).reshape(flat_shape)
    grad_route, grad_gate_act, grad_up_act = expert_backward(grad_rows, kept, weights)
    returned_grad = move_slots(grad_route.astype(LOW).reshape(slot_shape)).reshape(flat_shape)
    grad = jnp.sum(
        returned_grad[route_slot].reshape(row_count, top_count, model_width).astype(WIDE), axis=1
    )
    by_expert = jnp.sum(jnp.where(choose, grad_gates[:, :, None], 0.0), axis=1)
    pairs = [(rows, grad_gate_act), (rows, grad_up_act), (grad_rows, kept[2])]
    grads = tuple(owned_grad(weight_total(*pair)) for pair in pairs)
    return (grad, by_expert, mixture, grads)


def local(
    hidden_in,
    cotangent,
    w_query,
    w_key,
    w_value,
    w_out,
    w_router,
    norm_first,
    norm_second,
    query_gain,
    key_gain,
    w_gate,
    w_up,
    w_down,
    expert_ids,
):
    group_index = lax.axis_index(("context", "tensor"))
    row_count, model_width = hidden_in.shape
    column_span = w_query.shape[1]
    expert_count = w_router.shape[1]
    top_count = expert_ids.shape[1]
    capacity = max(2, row_count * top_count * 5 // (4 * expert_count))
    by_blocks = 2 * capacity >= row_count
    device_count = model_width // norm_first.shape[0]

    router_rows = w_router.shape[0]
    small = gather_small(
        jnp.concatenate(
            [
                w_router.reshape(-1),
                norm_first,
                norm_second,
                query_gain,
                key_gain,
                expert_ids.T.reshape(-1).astype(LOW),
            ],
            axis=0,
        )
    )
    hidden_blocks = gather_group(hidden_in)
    hidden_blocks[3], gate_early = sync(hidden_blocks[3], w_gate[0])
    gate_weight = whole_weight(gate_early)
    packed = lax.all_gather(
        jnp.concatenate([w_query, w_key, w_value, w_out], axis=1), "shard", axis=0, tiled=True
    )
    router_size = router_rows * expert_count
    router_full = small[:, :router_size].reshape(model_width, expert_count)
    gains = [
        small[:, router_size + i * router_rows : router_size + (i + 1) * router_rows]
        .reshape(model_width)
        .astype(WIDE)
        for i in range(4)
    ]
    gain_first, gain_second, gain_query, gain_key = gains
    if by_blocks:
        tensors = lax.axis_size("tensor")
        all_ids = small[:, router_size + 4 * router_rows :].astype(jnp.int32)
        all_ids = all_ids.reshape(-1, tensors, top_count, row_count)
        all_ids = lax.dynamic_index_in_dim(all_ids, lax.axis_index("tensor"), 1, False)

    qkv_cols = packed[:, : 3 * column_span]
    out_cols = packed[:, 3 * column_span :]
    inputs = hidden_in.astype(WIDE)
    factor_first = rms_scale(inputs, gain_first)[1]
    low_blocks, pre_blocks = [], []
    for block in hidden_blocks:
        low_block = rms_scale(block.astype(WIDE), gain_first)[0].astype(LOW)
        low_blocks.append(low_block)
        pre_blocks.append(plain(low_block, qkv_cols))
    low_group = jnp.concatenate(low_blocks, axis=0)
    pre = jnp.concatenate(pre_blocks, axis=0)
    group_rows = low_group.shape[0]
    line = jnp.arange(group_rows, dtype=jnp.int32)
    place = ((line // row_count) ^ group_index) * row_count + line % row_count
    cosine, sine = rope_tables(place)
    gain_cols = jnp.stack(
        [
            lax.dynamic_slice_in_dim(gain, group_index * column_span, column_span, 0)
            for gain in (gain_query, gain_key)
        ]
    )

    def over_group(stacked):
        stacked = stacked.reshape(2, 4, -1)
        stacked = stacked + swap(stacked, "tensor")[:, jnp.array([1, 0, 3, 2])]
        stacked = stacked + swap(stacked, "context")[:, jnp.array([2, 3, 0, 1])]
        return stacked.reshape(2, -1)

    own_squares, early_cot = sync(
        jnp.stack(
            [
                jnp.sum(jnp.square(pre[:, i * column_span : (i + 1) * column_span]), axis=1)
                for i in range(2)
            ]
        ),
        cotangent,
    )
    if by_blocks:
        cot_near = gather_chips(early_cot)
    squares = over_group(own_squares)
    query_heads, key_heads, value_heads = prepare(
        pre, squares, gain_cols, cosine, sine, model_width, row_count
    )
    group = group_index[None].astype(jnp.int32)
    blocks, logs = [None] * 4, [None] * 4
    for k in (3, 2, 1, 0):
        blocks[k], logs[k] = attend_block(
            k, group, query_heads, key_heads, value_heads, row_count
        )
    parts = [contract_last(block, out_cols) for block in blocks]
    far_part, gate_weight = sync(parts[3].astype(LOW), gate_weight)
    far = swap(far_part, "tensor")
    far, near_part, part = sync(far, parts[1].astype(LOW), parts[2])
    across = swap((part + far.astype(WIDE)).astype(LOW), "context")
    near = swap(near_part, "tensor")
    if by_blocks:
        across, cot_near = sync(across, cot_near)
    middle = inputs + parts[0] + near.astype(WIDE) + across.astype(WIDE)
    normed_second, factor_second = rms_scale(middle, gain_second)
    low_second = normed_second.astype(LOW)
    router_probs = softmax_rows(plain(low_second, router_full))
    low_second, late_up, late_down = sync(low_second, w_up[0], w_down[0])
    if by_blocks:
        grad_from_experts, grad_router_probs, later = experts_by_blocks(
            low_second,
            cot_near,
            cotangent,
            all_ids,
            router_full,
            gate_weight,
            late_up,
            late_down,
            capacity,
        )
        mixture_parts, rest_parts, gate_grad, down_grad, up_theirs, up_pair = later
        up_halves = halves(up_theirs)
    else:
        weights = (gate_weight, whole_weight(late_up), whole_weight(late_down))
        grad_from_experts, grad_router_probs, mixture, expert_grads = experts_by_slots(
            low_second, cotangent, expert_ids, router_probs, weights, capacity
        )
    grad_logits = (
        router_probs
        * (grad_router_probs - jnp.sum(router_probs * grad_router_probs, axis=1, keepdims=True))
    ).astype(LOW)
    grad_router_weight = contract_first(low_second, grad_logits)
    grad_second = grad_from_experts + contract_last(grad_logits, router_full)
    grad_normed_second, grad_gain_second = rms_back(middle, factor_second, gain_second, grad_second)
    grad_middle = cotangent.astype(WIDE) + grad_normed_second
    grad_branch = grad_middle.astype(LOW)
    near_piece, across = swap(grad_branch, "tensor"), swap(grad_branch, "context")

    def piece_back(k, piece, sums):
        grad_queries, *sums = attend_block_back(
            k,
            group,
            query_heads,
            key_heads,
            value_heads,
            plain(piece, out_cols).astype(LOW),
            logs[k],
            sums,
            row_count,
        )
        return (grad_queries, tuple(sums))

    own_query, own_sums = piece_back(0, grad_branch, None)
    if by_blocks:
        rest = sum_chips(rest_parts).astype(LOW)
    if by_blocks:
        across, own_sums, rest, gate_grad = sync(across, tuple(own_sums), rest, gate_grad)
        others = lax.all_gather(rest, "context", axis=0, tiled=False)
    last = swap(across, "tensor")
    near_query, near_sums = piece_back(1, near_piece, own_sums)
    across_query, across_sums = piece_back(2, across, near_sums)
    last, across_sums = sync(last, across_sums)
    if by_blocks:
        last, up_early, mixture_parts = sync(last, up_halves[0], mixture_parts)
        mixture = sum_chips(mixture_parts)
    pieces = [grad_branch, near_piece, across, last]
    last_query, sums = piece_back(3, last, across_sums)
    grad_queries = [own_query, near_query, across_query, last_query]
    grad_query_heads = jnp.concatenate(grad_queries, axis=0)
    out_total = contract_first(pieces[0], blocks[0])
    for k in range(1, 4):
        out_total = out_total + contract_first(pieces[k], blocks[k])
    out_total = out_total.astype(LOW)
    totals, gain_grads = norm_call(
        norm_sums_kernel,
        (grad_query_heads, sums[0], pre, squares, gain_cols, cosine, sine),
        ("rows", "rows", "rows", "line", "whole", "rows", "rows"),
        (((2, group_rows), WIDE, "line"), ((2, column_span), WIDE, "whole")),
        model_width,
        row_count,
    )
    if by_blocks:
        totals, up_first = sync(totals, swap(up_early, "tensor"))
    totals = over_group(totals)
    if by_blocks:
        totals, up_late = sync(totals, up_halves[1])
    (grad_pre,) = norm_call(
        norm_grads_kernel,
        (grad_query_heads, *sums, pre, squares, totals, gain_cols, cosine, sine),
        ("rows", "rows", "rows", "rows", "line", "line", "whole", "rows", "rows"),
        (((group_rows, 3 * column_span), LOW, "rows"),),
        model_width,
        row_count,
    )

    def block_of(values, k):
        return values[k * row_count : (k + 1) * row_count]

    far_part = contract_last(block_of(grad_pre, 3), qkv_cols).astype(LOW)
    if by_blocks:
        far_part, grad_pre, up_second, others, mixture, out_total = sync(
            far_part, grad_pre, swap(up_late, "tensor"), others, mixture, out_total
        )
        other = lax.dynamic_index_in_dim(others, lax.axis_index("context") ^ 1, 0, False)
        mixture = mixture + other.astype(WIDE)
    block_output = (middle + mixture).astype(LOW)
    out_dealt = lax.all_to_all(out_total, "shard", split_axis=0, concat_axis=0, tiled=True)
    far = swap(far_part, "tensor")
    head_total = contract_first(low_group, grad_pre).astype(LOW)
    parts = [contract_last(block_of(grad_pre, k), qkv_cols) for k in range(3)]
    zero_gain = jnp.zeros((2, model_width), WIDE)
    grad_gains = lax.dynamic_update_slice(zero_gain, gain_grads, (0, group_index * column_span))
    by_device = [
        one.reshape(device_count, -1)
        for one in (grad_router_weight, grad_gain_second, grad_gains[0], grad_gains[1])
    ]
    early = scatter_small(jnp.concatenate(by_device, axis=1))
    far, head_total, near_part, early, out_dealt, *parts = sync(
        far, head_total, parts[1].astype(LOW), early, out_dealt, parts[0], parts[2]
    )
    across = swap((parts[1] + far.astype(WIDE)).astype(LOW), "context")
    near = swap(near_part, "tensor")
    head_grads = lax.psum_scatter(head_total, "shard", scatter_dimension=0, tiled=True).astype(WIDE)
    if by_blocks:
        up_arrived = jnp.concatenate([up_first, up_second], axis=0)
        near, gate_grad, down_grad, up_arrived = sync(near, gate_grad, down_grad, up_arrived)
        expert_grads = (gate_grad, own_grad(*up_pair, up_arrived), down_grad)
    out_grad = jnp.sum(
        out_dealt.reshape((lax.axis_size("shard"),) + w_out.shape).astype(WIDE), axis=0
    )
    grad_first = parts[0] + near.astype(WIDE) + across.astype(WIDE)
    grad_normed_first, grad_gain_first = rms_back(inputs, factor_first, gain_first, grad_first)
    grad_input = grad_middle + grad_normed_first
    late = scatter_small(grad_gain_first.reshape(device_count, -1))
    router_grad = early[:router_size].reshape(router_rows, expert_count)
    rest = early[router_size:].reshape(3, router_rows)
    return (
        block_output,
        grad_input,
        head_grads[:, :column_span],
        head_grads[:, column_span : 2 * column_span],
        head_grads[:, 2 * column_span : 3 * column_span],
        out_grad,
        router_grad,
        late,
        rest[0],
        rest[1],
        rest[2],
        *(grad.astype(WIDE)[None] for grad in expert_grads),
    )


def solution(mesh):
    rows = P(("shard", "context", "tensor"), None)
    columns = P("shard", ("context", "tensor"))
    vector = P(("shard", "context", "tensor"))
    expert = P(("shard", "context"), None, "tensor")
    return jax.shard_map(
        local,
        mesh=mesh,
        in_specs=(
            (rows, rows)
            + (columns,) * 4
            + (rows,)
            + (vector,) * 4
            + (expert,) * 3
            + (rows,)
        ),
        out_specs=((rows, rows) + (columns,) * 4 + (rows,) + (vector,) * 4 + (expert,) * 3),
        check_vma=False,
    )
```

```python
import jax
import jax.numpy as jnp
from jax import lax
from jax.experimental import pallas as pl
from jax.experimental.pallas import tpu as pltpu
from jax.sharding import PartitionSpec as P

HDIM = 128


EPSILON = 1e-05
MASKED = -1e30
LOW = jnp.bfloat16
WIDE = jnp.float32
SWAP = ((0, 1), (1, 0))


def sync(*values):
    return lax.optimization_barrier(values)


def rms_scale(values, gain):
    factor = lax.rsqrt(jnp.mean(values * values, axis=-1, keepdims=True) + EPSILON)
    return (values * factor * gain, factor)


def rms_back(values, factor, gain, grad_out):
    scaled = grad_out * gain
    mean_term = jnp.mean(scaled * values, axis=-1, keepdims=True)
    grad_values = factor * scaled - values * (factor * factor * factor) * mean_term
    return (grad_values, jnp.sum(grad_out * values * factor, axis=0))


def rope_tables(positions):
    half_size = HDIM // 2
    frequency = 10000.0 ** (-2.0 * jnp.arange(half_size, dtype=WIDE) / HDIM)
    angles = positions.astype(WIDE)[:, None] * frequency[None, :]
    cosine, sine = jnp.cos(angles), jnp.sin(angles)
    return (
        jnp.concatenate([cosine, cosine], axis=1),
        jnp.concatenate([-sine, sine], axis=1),
    )


def contract_last(left, right):
    return lax.dot_general(
        left, right, (((1,), (1,)), ((), ())), preferred_element_type=jnp.float32
    )


def contract_first(left, right):
    return lax.dot_general(
        left, right, (((0,), (0,)), ((), ())), preferred_element_type=jnp.float32
    )


def plain(left, right):
    return jnp.dot(left, right, preferred_element_type=jnp.float32)


def swap(values, axis):
    return lax.ppermute(values, axis, SWAP)


def hop(values, distance):
    count = lax.axis_size("shard")
    return lax.ppermute(values, "shard", tuple((i, i ^ distance) for i in range(count)))


def gather_group(block):
    near = swap(block, "tensor")
    across = swap(block, "context")
    return [block, near, across, swap(across, "tensor")]


def scatter_group(parts):
    far, near = sync(swap(parts[3].astype(LOW), "tensor"), parts[1].astype(LOW))
    across = swap((parts[2] + far.astype(WIDE)).astype(LOW), "context")
    return parts[0] + swap(near, "tensor").astype(WIDE) + across.astype(WIDE)


def over_chips(blocks):
    count = lax.axis_size("shard")
    groups = [list(range(core, count, 2)) for core in range(2)]
    return lax.all_to_all(
        blocks, "shard", split_axis=0, concat_axis=0, axis_index_groups=groups, tiled=True
    )


def gather_chips(block):
    chips = lax.axis_size("shard") // 2
    return over_chips(jnp.broadcast_to(block[None], (chips,) + block.shape))


DEVICES = ("shard", "context", "tensor")


def deal(rows):
    return lax.all_to_all(rows, DEVICES, split_axis=0, concat_axis=0, tiled=True)


def device_total():
    return lax.axis_size("shard") * lax.axis_size("context") * lax.axis_size("tensor")


def gather_small(row):
    return deal(jnp.broadcast_to(row[None], (device_total(), row.shape[0])))


def scatter_small(rows):
    return jnp.sum(deal(rows), axis=0)


def params():
    return pltpu.CompilerParams(vmem_limit_bytes=48 * 1024 * 1024)


def as_column(row, width):
    return jnp.broadcast_to(row, (width, row.shape[1])).T


def turn(values, cosine, sine):
    return values * cosine + pltpu.roll(values, HDIM // 2, 1) * sine


def norm_factors(squares_ref, width):
    factors = lax.rsqrt(squares_ref[...] / width + EPSILON)
    return as_column(factors[0:1], HDIM), as_column(factors[1:2], HDIM)


def prepare_kernel(width, pre_ref, squares_ref, gain_ref, cos_ref, sin_ref, q_ref, k_ref, v_ref):
    span = q_ref.shape[1]
    cosine, sine = cos_ref[...], sin_ref[...]
    factors = norm_factors(squares_ref, width)
    for which, out_ref in ((0, q_ref), (1, k_ref)):
        for first in range(0, span, HDIM):
            cols = slice(which * span + first, which * span + first + HDIM)
            gain = gain_ref[which : which + 1, first : first + HDIM]
            normed = pre_ref[:, cols] * factors[which] * gain
            out_ref[:, first : first + HDIM] = turn(normed, cosine, sine).astype(LOW)
    v_ref[...] = pre_ref[:, 2 * span :].astype(LOW)


def prepare(pre, squares, gain_cols, cosine, sine, width, block):
    rows, total = pre.shape
    span = total // 3
    row_block = lambda cols: pl.BlockSpec((block, cols), lambda i: (i, 0))
    return pl.pallas_call(
        lambda *refs: prepare_kernel(width, *refs),
        grid=(rows // block,),
        in_specs=[
            row_block(total),
            pl.BlockSpec((2, block), lambda i: (0, i)),
            pl.BlockSpec((2, span), lambda i: (0, 0)),
            row_block(HDIM),
            row_block(HDIM),
        ],
        out_specs=[row_block(span)] * 3,
        out_shape=[jax.ShapeDtypeStruct((rows, span), LOW)] * 3,
        compiler_params=params(),
        cost_estimate=pl.CostEstimate(
            flops=10 * rows * total, bytes_accessed=6 * rows * total, transcendentals=0
        ),
    )(pre, squares, gain_cols, cosine, sine)


def visible(group, which, keys, queries):
    line = lax.broadcasted_iota(jnp.int32, (keys, queries), 0)
    key_place = ((line // queries) ^ group) * queries + line % queries
    query_place = (which ^ group) * queries + lax.broadcasted_iota(
        jnp.int32, (keys, queries), 1
    )
    return query_place >= key_place


def dot_last(left, right):
    return lax.dot_general(left, right, (((1,), (1,)), ((), ())), preferred_element_type=WIDE)


def dot_first(left, right):
    return lax.dot_general(left, right, (((0,), (0,)), ((), ())), preferred_element_type=WIDE)


def attend_kernel(which, group_ref, q_ref, k_ref, v_ref, out_ref, log_ref):
    keys, queries = k_ref.shape[0], q_ref.shape[0]
    scores = dot_last(k_ref[...], q_ref[...]) * HDIM ** (-0.5)
    scores = jnp.where(visible(group_ref[0], which, keys, queries), scores, MASKED)
    maximum = jnp.max(scores, axis=0, keepdims=True)
    weights = jnp.exp(scores - maximum)
    total = jnp.sum(weights, axis=0, keepdims=True)
    attn_low = (weights * (1.0 / total)).astype(LOW)
    out_ref[...] = dot_first(v_ref[...], attn_low).T.astype(LOW)
    log_ref[...] = (maximum + jnp.log(total))[None]


def attend_block(which, group, queries, keys, values, block):
    rows, span = queries.shape
    heads = span // HDIM
    whole = pl.BlockSpec((rows, HDIM), lambda h, g: (0, h))
    return pl.pallas_call(
        lambda *refs: attend_kernel(which, *refs),
        grid_spec=pltpu.PrefetchScalarGridSpec(
            num_scalar_prefetch=1,
            grid=(heads,),
            in_specs=[pl.BlockSpec((block, HDIM), lambda h, g: (which, h)), whole, whole],
            out_specs=[
                pl.BlockSpec((block, HDIM), lambda h, g: (0, h)),
                pl.BlockSpec((1, 1, block), lambda h, g: (h, 0, 0)),
            ],
        ),
        out_shape=[
            jax.ShapeDtypeStruct((block, span), LOW),
            jax.ShapeDtypeStruct((heads, 1, block), WIDE),
        ],
        compiler_params=params(),
        cost_estimate=pl.CostEstimate(
            flops=4 * block * rows * span,
            bytes_accessed=4 * rows * span,
            transcendentals=block * rows * heads,
        ),
    )(group, queries, keys, values)


def attend_back_kernel(which, first, group_ref, q_ref, k_ref, v_ref, grad_ref, log_ref, *refs):
    keys, queries = k_ref.shape[0], q_ref.shape[0]
    grad_q_ref, grad_k_ref, grad_v_ref = refs[-3:]
    scores = dot_last(k_ref[...], q_ref[...]) * HDIM ** (-0.5)
    probs = jnp.exp(scores - log_ref[0])
    probs = jnp.where(visible(group_ref[0], which, keys, queries), probs, 0.0)
    grad_probs = dot_last(v_ref[...], grad_ref[...])
    delta = jnp.sum(probs * grad_probs, axis=0, keepdims=True)
    grad_scores = (probs * (grad_probs - delta)).astype(LOW)
    grad_q_ref[...] = (dot_first(k_ref[...], grad_scores).T * HDIM ** (-0.5)).astype(LOW)
    key_part = plain(grad_scores, q_ref[...]) * HDIM ** (-0.5)
    value_part = plain(probs.astype(LOW), grad_ref[...])
    grad_k_ref[...] = key_part if first else refs[0][...] + key_part
    grad_v_ref[...] = value_part if first else refs[1][...] + value_part


def attend_block_back(which, group, queries, keys, values, grad, logs, sums, block):
    rows, span = queries.shape
    heads = span // HDIM
    whole = pl.BlockSpec((rows, HDIM), lambda h, g: (0, h))
    own = pl.BlockSpec((block, HDIM), lambda h, g: (0, h))
    carried = [] if sums is None else list(sums)
    return pl.pallas_call(
        lambda *refs: attend_back_kernel(which, sums is None, *refs),
        grid_spec=pltpu.PrefetchScalarGridSpec(
            num_scalar_prefetch=1,
            grid=(heads,),
            in_specs=[
                pl.BlockSpec((block, HDIM), lambda h, g: (which, h)),
                whole,
                whole,
                own,
                pl.BlockSpec((1, 1, block), lambda h, g: (h, 0, 0)),
            ]
            + [whole] * len(carried),
            out_specs=[own, whole, whole],
        ),
        out_shape=[
            jax.ShapeDtypeStruct((block, span), LOW),
            jax.ShapeDtypeStruct((rows, span), WIDE),
            jax.ShapeDtypeStruct((rows, span), WIDE),
        ],
        compiler_params=params(),
        cost_estimate=pl.CostEstimate(
            flops=10 * block * rows * span,
            bytes_accessed=20 * rows * span,
            transcendentals=block * rows * heads,
        ),
    )(group, queries, keys, values, grad, logs, *carried)


def turned_back(which, first, grads, cosine, sine):
    values = grads[which][:, first : first + HDIM].astype(WIDE)
    return turn(values, cosine, -sine)


def norm_sums_kernel(
    width, gq_ref, gk_ref, pre_ref, squares_ref, gain_ref, cos_ref, sin_ref, total_ref, col_ref
):
    span = gq_ref.shape[1]
    cosine, sine = cos_ref[...], sin_ref[...]
    factors = norm_factors(squares_ref, width)

    @pl.when(pl.program_id(0) == 0)
    def _():
        col_ref[...] = jnp.zeros_like(col_ref)

    for which in range(2):
        total = jnp.zeros(cosine.shape, WIDE)
        for first in range(0, span, HDIM):
            grad = turned_back(which, first, (gq_ref, gk_ref), cosine, sine)
            cols = slice(which * span + first, which * span + first + HDIM)
            product = grad * pre_ref[:, cols]
            total = total + product * gain_ref[which : which + 1, first : first + HDIM]
            col_ref[which : which + 1, first : first + HDIM] += jnp.sum(
                product * factors[which], axis=0, keepdims=True
            )
        total_ref[which : which + 1, :] = jnp.sum(total.T, axis=0, keepdims=True)


def norm_grads_kernel(
    width,
    gq_ref,
    gk_ref,
    gv_ref,
    pre_ref,
    squares_ref,
    total_ref,
    gain_ref,
    cos_ref,
    sin_ref,
    out_ref,
):
    span = gq_ref.shape[1]
    cosine, sine = cos_ref[...], sin_ref[...]
    factors = norm_factors(squares_ref, width)
    for which in range(2):
        factor = factors[which]
        mean = as_column(total_ref[which : which + 1] / width, HDIM)
        pull = factor * factor * factor * mean
        for first in range(0, span, HDIM):
            grad = turned_back(which, first, (gq_ref, gk_ref), cosine, sine)
            cols = slice(which * span + first, which * span + first + HDIM)
            scaled = grad * gain_ref[which : which + 1, first : first + HDIM]
            out_ref[:, cols] = (factor * scaled - pre_ref[:, cols] * pull).astype(LOW)
    out_ref[:, 2 * span :] = gv_ref[...].astype(LOW)


def norm_call(body, operands, kinds, outs, width, block):
    def spec(shape, kind):
        if kind == "rows":
            return pl.BlockSpec((block, shape[1]), lambda i: (i, 0))
        if kind == "line":
            return pl.BlockSpec((shape[0], block), lambda i: (0, i))
        return pl.BlockSpec(shape, lambda i: (0, 0))

    size = sum(o.size * o.dtype.itemsize for o in operands)
    return pl.pallas_call(
        lambda *refs: body(width, *refs),
        grid=(operands[0].shape[0] // block,),
        in_specs=[spec(o.shape, kind) for o, kind in zip(operands, kinds)],
        out_specs=[spec(shape, kind) for shape, _, kind in outs],
        out_shape=[jax.ShapeDtypeStruct(shape, dtype) for shape, dtype, _ in outs],
        compiler_params=params(),
        cost_estimate=pl.CostEstimate(flops=4 * size, bytes_accessed=size, transcendentals=0),
    )(*operands)


def silu_parts(gate_act):
    sigmoid_value = jax.nn.sigmoid(gate_act)
    return (gate_act * sigmoid_value, sigmoid_value)


def expert_hidden(rows, weights):
    gate_act = plain(rows, weights[0])
    up_act = plain(rows, weights[1])
    return (gate_act, up_act, (silu_parts(gate_act)[0] * up_act).astype(LOW))


def expert_produce(hidden_act, weights):
    return contract_last(hidden_act, weights[2]).astype(LOW)


def expert_forward(rows, weights):
    kept = expert_hidden(rows, weights)
    return (expert_produce(kept[2], weights), kept)


def expert_backward(grad_rows, kept, weights):
    gate_weight, up_weight, down_weight = weights
    gate_act, up_act, hidden_act = kept
    grad_hidden = plain(grad_rows, down_weight)
    activated, sigmoid_value = silu_parts(gate_act)
    grad_gate_act = (
        grad_hidden * up_act * sigmoid_value * (1.0 + gate_act * (1.0 - sigmoid_value))
    ).astype(LOW)
    grad_up_act = (grad_hidden * activated).astype(LOW)
    grad_route = contract_last(grad_gate_act, gate_weight) + contract_last(grad_up_act, up_weight)
    return (grad_route, grad_gate_act, grad_up_act)


def weight_total(left, right):
    return contract_first(left, right).astype(LOW)


def columns_of(values, tensor):
    half = values.shape[1] // 2
    return lax.dynamic_slice_in_dim(values, tensor * half, half, 1)


def their_grad(left, right):
    return contract_first(left, columns_of(right, 1 - lax.axis_index("tensor"))).astype(LOW)


def my_grad(left, right):
    return contract_first(left, columns_of(right, lax.axis_index("tensor")))


def owned_grad(total):
    return lax.psum_scatter(total, "tensor", scatter_dimension=1, tiled=True)


def halves(values):
    half = values.shape[0] // 2
    return (values[:half], values[half:])


def whole_weight(held):
    return lax.all_gather(held, "tensor", axis=1, tiled=True)


def softmax_rows(logits):
    weights = jnp.exp(logits - jnp.max(logits, axis=-1, keepdims=True))
    return weights / jnp.sum(weights, axis=-1, keepdims=True)


def pick_rows(picks, other_picks, blocks):
    pick = jnp.concatenate([picks, other_picks], axis=1)
    chosen = jnp.einsum("bst,btd->bsd", pick, blocks, preferred_element_type=jnp.float32)
    chosen = chosen.astype(LOW)
    capacity, width = picks.shape[1], blocks.shape[2]
    kept = chosen[:, :capacity].reshape(-1, width)
    arrived = hop(chosen[:, capacity:].reshape(-1, width), 1)
    return jnp.concatenate([kept, arrived], axis=0)


def slot_picks(ids, expert, capacity):
    routed = jnp.any(ids == expert, axis=1)
    tokens = ids.shape[2]
    line = jnp.arange(tokens, dtype=jnp.int32)
    earlier = (line[:, None] < line[None, :]).astype(LOW)
    position = plain(routed.astype(LOW), earlier).astype(jnp.int32)
    position = jnp.where(routed, position, -1)
    slots = jnp.arange(capacity, dtype=jnp.int32)
    return (position[:, None, :] == slots[None, :, None]).astype(LOW)


def chip_parts(rows, picks, other_picks):
    half = rows.shape[0] // 2
    return combine(rows[:half], hop(rows[half:], 1), picks, other_picks)


def combine(kept, arrived, picks, other_picks):
    shape = picks.shape[:2] + kept.shape[1:]
    both = jnp.concatenate([kept.reshape(shape), arrived.reshape(shape)], axis=1)
    pick = jnp.concatenate([picks, other_picks], axis=1)
    parts = jnp.einsum("bst,bsd->btd", pick, both, preferred_element_type=jnp.float32)
    return parts.astype(LOW)


def sum_chips(parts):
    return jnp.sum(over_chips(parts).astype(WIDE), axis=0)


def experts_by_blocks(
    low_second, cot_near, cotangent, all_ids, router, gate_weight, w_up, w_down, capacity
):
    shard, context = lax.axis_index("shard"), lax.axis_index("context")
    contexts = lax.axis_size("context")
    expert = shard * contexts + context
    other_expert = (shard ^ 1) * contexts + context
    token_count = low_second.shape[0]
    chips = lax.axis_size("shard") // 2
    same_core = 2 * jnp.arange(chips, dtype=jnp.int32) + (shard & 1)
    picks = []
    for turn in range(2):
        ids = jnp.take(all_ids, same_core * contexts + (context ^ turn), axis=0)
        far_ids = jnp.take(all_ids, (same_core ^ 1) * contexts + (context ^ turn), axis=0)
        picks.append(
            (
                slot_picks(ids, expert, capacity),
                slot_picks(ids, other_expert, capacity),
                slot_picks(far_ids, expert, capacity),
            )
        )

    def arrive(turn, rows):
        probs = softmax_rows(plain(rows, router))
        mine = jnp.arange(probs.shape[1], dtype=jnp.int32)[None, :] == expert
        return jnp.sum(jnp.where(mine, probs, 0.0), axis=1, keepdims=True)

    def leave(turn, produced, cot_rows, gate):
        cot_wide = cot_rows.astype(WIDE)
        produced_wide = produced.astype(WIDE)
        slot_grad = jnp.sum(produced_wide * cot_wide, axis=1)
        all_picks = jnp.concatenate([picks[turn][0], picks[turn][2]], axis=0).astype(WIDE)
        gate_grad = jnp.sum(all_picks * slot_grad.reshape(2 * chips, capacity)[:, :, None], axis=1)
        return (gate_grad, (gate * cot_wide).astype(LOW), (gate * produced_wide).astype(LOW))

    up_weight = whole_weight(w_up)
    near_chunk, across, w_down, cot_near, cotangent = sync(
        gather_chips(low_second), swap(low_second, "context"), w_down, cot_near, cotangent
    )
    cot_across = swap(cotangent, "context")
    near_rows = pick_rows(*picks[0][:2], near_chunk)
    down_weight = whole_weight(w_down)
    weights = (gate_weight, up_weight, down_weight)
    near_kept = expert_hidden(near_rows, weights)
    near_hidden, far_chunk, cot_across = sync(near_kept[2], gather_chips(across), cot_across)
    near_kept = near_kept[:2] + (near_hidden,)
    cot_far = gather_chips(cot_across)
    far_rows = pick_rows(*picks[1][:2], far_chunk)
    far_rows, down_weight = sync(far_rows, down_weight)
    weights = (gate_weight, up_weight, down_weight)
    far_kept = expert_hidden(far_rows, weights)
    near_cot, far_cot = pick_rows(*picks[0][:2], cot_near), pick_rows(*picks[1][:2], cot_far)
    gate = arrive(0, near_rows)
    produced = expert_produce(near_hidden, weights)
    near_gate_grad, near_grad_rows, weighted = leave(0, produced, near_cot, gate)
    mixture_parts = chip_parts(weighted, *picks[0][:2])
    gate = arrive(1, far_rows)
    produced = expert_produce(far_kept[2], weights)
    far_gate_grad, far_grad_rows, far_weighted = leave(1, produced, far_cot, gate)
    rest_parts = chip_parts(far_weighted, *picks[1][:2])
    lines = jnp.stack([near_gate_grad, far_gate_grad], axis=1)
    lines = jnp.where(context == 0, lines, lines[:, ::-1])
    mine, far = lines[:chips], lines[chips:]
    low_core = (shard & 1) == 0
    lines = jnp.stack([jnp.where(low_core, mine, far), jnp.where(low_core, far, mine)], axis=1)
    lines = lines.reshape(-1, token_count)
    by_expert = lax.all_to_all(lines, ("shard", "context"), split_axis=0, concat_axis=0, tiled=True)

    def both(near, far):
        return jnp.concatenate([near, far], axis=0)

    far_route, far_gate_act, far_up_act = expert_backward(far_grad_rows, far_kept, weights)
    far_route, near_grad_rows, far_grad_rows = sync(far_route, near_grad_rows, far_grad_rows)
    down_pair = (both(near_grad_rows, far_grad_rows), both(near_kept[2], far_kept[2]))
    down_total = weight_total(*down_pair)
    far_parts = chip_parts(far_route.astype(LOW), *picks[1][:2])
    near_grad_rows, far_parts, by_expert, down_total = sync(
        near_grad_rows, far_parts, by_expert, down_total
    )
    down_grad = owned_grad(down_total)
    near_route, near_gate_act, near_up_act = expert_backward(near_grad_rows, near_kept, weights)
    near_route = near_route.astype(LOW)
    near_half = near_route.shape[0] // 2
    near_swapped = hop(near_route[near_half:], 1)
    near_route, near_gate_act = sync(near_route, near_gate_act)
    all_rows = both(near_rows, far_rows)
    near_swapped, far_grad, near_up_act, gate_total = sync(
        near_swapped,
        sum_chips(far_parts).astype(LOW),
        near_up_act,
        weight_total(all_rows, both(near_gate_act, far_gate_act)),
    )
    gate_grad = owned_grad(gate_total)
    near_parts = combine(near_route[:near_half], near_swapped, *picks[0][:2])
    far_arrived = swap(far_grad, "context")
    far_arrived, mixture_parts, rest_parts = sync(far_arrived, mixture_parts, rest_parts)
    grad, mixture_parts, rest_parts, down_grad, far_up_act = sync(
        sum_chips(near_parts) + far_arrived.astype(WIDE),
        mixture_parts,
        rest_parts,
        down_grad,
        far_up_act,
    )
    up_pair = (all_rows, both(near_up_act, far_up_act))
    later = (mixture_parts, rest_parts, gate_grad, down_grad, up_pair)
    return (grad, by_expert.T, later)


def move_slots(buffer):
    return lax.all_to_all(buffer, ("shard", "context"), split_axis=0, concat_axis=0, tiled=True)


def experts_by_slots(low_second, cotangent, expert_ids, router_probs, weights, capacity):
    row_count, model_width = low_second.shape
    expert_count = router_probs.shape[1]
    top_count = expert_ids.shape[1]
    choose = expert_ids[:, :, None] == jnp.arange(expert_count, dtype=jnp.int32)[None, None, :]
    gate_probs = jnp.sum(jnp.where(choose, router_probs[:, None, :], 0.0), axis=2)
    route_total = row_count * top_count
    flat_ids = expert_ids.reshape(-1)
    onehot = (flat_ids[:, None] == jnp.arange(expert_count, dtype=jnp.int32)[None, :]).astype(
        jnp.int32
    )
    before = jnp.cumsum(onehot, axis=0) - onehot
    route_slot = flat_ids * capacity + jnp.sum(before * onehot, axis=1)
    route_of_slot = (
        jnp.full((expert_count * capacity,), route_total, jnp.int32)
        .at[route_slot]
        .set(jnp.arange(route_total, dtype=jnp.int32))
    )
    filled = route_of_slot < route_total
    route_clipped = jnp.minimum(route_of_slot, route_total - 1)
    token_of_slot = route_clipped // top_count
    slot_shape = (expert_count, capacity, model_width)
    flat_shape = (expert_count * capacity, model_width)
    sending = jnp.where(filled[:, None], low_second[token_of_slot], jnp.zeros((), LOW))
    rows = move_slots(sending.reshape(slot_shape)).reshape(flat_shape)
    produced, kept = expert_forward(rows, weights)
    returned = move_slots(produced.reshape(slot_shape)).reshape(flat_shape)
    chosen = returned[route_slot].reshape(row_count, top_count, model_width).astype(WIDE)
    mixture = jnp.sum(gate_probs[:, :, None] * chosen, axis=1)
    grad_top = cotangent.astype(WIDE)
    grad_gates = jnp.sum(chosen * grad_top[:, None, :], axis=2)
    slot_gate = jnp.where(filled, gate_probs.reshape(-1)[route_clipped], 0.0)
    sending_grad = (slot_gate[:, None] * grad_top[token_of_slot]).astype(LOW)
    grad_rows = move_slots(sending_grad.reshape(slot_shape)).reshape(flat_shape)
    grad_route, grad_gate_act, grad_up_act = expert_backward(grad_rows, kept, weights)
    returned_grad = move_slots(grad_route.astype(LOW).reshape(slot_shape)).reshape(flat_shape)
    grad = jnp.sum(
        returned_grad[route_slot].reshape(row_count, top_count, model_width).astype(WIDE), axis=1
    )
    by_expert = jnp.sum(jnp.where(choose, grad_gates[:, :, None], 0.0), axis=1)
    pairs = [(rows, grad_gate_act), (rows, grad_up_act), (grad_rows, kept[2])]
    grads = tuple(owned_grad(weight_total(*pair)) for pair in pairs)
    return (grad, by_expert, mixture, grads)


def local(
    hidden_in,
    cotangent,
    w_query,
    w_key,
    w_value,
    w_out,
    w_router,
    norm_first,
    norm_second,
    query_gain,
    key_gain,
    w_gate,
    w_up,
    w_down,
    expert_ids,
):
    group_index = lax.axis_index(("context", "tensor"))
    row_count, model_width = hidden_in.shape
    column_span = w_query.shape[1]
    expert_count = w_router.shape[1]
    top_count = expert_ids.shape[1]
    capacity = max(2, row_count * top_count * 5 // (4 * expert_count))
    by_blocks = 2 * capacity >= row_count
    device_count = model_width // norm_first.shape[0]

    router_rows = w_router.shape[0]
    small = gather_small(
        jnp.concatenate(
            [
                w_router.reshape(-1),
                norm_first,
                norm_second,
                query_gain,
                key_gain,
                expert_ids.T.reshape(-1).astype(LOW),
            ],
            axis=0,
        )
    )
    hidden_blocks = gather_group(hidden_in)
    hidden_blocks[3], gate_early = sync(hidden_blocks[3], w_gate[0])
    gate_weight = whole_weight(gate_early)
    packed = lax.all_gather(
        jnp.concatenate([w_query, w_key, w_value, w_out], axis=1), "shard", axis=0, tiled=True
    )
    router_size = router_rows * expert_count
    router_full = small[:, :router_size].reshape(model_width, expert_count)
    gains = [
        small[:, router_size + i * router_rows : router_size + (i + 1) * router_rows]
        .reshape(model_width)
        .astype(WIDE)
        for i in range(4)
    ]
    gain_first, gain_second, gain_query, gain_key = gains
    if by_blocks:
        tensors = lax.axis_size("tensor")
        all_ids = small[:, router_size + 4 * router_rows :].astype(jnp.int32)
        all_ids = all_ids.reshape(-1, tensors, top_count, row_count)
        all_ids = lax.dynamic_index_in_dim(all_ids, lax.axis_index("tensor"), 1, False)

    qkv_cols = packed[:, : 3 * column_span]
    out_cols = packed[:, 3 * column_span :]
    inputs = hidden_in.astype(WIDE)
    factor_first = rms_scale(inputs, gain_first)[1]
    low_blocks, pre_blocks = [], []
    for block in hidden_blocks:
        low_block = rms_scale(block.astype(WIDE), gain_first)[0].astype(LOW)
        low_blocks.append(low_block)
        pre_blocks.append(plain(low_block, qkv_cols))
    low_group = jnp.concatenate(low_blocks, axis=0)
    pre = jnp.concatenate(pre_blocks, axis=0)
    group_rows = low_group.shape[0]
    line = jnp.arange(group_rows, dtype=jnp.int32)
    place = ((line // row_count) ^ group_index) * row_count + line % row_count
    cosine, sine = rope_tables(place)
    gain_cols = jnp.stack(
        [
            lax.dynamic_slice_in_dim(gain, group_index * column_span, column_span, 0)
            for gain in (gain_query, gain_key)
        ]
    )

    def over_group(stacked):
        stacked = stacked.reshape(2, 4, -1)
        stacked = stacked + swap(stacked, "tensor")[:, jnp.array([1, 0, 3, 2])]
        stacked = stacked + swap(stacked, "context")[:, jnp.array([2, 3, 0, 1])]
        return stacked.reshape(2, -1)

    own_squares, early_cot = sync(
        jnp.stack(
            [
                jnp.sum(jnp.square(pre[:, i * column_span : (i + 1) * column_span]), axis=1)
                for i in range(2)
            ]
        ),
        cotangent,
    )
    if by_blocks:
        cot_near = gather_chips(early_cot)
    squares = over_group(own_squares)
    query_heads, key_heads, value_heads = prepare(
        pre, squares, gain_cols, cosine, sine, model_width, row_count
    )
    group = group_index[None].astype(jnp.int32)
    blocks, logs = [None] * 4, [None] * 4
    for k in (3, 2, 1, 0):
        blocks[k], logs[k] = attend_block(
            k, group, query_heads, key_heads, value_heads, row_count
        )
    parts = [contract_last(block, out_cols) for block in blocks]
    far_part, gate_weight = sync(parts[3].astype(LOW), gate_weight)
    far = swap(far_part, "tensor")
    far, near_part, part = sync(far, parts[1].astype(LOW), parts[2])
    across = swap((part + far.astype(WIDE)).astype(LOW), "context")
    near = swap(near_part, "tensor")
    if by_blocks:
        across, cot_near = sync(across, cot_near)
    middle = inputs + parts[0] + near.astype(WIDE) + across.astype(WIDE)
    normed_second, factor_second = rms_scale(middle, gain_second)
    low_second = normed_second.astype(LOW)
    router_probs = softmax_rows(plain(low_second, router_full))
    low_second, late_up, late_down = sync(low_second, w_up[0], w_down[0])
    if by_blocks:
        grad_from_experts, grad_router_probs, later = experts_by_blocks(
            low_second,
            cot_near,
            cotangent,
            all_ids,
            router_full,
            gate_weight,
            late_up,
            late_down,
            capacity,
        )
        mixture_parts, rest_parts, gate_grad, down_grad, up_pair = later
    else:
        weights = (gate_weight, whole_weight(late_up), whole_weight(late_down))
        grad_from_experts, grad_router_probs, mixture, expert_grads = experts_by_slots(
            low_second, cotangent, expert_ids, router_probs, weights, capacity
        )
    grad_logits = (
        router_probs
        * (grad_router_probs - jnp.sum(router_probs * grad_router_probs, axis=1, keepdims=True))
    ).astype(LOW)
    grad_router_weight = contract_first(low_second, grad_logits)
    grad_second = grad_from_experts + contract_last(grad_logits, router_full)
    grad_normed_second, grad_gain_second = rms_back(middle, factor_second, gain_second, grad_second)
    grad_middle = cotangent.astype(WIDE) + grad_normed_second
    grad_branch = grad_middle.astype(LOW)
    near_piece, across = swap(grad_branch, "tensor"), swap(grad_branch, "context")

    def piece_back(k, piece, sums):
        grad_queries, *sums = attend_block_back(
            k,
            group,
            query_heads,
            key_heads,
            value_heads,
            plain(piece, out_cols).astype(LOW),
            logs[k],
            sums,
            row_count,
        )
        return (grad_queries, tuple(sums))

    own_query, own_sums = piece_back(0, grad_branch, None)
    if by_blocks:
        rest = sum_chips(rest_parts).astype(LOW)
    if by_blocks:
        across, own_sums, rest, gate_grad, up_mine, up_theirs = sync(
            across, tuple(own_sums), rest, gate_grad, my_grad(*up_pair), their_grad(*up_pair)
        )
        up_halves = halves(up_theirs)
        others = lax.all_gather(rest, "context", axis=0, tiled=False)
    last = swap(across, "tensor")
    near_query, near_sums = piece_back(1, near_piece, own_sums)
    across_query, across_sums = piece_back(2, across, near_sums)
    last, across_sums = sync(last, across_sums)
    if by_blocks:
        last, up_early, mixture_parts = sync(last, up_halves[0], mixture_parts)
        mixture = sum_chips(mixture_parts)
    pieces = [grad_branch, near_piece, across, last]
    last_query, sums = piece_back(3, last, across_sums)
    grad_queries = [own_query, near_query, across_query, last_query]
    grad_query_heads = jnp.concatenate(grad_queries, axis=0)
    out_total = contract_first(pieces[0], blocks[0])
    for k in range(1, 4):
        out_total = out_total + contract_first(pieces[k], blocks[k])
    out_total = out_total.astype(LOW)
    totals, gain_grads = norm_call(
        norm_sums_kernel,
        (grad_query_heads, sums[0], pre, squares, gain_cols, cosine, sine),
        ("rows", "rows", "rows", "line", "whole", "rows", "rows"),
        (((2, group_rows), WIDE, "line"), ((2, column_span), WIDE, "whole")),
        model_width,
        row_count,
    )
    if by_blocks:
        totals, up_first = sync(totals, swap(up_early, "tensor"))
    totals = over_group(totals)
    if by_blocks:
        totals, up_late = sync(totals, up_halves[1])
    (grad_pre,) = norm_call(
        norm_grads_kernel,
        (grad_query_heads, *sums, pre, squares, totals, gain_cols, cosine, sine),
        ("rows", "rows", "rows", "rows", "line", "line", "whole", "rows", "rows"),
        (((group_rows, 3 * column_span), LOW, "rows"),),
        model_width,
        row_count,
    )

    def block_of(values, k):
        return values[k * row_count : (k + 1) * row_count]

    far_part = contract_last(block_of(grad_pre, 3), qkv_cols).astype(LOW)
    if by_blocks:
        far_part, grad_pre, out_total, mixture = sync(far_part, grad_pre, out_total, mixture)
    out_dealt = lax.all_to_all(out_total, "shard", split_axis=0, concat_axis=0, tiled=True)
    far = swap(far_part, "tensor")
    head_total = contract_first(low_group, grad_pre).astype(LOW)
    parts = [contract_last(block_of(grad_pre, k), qkv_cols) for k in range(3)]
    far, head_total, near_part, out_dealt, *parts = sync(
        far, head_total, parts[1].astype(LOW), out_dealt, parts[0], parts[2]
    )
    if by_blocks:
        other = lax.dynamic_index_in_dim(others, lax.axis_index("context") ^ 1, 0, False)
        mixture = mixture + other.astype(WIDE)
    block_output = (middle + mixture).astype(LOW)
    across = swap((parts[1] + far.astype(WIDE)).astype(LOW), "context")
    near = swap(near_part, "tensor")
    head_grads = lax.psum_scatter(head_total, "shard", scatter_dimension=0, tiled=True).astype(WIDE)
    if by_blocks:
        near, across, gate_grad, down_grad, up_late = sync(
            near, across, gate_grad, down_grad, up_late
        )
        up_arrived = jnp.concatenate([up_first, swap(up_late, "tensor")], axis=0)
        expert_grads = (gate_grad, up_mine + up_arrived.astype(WIDE), down_grad)
    out_grad = jnp.sum(
        out_dealt.reshape((lax.axis_size("shard"),) + w_out.shape).astype(WIDE), axis=0
    )
    grad_first = parts[0] + near.astype(WIDE) + across.astype(WIDE)
    grad_normed_first, grad_gain_first = rms_back(inputs, factor_first, gain_first, grad_first)
    grad_input = grad_middle + grad_normed_first
    zero_gain = jnp.zeros((2, model_width), WIDE)
    grad_gains = lax.dynamic_update_slice(zero_gain, gain_grads, (0, group_index * column_span))
    by_device = [
        one.reshape(device_count, -1)
        for one in (grad_router_weight, grad_gain_first, grad_gain_second, grad_gains[0], grad_gains[1])
    ]
    small_grads = scatter_small(jnp.concatenate(by_device, axis=1))
    router_grad = small_grads[:router_size].reshape(router_rows, expert_count)
    gain_totals = small_grads[router_size:].reshape(4, router_rows)
    return (
        block_output,
        grad_input,
        head_grads[:, :column_span],
        head_grads[:, column_span : 2 * column_span],
        head_grads[:, 2 * column_span : 3 * column_span],
        out_grad,
        router_grad,
        *(gain_totals[i] for i in range(4)),
        *(grad.astype(WIDE)[None] for grad in expert_grads),
    )


def solution(mesh):
    rows = P(("shard", "context", "tensor"), None)
    columns = P("shard", ("context", "tensor"))
    vector = P(("shard", "context", "tensor"))
    expert = P(("shard", "context"), None, "tensor")
    return jax.shard_map(
        local,
        mesh=mesh,
        in_specs=(
            (rows, rows)
            + (columns,) * 4
            + (rows,)
            + (vector,) * 4
            + (expert,) * 3
            + (rows,)
        ),
        out_specs=((rows, rows) + (columns,) * 4 + (rows,) + (vector,) * 4 + (expert,) * 3),
        check_vma=False,
    )
```

```python
import jax
import jax.numpy as jnp
from jax import lax
from jax.experimental import pallas as pl
from jax.experimental.pallas import tpu as pltpu
from jax.sharding import PartitionSpec as P

HDIM = 128


EPSILON = 1e-05
MASKED = -1e30
LOW = jnp.bfloat16
WIDE = jnp.float32
SWAP = ((0, 1), (1, 0))


def sync(*values):
    return lax.optimization_barrier(values)


def rms_scale(values, gain):
    factor = lax.rsqrt(jnp.mean(values * values, axis=-1, keepdims=True) + EPSILON)
    return (values * factor * gain, factor)


def rms_back(values, factor, gain, grad_out):
    scaled = grad_out * gain
    mean_term = jnp.mean(scaled * values, axis=-1, keepdims=True)
    grad_values = factor * scaled - values * (factor * factor * factor) * mean_term
    return (grad_values, jnp.sum(grad_out * values * factor, axis=0))


def rope_tables(positions):
    half_size = HDIM // 2
    frequency = 10000.0 ** (-2.0 * jnp.arange(half_size, dtype=WIDE) / HDIM)
    angles = positions.astype(WIDE)[:, None] * frequency[None, :]
    cosine, sine = jnp.cos(angles), jnp.sin(angles)
    return (
        jnp.concatenate([cosine, cosine], axis=1),
        jnp.concatenate([-sine, sine], axis=1),
    )


def contract_last(left, right):
    return lax.dot_general(
        left, right, (((1,), (1,)), ((), ())), preferred_element_type=jnp.float32
    )


def contract_first(left, right):
    return lax.dot_general(
        left, right, (((0,), (0,)), ((), ())), preferred_element_type=jnp.float32
    )


def plain(left, right):
    return jnp.dot(left, right, preferred_element_type=jnp.float32)


def swap(values, axis):
    return lax.ppermute(values, axis, SWAP)


def hop(values, distance):
    count = lax.axis_size("shard")
    return lax.ppermute(values, "shard", tuple((i, i ^ distance) for i in range(count)))


def gather_group(block):
    near = swap(block, "tensor")
    across = swap(block, "context")
    return [block, near, across, swap(across, "tensor")]


def scatter_group(parts):
    far, near = sync(swap(parts[3].astype(LOW), "tensor"), parts[1].astype(LOW))
    across = swap((parts[2] + far.astype(WIDE)).astype(LOW), "context")
    return parts[0] + swap(near, "tensor").astype(WIDE) + across.astype(WIDE)


def over_chips(blocks):
    count = lax.axis_size("shard")
    groups = [list(range(core, count, 2)) for core in range(2)]
    return lax.all_to_all(
        blocks, "shard", split_axis=0, concat_axis=0, axis_index_groups=groups, tiled=True
    )


def gather_chips(block):
    chips = lax.axis_size("shard") // 2
    return over_chips(jnp.broadcast_to(block[None], (chips,) + block.shape))


DEVICES = ("shard", "context", "tensor")


def deal(rows):
    return lax.all_to_all(rows, DEVICES, split_axis=0, concat_axis=0, tiled=True)


def device_total():
    return lax.axis_size("shard") * lax.axis_size("context") * lax.axis_size("tensor")


def gather_small(row):
    return deal(jnp.broadcast_to(row[None], (device_total(), row.shape[0])))


def scatter_small(rows):
    return jnp.sum(deal(rows), axis=0)


def params():
    return pltpu.CompilerParams(vmem_limit_bytes=48 * 1024 * 1024)


def as_column(row, width):
    return jnp.broadcast_to(row, (width, row.shape[1])).T


def turn(values, cosine, sine):
    return values * cosine + pltpu.roll(values, HDIM // 2, 1) * sine


def norm_factors(squares_ref, width):
    factors = lax.rsqrt(squares_ref[...] / width + EPSILON)
    return as_column(factors[0:1], HDIM), as_column(factors[1:2], HDIM)


def prepare_kernel(width, pre_ref, squares_ref, gain_ref, cos_ref, sin_ref, q_ref, k_ref, v_ref):
    span = q_ref.shape[1]
    cosine, sine = cos_ref[...], sin_ref[...]
    factors = norm_factors(squares_ref, width)
    for which, out_ref in ((0, q_ref), (1, k_ref)):
        for first in range(0, span, HDIM):
            cols = slice(which * span + first, which * span + first + HDIM)
            gain = gain_ref[which : which + 1, first : first + HDIM]
            normed = pre_ref[:, cols] * factors[which] * gain
            out_ref[:, first : first + HDIM] = turn(normed, cosine, sine).astype(LOW)
    v_ref[...] = pre_ref[:, 2 * span :].astype(LOW)


def prepare(pre, squares, gain_cols, cosine, sine, width, block):
    rows, total = pre.shape
    span = total // 3
    row_block = lambda cols: pl.BlockSpec((block, cols), lambda i: (i, 0))
    return pl.pallas_call(
        lambda *refs: prepare_kernel(width, *refs),
        grid=(rows // block,),
        in_specs=[
            row_block(total),
            pl.BlockSpec((2, block), lambda i: (0, i)),
            pl.BlockSpec((2, span), lambda i: (0, 0)),
            row_block(HDIM),
            row_block(HDIM),
        ],
        out_specs=[row_block(span)] * 3,
        out_shape=[jax.ShapeDtypeStruct((rows, span), LOW)] * 3,
        compiler_params=params(),
        cost_estimate=pl.CostEstimate(
            flops=10 * rows * total, bytes_accessed=6 * rows * total, transcendentals=0
        ),
    )(pre, squares, gain_cols, cosine, sine)


def visible(group, which, keys, queries):
    line = lax.broadcasted_iota(jnp.int32, (keys, queries), 0)
    key_place = ((line // queries) ^ group) * queries + line % queries
    query_place = (which ^ group) * queries + lax.broadcasted_iota(
        jnp.int32, (keys, queries), 1
    )
    return query_place >= key_place


def dot_last(left, right):
    return lax.dot_general(left, right, (((1,), (1,)), ((), ())), preferred_element_type=WIDE)


def dot_first(left, right):
    return lax.dot_general(left, right, (((0,), (0,)), ((), ())), preferred_element_type=WIDE)


def attend_kernel(which, group_ref, q_ref, k_ref, v_ref, out_ref, log_ref):
    keys, queries = k_ref.shape[0], q_ref.shape[0]
    scores = dot_last(k_ref[...], q_ref[...]) * HDIM ** (-0.5)
    scores = jnp.where(visible(group_ref[0], which, keys, queries), scores, MASKED)
    maximum = jnp.max(scores, axis=0, keepdims=True)
    weights = jnp.exp(scores - maximum)
    total = jnp.sum(weights, axis=0, keepdims=True)
    attn_low = (weights * (1.0 / total)).astype(LOW)
    out_ref[...] = dot_first(v_ref[...], attn_low).T.astype(LOW)
    log_ref[...] = (maximum + jnp.log(total))[None]


def attend_block(which, group, queries, keys, values, block):
    rows, span = queries.shape
    heads = span // HDIM
    whole = pl.BlockSpec((rows, HDIM), lambda h, g: (0, h))
    return pl.pallas_call(
        lambda *refs: attend_kernel(which, *refs),
        grid_spec=pltpu.PrefetchScalarGridSpec(
            num_scalar_prefetch=1,
            grid=(heads,),
            in_specs=[pl.BlockSpec((block, HDIM), lambda h, g: (which, h)), whole, whole],
            out_specs=[
                pl.BlockSpec((block, HDIM), lambda h, g: (0, h)),
                pl.BlockSpec((1, 1, block), lambda h, g: (h, 0, 0)),
            ],
        ),
        out_shape=[
            jax.ShapeDtypeStruct((block, span), LOW),
            jax.ShapeDtypeStruct((heads, 1, block), WIDE),
        ],
        compiler_params=params(),
        cost_estimate=pl.CostEstimate(
            flops=4 * block * rows * span,
            bytes_accessed=4 * rows * span,
            transcendentals=block * rows * heads,
        ),
    )(group, queries, keys, values)


def attend_back_kernel(which, first, group_ref, q_ref, k_ref, v_ref, grad_ref, log_ref, *refs):
    keys, queries = k_ref.shape[0], q_ref.shape[0]
    grad_q_ref, grad_k_ref, grad_v_ref = refs[-3:]
    scores = dot_last(k_ref[...], q_ref[...]) * HDIM ** (-0.5)
    probs = jnp.exp(scores - log_ref[0])
    probs = jnp.where(visible(group_ref[0], which, keys, queries), probs, 0.0)
    grad_probs = dot_last(v_ref[...], grad_ref[...])
    delta = jnp.sum(probs * grad_probs, axis=0, keepdims=True)
    grad_scores = (probs * (grad_probs - delta)).astype(LOW)
    grad_q_ref[...] = (dot_first(k_ref[...], grad_scores).T * HDIM ** (-0.5)).astype(LOW)
    key_part = plain(grad_scores, q_ref[...]) * HDIM ** (-0.5)
    value_part = plain(probs.astype(LOW), grad_ref[...])
    grad_k_ref[...] = key_part if first else refs[0][...] + key_part
    grad_v_ref[...] = value_part if first else refs[1][...] + value_part


def attend_block_back(which, group, queries, keys, values, grad, logs, sums, block):
    rows, span = queries.shape
    heads = span // HDIM
    whole = pl.BlockSpec((rows, HDIM), lambda h, g: (0, h))
    own = pl.BlockSpec((block, HDIM), lambda h, g: (0, h))
    carried = [] if sums is None else list(sums)
    return pl.pallas_call(
        lambda *refs: attend_back_kernel(which, sums is None, *refs),
        grid_spec=pltpu.PrefetchScalarGridSpec(
            num_scalar_prefetch=1,
            grid=(heads,),
            in_specs=[
                pl.BlockSpec((block, HDIM), lambda h, g: (which, h)),
                whole,
                whole,
                own,
                pl.BlockSpec((1, 1, block), lambda h, g: (h, 0, 0)),
            ]
            + [whole] * len(carried),
            out_specs=[own, whole, whole],
        ),
        out_shape=[
            jax.ShapeDtypeStruct((block, span), LOW),
            jax.ShapeDtypeStruct((rows, span), WIDE),
            jax.ShapeDtypeStruct((rows, span), WIDE),
        ],
        compiler_params=params(),
        cost_estimate=pl.CostEstimate(
            flops=10 * block * rows * span,
            bytes_accessed=20 * rows * span,
            transcendentals=block * rows * heads,
        ),
    )(group, queries, keys, values, grad, logs, *carried)


def turned_back(which, first, grads, cosine, sine):
    values = grads[which][:, first : first + HDIM].astype(WIDE)
    return turn(values, cosine, -sine)


def norm_sums_kernel(
    width, gq_ref, gk_ref, pre_ref, squares_ref, gain_ref, cos_ref, sin_ref, total_ref, col_ref
):
    span = gq_ref.shape[1]
    cosine, sine = cos_ref[...], sin_ref[...]
    factors = norm_factors(squares_ref, width)

    @pl.when(pl.program_id(0) == 0)
    def _():
        col_ref[...] = jnp.zeros_like(col_ref)

    for which in range(2):
        total = jnp.zeros(cosine.shape, WIDE)
        for first in range(0, span, HDIM):
            grad = turned_back(which, first, (gq_ref, gk_ref), cosine, sine)
            cols = slice(which * span + first, which * span + first + HDIM)
            product = grad * pre_ref[:, cols]
            total = total + product * gain_ref[which : which + 1, first : first + HDIM]
            col_ref[which : which + 1, first : first + HDIM] += jnp.sum(
                product * factors[which], axis=0, keepdims=True
            )
        total_ref[which : which + 1, :] = jnp.sum(total.T, axis=0, keepdims=True)


def norm_grads_kernel(
    width,
    gq_ref,
    gk_ref,
    gv_ref,
    pre_ref,
    squares_ref,
    total_ref,
    gain_ref,
    cos_ref,
    sin_ref,
    out_ref,
):
    span = gq_ref.shape[1]
    cosine, sine = cos_ref[...], sin_ref[...]
    factors = norm_factors(squares_ref, width)
    for which in range(2):
        factor = factors[which]
        mean = as_column(total_ref[which : which + 1] / width, HDIM)
        pull = factor * factor * factor * mean
        for first in range(0, span, HDIM):
            grad = turned_back(which, first, (gq_ref, gk_ref), cosine, sine)
            cols = slice(which * span + first, which * span + first + HDIM)
            scaled = grad * gain_ref[which : which + 1, first : first + HDIM]
            out_ref[:, cols] = (factor * scaled - pre_ref[:, cols] * pull).astype(LOW)
    out_ref[:, 2 * span :] = gv_ref[...].astype(LOW)


def norm_call(body, operands, kinds, outs, width, block):
    def spec(shape, kind):
        if kind == "rows":
            return pl.BlockSpec((block, shape[1]), lambda i: (i, 0))
        if kind == "line":
            return pl.BlockSpec((shape[0], block), lambda i: (0, i))
        return pl.BlockSpec(shape, lambda i: (0, 0))

    size = sum(o.size * o.dtype.itemsize for o in operands)
    return pl.pallas_call(
        lambda *refs: body(width, *refs),
        grid=(operands[0].shape[0] // block,),
        in_specs=[spec(o.shape, kind) for o, kind in zip(operands, kinds)],
        out_specs=[spec(shape, kind) for shape, _, kind in outs],
        out_shape=[jax.ShapeDtypeStruct(shape, dtype) for shape, dtype, _ in outs],
        compiler_params=params(),
        cost_estimate=pl.CostEstimate(flops=4 * size, bytes_accessed=size, transcendentals=0),
    )(*operands)


def silu_parts(gate_act):
    sigmoid_value = jax.nn.sigmoid(gate_act)
    return (gate_act * sigmoid_value, sigmoid_value)


def expert_hidden(rows, weights):
    gate_act = plain(rows, weights[0])
    up_act = plain(rows, weights[1])
    return (gate_act, up_act, (silu_parts(gate_act)[0] * up_act).astype(LOW))


def expert_produce(hidden_act, weights):
    return contract_last(hidden_act, weights[2]).astype(LOW)


def expert_forward(rows, weights):
    kept = expert_hidden(rows, weights)
    return (expert_produce(kept[2], weights), kept)


def expert_backward(grad_rows, kept, weights):
    gate_weight, up_weight, down_weight = weights
    gate_act, up_act, hidden_act = kept
    grad_hidden = plain(grad_rows, down_weight)
    activated, sigmoid_value = silu_parts(gate_act)
    grad_gate_act = (
        grad_hidden * up_act * sigmoid_value * (1.0 + gate_act * (1.0 - sigmoid_value))
    ).astype(LOW)
    grad_up_act = (grad_hidden * activated).astype(LOW)
    grad_route = contract_last(grad_gate_act, gate_weight) + contract_last(grad_up_act, up_weight)
    return (grad_route, grad_gate_act, grad_up_act)


def weight_total(left, right):
    return contract_first(left, right).astype(LOW)


def columns_of(values, tensor):
    half = values.shape[1] // 2
    return lax.dynamic_slice_in_dim(values, tensor * half, half, 1)


def their_grad(left, right):
    return contract_first(left, columns_of(right, 1 - lax.axis_index("tensor"))).astype(LOW)


def my_grad(left, right):
    return contract_first(left, columns_of(right, lax.axis_index("tensor")))


def owned_grad(total):
    return lax.psum_scatter(total, "tensor", scatter_dimension=1, tiled=True)


def halves(values):
    half = values.shape[0] // 2
    return (values[:half], values[half:])


def whole_weight(held):
    return lax.all_gather(held, "tensor", axis=1, tiled=True)


def softmax_rows(logits):
    weights = jnp.exp(logits - jnp.max(logits, axis=-1, keepdims=True))
    return weights / jnp.sum(weights, axis=-1, keepdims=True)


def pick_rows(picks, other_picks, blocks):
    pick = jnp.concatenate([picks, other_picks], axis=1)
    chosen = jnp.einsum("bst,btd->bsd", pick, blocks, preferred_element_type=jnp.float32)
    chosen = chosen.astype(LOW)
    capacity, width = picks.shape[1], blocks.shape[2]
    kept = chosen[:, :capacity].reshape(-1, width)
    arrived = hop(chosen[:, capacity:].reshape(-1, width), 1)
    return jnp.concatenate([kept, arrived], axis=0)


def slot_picks(ids, expert, capacity):
    routed = jnp.any(ids == expert, axis=1)
    tokens = ids.shape[2]
    line = jnp.arange(tokens, dtype=jnp.int32)
    earlier = (line[:, None] < line[None, :]).astype(LOW)
    position = plain(routed.astype(LOW), earlier).astype(jnp.int32)
    position = jnp.where(routed, position, -1)
    slots = jnp.arange(capacity, dtype=jnp.int32)
    return (position[:, None, :] == slots[None, :, None]).astype(LOW)


def chip_parts(rows, picks, other_picks):
    half = rows.shape[0] // 2
    return combine(rows[:half], hop(rows[half:], 1), picks, other_picks)


def combine(kept, arrived, picks, other_picks):
    shape = picks.shape[:2] + kept.shape[1:]
    both = jnp.concatenate([kept.reshape(shape), arrived.reshape(shape)], axis=1)
    pick = jnp.concatenate([picks, other_picks], axis=1)
    parts = jnp.einsum("bst,bsd->btd", pick, both, preferred_element_type=jnp.float32)
    return parts.astype(LOW)


def sum_chips(parts):
    return jnp.sum(over_chips(parts).astype(WIDE), axis=0)


def experts_by_blocks(
    low_second, cot_near, cotangent, all_ids, router, gate_weight, w_up, w_down, capacity
):
    shard, context = lax.axis_index("shard"), lax.axis_index("context")
    contexts = lax.axis_size("context")
    expert = shard * contexts + context
    other_expert = (shard ^ 1) * contexts + context
    token_count = low_second.shape[0]
    chips = lax.axis_size("shard") // 2
    same_core = 2 * jnp.arange(chips, dtype=jnp.int32) + (shard & 1)
    picks = []
    for turn in range(2):
        ids = jnp.take(all_ids, same_core * contexts + (context ^ turn), axis=0)
        far_ids = jnp.take(all_ids, (same_core ^ 1) * contexts + (context ^ turn), axis=0)
        picks.append(
            (
                slot_picks(ids, expert, capacity),
                slot_picks(ids, other_expert, capacity),
                slot_picks(far_ids, expert, capacity),
            )
        )

    def arrive(turn, rows):
        probs = softmax_rows(plain(rows, router))
        mine = jnp.arange(probs.shape[1], dtype=jnp.int32)[None, :] == expert
        return jnp.sum(jnp.where(mine, probs, 0.0), axis=1, keepdims=True)

    def leave(turn, produced, cot_rows, gate):
        cot_wide = cot_rows.astype(WIDE)
        produced_wide = produced.astype(WIDE)
        slot_grad = jnp.sum(produced_wide * cot_wide, axis=1)
        all_picks = jnp.concatenate([picks[turn][0], picks[turn][2]], axis=0).astype(WIDE)
        gate_grad = jnp.sum(all_picks * slot_grad.reshape(2 * chips, capacity)[:, :, None], axis=1)
        return (gate_grad, (gate * cot_wide).astype(LOW), (gate * produced_wide).astype(LOW))

    up_weight = whole_weight(w_up)
    near_chunk, across, w_down, cot_near, cotangent = sync(
        gather_chips(low_second), swap(low_second, "context"), w_down, cot_near, cotangent
    )
    cot_across = swap(cotangent, "context")
    near_rows = pick_rows(*picks[0][:2], near_chunk)
    down_weight = whole_weight(w_down)
    weights = (gate_weight, up_weight, down_weight)
    near_kept = expert_hidden(near_rows, weights)
    near_hidden, far_chunk = sync(near_kept[2], gather_chips(across))
    near_kept = near_kept[:2] + (near_hidden,)
    far_rows = pick_rows(*picks[1][:2], far_chunk)
    far_rows, cot_across = sync(far_rows, cot_across)
    far_kept = expert_hidden(far_rows, weights)
    far_hidden, cot_far, down_weight = sync(far_kept[2], gather_chips(cot_across), down_weight)
    far_kept = far_kept[:2] + (far_hidden,)
    weights = (gate_weight, up_weight, down_weight)
    near_cot, far_cot = pick_rows(*picks[0][:2], cot_near), pick_rows(*picks[1][:2], cot_far)
    gate = arrive(0, near_rows)
    produced = expert_produce(near_hidden, weights)
    near_gate_grad, near_grad_rows, weighted = leave(0, produced, near_cot, gate)
    mixture_parts = chip_parts(weighted, *picks[0][:2])
    gate = arrive(1, far_rows)
    produced = expert_produce(far_kept[2], weights)
    far_gate_grad, far_grad_rows, far_weighted = leave(1, produced, far_cot, gate)
    rest_parts = chip_parts(far_weighted, *picks[1][:2])
    lines = jnp.stack([near_gate_grad, far_gate_grad], axis=1)
    lines = jnp.where(context == 0, lines, lines[:, ::-1])
    mine, far = lines[:chips], lines[chips:]
    low_core = (shard & 1) == 0
    lines = jnp.stack([jnp.where(low_core, mine, far), jnp.where(low_core, far, mine)], axis=1)
    lines = lines.reshape(-1, token_count)
    by_expert = lax.all_to_all(lines, ("shard", "context"), split_axis=0, concat_axis=0, tiled=True)

    def both(near, far):
        return jnp.concatenate([near, far], axis=0)

    far_route, far_gate_act, far_up_act = expert_backward(far_grad_rows, far_kept, weights)
    far_route, near_grad_rows, far_grad_rows = sync(far_route, near_grad_rows, far_grad_rows)
    down_pair = (both(near_grad_rows, far_grad_rows), both(near_kept[2], far_kept[2]))
    down_total = weight_total(*down_pair)
    far_parts = chip_parts(far_route.astype(LOW), *picks[1][:2])
    near_grad_rows, far_parts, by_expert, down_total = sync(
        near_grad_rows, far_parts, by_expert, down_total
    )
    down_grad = owned_grad(down_total)
    near_route, near_gate_act, near_up_act = expert_backward(near_grad_rows, near_kept, weights)
    near_route = near_route.astype(LOW)
    near_half = near_route.shape[0] // 2
    near_swapped = hop(near_route[near_half:], 1)
    near_route, near_gate_act = sync(near_route, near_gate_act)
    all_rows = both(near_rows, far_rows)
    near_swapped, far_grad, near_up_act, gate_total = sync(
        near_swapped,
        sum_chips(far_parts).astype(LOW),
        near_up_act,
        weight_total(all_rows, both(near_gate_act, far_gate_act)),
    )
    gate_grad = owned_grad(gate_total)
    near_parts = combine(near_route[:near_half], near_swapped, *picks[0][:2])
    far_arrived = swap(far_grad, "context")
    far_arrived, mixture_parts, rest_parts = sync(far_arrived, mixture_parts, rest_parts)
    grad, mixture_parts, rest_parts, down_grad, far_up_act = sync(
        sum_chips(near_parts) + far_arrived.astype(WIDE),
        mixture_parts,
        rest_parts,
        down_grad,
        far_up_act,
    )
    up_pair = (all_rows, both(near_up_act, far_up_act))
    later = (mixture_parts, rest_parts, gate_grad, down_grad, up_pair)
    return (grad, by_expert.T, later)


def move_slots(buffer):
    return lax.all_to_all(buffer, ("shard", "context"), split_axis=0, concat_axis=0, tiled=True)


def experts_by_slots(low_second, cotangent, expert_ids, router_probs, weights, capacity):
    row_count, model_width = low_second.shape
    expert_count = router_probs.shape[1]
    top_count = expert_ids.shape[1]
    choose = expert_ids[:, :, None] == jnp.arange(expert_count, dtype=jnp.int32)[None, None, :]
    gate_probs = jnp.sum(jnp.where(choose, router_probs[:, None, :], 0.0), axis=2)
    route_total = row_count * top_count
    flat_ids = expert_ids.reshape(-1)
    onehot = (flat_ids[:, None] == jnp.arange(expert_count, dtype=jnp.int32)[None, :]).astype(
        jnp.int32
    )
    before = jnp.cumsum(onehot, axis=0) - onehot
    route_slot = flat_ids * capacity + jnp.sum(before * onehot, axis=1)
    route_of_slot = (
        jnp.full((expert_count * capacity,), route_total, jnp.int32)
        .at[route_slot]
        .set(jnp.arange(route_total, dtype=jnp.int32))
    )
    filled = route_of_slot < route_total
    route_clipped = jnp.minimum(route_of_slot, route_total - 1)
    token_of_slot = route_clipped // top_count
    slot_shape = (expert_count, capacity, model_width)
    flat_shape = (expert_count * capacity, model_width)
    sending = jnp.where(filled[:, None], low_second[token_of_slot], jnp.zeros((), LOW))
    rows = move_slots(sending.reshape(slot_shape)).reshape(flat_shape)
    produced, kept = expert_forward(rows, weights)
    returned = move_slots(produced.reshape(slot_shape)).reshape(flat_shape)
    chosen = returned[route_slot].reshape(row_count, top_count, model_width).astype(WIDE)
    mixture = jnp.sum(gate_probs[:, :, None] * chosen, axis=1)
    grad_top = cotangent.astype(WIDE)
    grad_gates = jnp.sum(chosen * grad_top[:, None, :], axis=2)
    slot_gate = jnp.where(filled, gate_probs.reshape(-1)[route_clipped], 0.0)
    sending_grad = (slot_gate[:, None] * grad_top[token_of_slot]).astype(LOW)
    grad_rows = move_slots(sending_grad.reshape(slot_shape)).reshape(flat_shape)
    grad_route, grad_gate_act, grad_up_act = expert_backward(grad_rows, kept, weights)
    returned_grad = move_slots(grad_route.astype(LOW).reshape(slot_shape)).reshape(flat_shape)
    grad = jnp.sum(
        returned_grad[route_slot].reshape(row_count, top_count, model_width).astype(WIDE), axis=1
    )
    by_expert = jnp.sum(jnp.where(choose, grad_gates[:, :, None], 0.0), axis=1)
    pairs = [(rows, grad_gate_act), (rows, grad_up_act), (grad_rows, kept[2])]
    grads = tuple(owned_grad(weight_total(*pair)) for pair in pairs)
    return (grad, by_expert, mixture, grads)


def local(
    hidden_in,
    cotangent,
    w_query,
    w_key,
    w_value,
    w_out,
    w_router,
    norm_first,
    norm_second,
    query_gain,
    key_gain,
    w_gate,
    w_up,
    w_down,
    expert_ids,
):
    group_index = lax.axis_index(("context", "tensor"))
    row_count, model_width = hidden_in.shape
    column_span = w_query.shape[1]
    expert_count = w_router.shape[1]
    top_count = expert_ids.shape[1]
    capacity = max(2, row_count * top_count * 5 // (4 * expert_count))
    by_blocks = 2 * capacity >= row_count
    device_count = model_width // norm_first.shape[0]

    router_rows = w_router.shape[0]
    small = gather_small(
        jnp.concatenate(
            [
                w_router.reshape(-1),
                norm_first,
                norm_second,
                query_gain,
                key_gain,
                expert_ids.T.reshape(-1).astype(LOW),
            ],
            axis=0,
        )
    )
    hidden_blocks = gather_group(hidden_in)
    hidden_blocks[3], gate_early = sync(hidden_blocks[3], w_gate[0])
    gate_weight = whole_weight(gate_early)
    packed = lax.all_gather(
        jnp.concatenate([w_query, w_key, w_value, w_out], axis=1), "shard", axis=0, tiled=True
    )
    router_size = router_rows * expert_count
    router_full = small[:, :router_size].reshape(model_width, expert_count)
    gains = [
        small[:, router_size + i * router_rows : router_size + (i + 1) * router_rows]
        .reshape(model_width)
        .astype(WIDE)
        for i in range(4)
    ]
    gain_first, gain_second, gain_query, gain_key = gains
    if by_blocks:
        tensors = lax.axis_size("tensor")
        all_ids = small[:, router_size + 4 * router_rows :].astype(jnp.int32)
        all_ids = all_ids.reshape(-1, tensors, top_count, row_count)
        all_ids = lax.dynamic_index_in_dim(all_ids, lax.axis_index("tensor"), 1, False)

    qkv_cols = packed[:, : 3 * column_span]
    out_cols = packed[:, 3 * column_span :]
    inputs = hidden_in.astype(WIDE)
    factor_first = rms_scale(inputs, gain_first)[1]
    low_blocks, pre_blocks = [], []
    for block in hidden_blocks:
        low_block = rms_scale(block.astype(WIDE), gain_first)[0].astype(LOW)
        low_blocks.append(low_block)
        pre_blocks.append(plain(low_block, qkv_cols))
    low_group = jnp.concatenate(low_blocks, axis=0)
    pre = jnp.concatenate(pre_blocks, axis=0)
    group_rows = low_group.shape[0]
    line = jnp.arange(group_rows, dtype=jnp.int32)
    place = ((line // row_count) ^ group_index) * row_count + line % row_count
    cosine, sine = rope_tables(place)
    gain_cols = jnp.stack(
        [
            lax.dynamic_slice_in_dim(gain, group_index * column_span, column_span, 0)
            for gain in (gain_query, gain_key)
        ]
    )

    def over_group(stacked):
        stacked = stacked.reshape(2, 4, -1)
        stacked = stacked + swap(stacked, "tensor")[:, jnp.array([1, 0, 3, 2])]
        stacked = stacked + swap(stacked, "context")[:, jnp.array([2, 3, 0, 1])]
        return stacked.reshape(2, -1)

    own_squares, early_cot = sync(
        jnp.stack(
            [
                jnp.sum(jnp.square(pre[:, i * column_span : (i + 1) * column_span]), axis=1)
                for i in range(2)
            ]
        ),
        cotangent,
    )
    if by_blocks:
        cot_near = gather_chips(early_cot)
    squares = over_group(own_squares)
    query_heads, key_heads, value_heads = prepare(
        pre, squares, gain_cols, cosine, sine, model_width, row_count
    )
    group = group_index[None].astype(jnp.int32)
    blocks, logs = [None] * 4, [None] * 4
    for k in (3, 2, 1, 0):
        blocks[k], logs[k] = attend_block(
            k, group, query_heads, key_heads, value_heads, row_count
        )
    parts = [contract_last(block, out_cols) for block in blocks]
    far_part, gate_weight = sync(parts[3].astype(LOW), gate_weight)
    far = swap(far_part, "tensor")
    far, near_part, part = sync(far, parts[1].astype(LOW), parts[2])
    across = swap((part + far.astype(WIDE)).astype(LOW), "context")
    near = swap(near_part, "tensor")
    if by_blocks:
        across, cot_near = sync(across, cot_near)
    middle = inputs + parts[0] + near.astype(WIDE) + across.astype(WIDE)
    normed_second, factor_second = rms_scale(middle, gain_second)
    low_second = normed_second.astype(LOW)
    router_probs = softmax_rows(plain(low_second, router_full))
    low_second, late_up, late_down = sync(low_second, w_up[0], w_down[0])
    if by_blocks:
        grad_from_experts, grad_router_probs, later = experts_by_blocks(
            low_second,
            cot_near,
            cotangent,
            all_ids,
            router_full,
            gate_weight,
            late_up,
            late_down,
            capacity,
        )
        mixture_parts, rest_parts, gate_grad, down_grad, up_pair = later
    else:
        weights = (gate_weight, whole_weight(late_up), whole_weight(late_down))
        grad_from_experts, grad_router_probs, mixture, expert_grads = experts_by_slots(
            low_second, cotangent, expert_ids, router_probs, weights, capacity
        )
    grad_logits = (
        router_probs
        * (grad_router_probs - jnp.sum(router_probs * grad_router_probs, axis=1, keepdims=True))
    ).astype(LOW)
    grad_router_weight = contract_first(low_second, grad_logits)
    grad_second = grad_from_experts + contract_last(grad_logits, router_full)
    grad_normed_second, grad_gain_second = rms_back(middle, factor_second, gain_second, grad_second)
    grad_middle = cotangent.astype(WIDE) + grad_normed_second
    grad_branch = grad_middle.astype(LOW)
    near_piece, across = swap(grad_branch, "tensor"), swap(grad_branch, "context")

    def piece_back(k, piece, sums):
        grad_queries, *sums = attend_block_back(
            k,
            group,
            query_heads,
            key_heads,
            value_heads,
            plain(piece, out_cols).astype(LOW),
            logs[k],
            sums,
            row_count,
        )
        return (grad_queries, tuple(sums))

    own_query, own_sums = piece_back(0, grad_branch, None)
    if by_blocks:
        rest = sum_chips(rest_parts).astype(LOW)
    if by_blocks:
        across, own_sums, rest, gate_grad, up_mine, up_theirs = sync(
            across, tuple(own_sums), rest, gate_grad, my_grad(*up_pair), their_grad(*up_pair)
        )
        up_halves = halves(up_theirs)
        others = lax.all_gather(rest, "context", axis=0, tiled=False)
    last = swap(across, "tensor")
    near_query, near_sums = piece_back(1, near_piece, own_sums)
    across_query, across_sums = piece_back(2, across, near_sums)
    last, across_sums = sync(last, across_sums)
    if by_blocks:
        last, up_early, mixture_parts = sync(last, up_halves[0], mixture_parts)
        mixture = sum_chips(mixture_parts)
    pieces = [grad_branch, near_piece, across, last]
    last_query, sums = piece_back(3, last, across_sums)
    grad_queries = [own_query, near_query, across_query, last_query]
    grad_query_heads = jnp.concatenate(grad_queries, axis=0)
    out_total = contract_first(pieces[0], blocks[0])
    for k in range(1, 4):
        out_total = out_total + contract_first(pieces[k], blocks[k])
    out_total = out_total.astype(LOW)
    totals, gain_grads = norm_call(
        norm_sums_kernel,
        (grad_query_heads, sums[0], pre, squares, gain_cols, cosine, sine),
        ("rows", "rows", "rows", "line", "whole", "rows", "rows"),
        (((2, group_rows), WIDE, "line"), ((2, column_span), WIDE, "whole")),
        model_width,
        row_count,
    )
    if by_blocks:
        totals, up_first = sync(totals, swap(up_early, "tensor"))
    totals = over_group(totals)
    if by_blocks:
        totals, up_late = sync(totals, up_halves[1])
    (grad_pre,) = norm_call(
        norm_grads_kernel,
        (grad_query_heads, *sums, pre, squares, totals, gain_cols, cosine, sine),
        ("rows", "rows", "rows", "rows", "line", "line", "whole", "rows", "rows"),
        (((group_rows, 3 * column_span), LOW, "rows"),),
        model_width,
        row_count,
    )

    def block_of(values, k):
        return values[k * row_count : (k + 1) * row_count]

    far_part = contract_last(block_of(grad_pre, 3), qkv_cols).astype(LOW)
    if by_blocks:
        far_part, grad_pre, out_total, mixture = sync(far_part, grad_pre, out_total, mixture)
    out_dealt = lax.all_to_all(out_total, "shard", split_axis=0, concat_axis=0, tiled=True)
    far = swap(far_part, "tensor")
    head_total = contract_first(low_group, grad_pre).astype(LOW)
    parts = [contract_last(block_of(grad_pre, k), qkv_cols) for k in range(3)]
    far, head_total, near_part, out_dealt, *parts = sync(
        far, head_total, parts[1].astype(LOW), out_dealt, parts[0], parts[2]
    )
    if by_blocks:
        other = lax.dynamic_index_in_dim(others, lax.axis_index("context") ^ 1, 0, False)
        mixture = mixture + other.astype(WIDE)
    block_output = (middle + mixture).astype(LOW)
    across = swap((parts[1] + far.astype(WIDE)).astype(LOW), "context")
    near = swap(near_part, "tensor")
    head_grads = lax.psum_scatter(head_total, "shard", scatter_dimension=0, tiled=True).astype(WIDE)
    if by_blocks:
        near, across, gate_grad, down_grad, up_late = sync(
            near, across, gate_grad, down_grad, up_late
        )
        up_arrived = jnp.concatenate([up_first, swap(up_late, "tensor")], axis=0)
        expert_grads = (gate_grad, up_mine + up_arrived.astype(WIDE), down_grad)
    out_grad = jnp.sum(
        out_dealt.reshape((lax.axis_size("shard"),) + w_out.shape).astype(WIDE), axis=0
    )
    grad_first = parts[0] + near.astype(WIDE) + across.astype(WIDE)
    grad_normed_first, grad_gain_first = rms_back(inputs, factor_first, gain_first, grad_first)
    grad_input = grad_middle + grad_normed_first
    zero_gain = jnp.zeros((2, model_width), WIDE)
    grad_gains = lax.dynamic_update_slice(zero_gain, gain_grads, (0, group_index * column_span))
    by_device = [
        one.reshape(device_count, -1)
        for one in (grad_router_weight, grad_gain_first, grad_gain_second, grad_gains[0], grad_gains[1])
    ]
    small_grads = scatter_small(jnp.concatenate(by_device, axis=1))
    router_grad = small_grads[:router_size].reshape(router_rows, expert_count)
    gain_totals = small_grads[router_size:].reshape(4, router_rows)
    return (
        block_output,
        grad_input,
        head_grads[:, :column_span],
        head_grads[:, column_span : 2 * column_span],
        head_grads[:, 2 * column_span : 3 * column_span],
        out_grad,
        router_grad,
        *(gain_totals[i] for i in range(4)),
        *(grad.astype(WIDE)[None] for grad in expert_grads),
    )


def solution(mesh):
    rows = P(("shard", "context", "tensor"), None)
    columns = P("shard", ("context", "tensor"))
    vector = P(("shard", "context", "tensor"))
    expert = P(("shard", "context"), None, "tensor")
    return jax.shard_map(
        local,
        mesh=mesh,
        in_specs=(
            (rows, rows)
            + (columns,) * 4
            + (rows,)
            + (vector,) * 4
            + (expert,) * 3
            + (rows,)
        ),
        out_specs=((rows, rows) + (columns,) * 4 + (rows,) + (vector,) * 4 + (expert,) * 3),
        check_vma=False,
    )
```

```python
import jax
import jax.numpy as jnp
from jax import lax
from jax.experimental import pallas as pl
from jax.experimental.pallas import tpu as pltpu
from jax.sharding import PartitionSpec as P

HDIM = 128


EPSILON = 1e-05
MASKED = -1e30
LOW = jnp.bfloat16
WIDE = jnp.float32
SWAP = ((0, 1), (1, 0))


def sync(*values):
    return lax.optimization_barrier(values)


def rms_scale(values, gain):
    factor = lax.rsqrt(jnp.mean(values * values, axis=-1, keepdims=True) + EPSILON)
    return (values * factor * gain, factor)


def rms_back(values, factor, gain, grad_out):
    scaled = grad_out * gain
    mean_term = jnp.mean(scaled * values, axis=-1, keepdims=True)
    grad_values = factor * scaled - values * (factor * factor * factor) * mean_term
    return (grad_values, jnp.sum(grad_out * values * factor, axis=0))


def rope_tables(positions):
    half_size = HDIM // 2
    frequency = 10000.0 ** (-2.0 * jnp.arange(half_size, dtype=WIDE) / HDIM)
    angles = positions.astype(WIDE)[:, None] * frequency[None, :]
    cosine, sine = jnp.cos(angles), jnp.sin(angles)
    return (
        jnp.concatenate([cosine, cosine], axis=1),
        jnp.concatenate([-sine, sine], axis=1),
    )


def contract_last(left, right):
    return lax.dot_general(
        left, right, (((1,), (1,)), ((), ())), preferred_element_type=jnp.float32
    )


def contract_first(left, right):
    return lax.dot_general(
        left, right, (((0,), (0,)), ((), ())), preferred_element_type=jnp.float32
    )


def plain(left, right):
    return jnp.dot(left, right, preferred_element_type=jnp.float32)


def swap(values, axis):
    return lax.ppermute(values, axis, SWAP)


def hop(values, distance):
    count = lax.axis_size("shard")
    return lax.ppermute(values, "shard", tuple((i, i ^ distance) for i in range(count)))


def gather_group(block):
    near = swap(block, "tensor")
    across = swap(block, "context")
    return [block, near, across, swap(across, "tensor")]


def scatter_group(parts):
    far, near = sync(swap(parts[3].astype(LOW), "tensor"), parts[1].astype(LOW))
    across = swap((parts[2] + far.astype(WIDE)).astype(LOW), "context")
    return parts[0] + swap(near, "tensor").astype(WIDE) + across.astype(WIDE)


def over_chips(blocks):
    count = lax.axis_size("shard")
    groups = [list(range(core, count, 2)) for core in range(2)]
    return lax.all_to_all(
        blocks, "shard", split_axis=0, concat_axis=0, axis_index_groups=groups, tiled=True
    )


def gather_chips(block):
    chips = lax.axis_size("shard") // 2
    return over_chips(jnp.broadcast_to(block[None], (chips,) + block.shape))


DEVICES = ("shard", "context", "tensor")


def deal(rows):
    return lax.all_to_all(rows, DEVICES, split_axis=0, concat_axis=0, tiled=True)


def device_total():
    return lax.axis_size("shard") * lax.axis_size("context") * lax.axis_size("tensor")


def gather_small(row):
    return deal(jnp.broadcast_to(row[None], (device_total(), row.shape[0])))


def scatter_small(rows):
    return jnp.sum(deal(rows), axis=0)


def params():
    return pltpu.CompilerParams(vmem_limit_bytes=48 * 1024 * 1024)


def as_column(row, width):
    return jnp.broadcast_to(row, (width, row.shape[1])).T


def turn(values, cosine, sine):
    return values * cosine + pltpu.roll(values, HDIM // 2, 1) * sine


def norm_factors(squares_ref, width):
    factors = lax.rsqrt(squares_ref[...] / width + EPSILON)
    return as_column(factors[0:1], HDIM), as_column(factors[1:2], HDIM)


def prepare_kernel(width, pre_ref, squares_ref, gain_ref, cos_ref, sin_ref, q_ref, k_ref, v_ref):
    span = q_ref.shape[1]
    cosine, sine = cos_ref[...], sin_ref[...]
    factors = norm_factors(squares_ref, width)
    for which, out_ref in ((0, q_ref), (1, k_ref)):
        for first in range(0, span, HDIM):
            cols = slice(which * span + first, which * span + first + HDIM)
            gain = gain_ref[which : which + 1, first : first + HDIM]
            normed = pre_ref[:, cols] * factors[which] * gain
            out_ref[:, first : first + HDIM] = turn(normed, cosine, sine).astype(LOW)
    v_ref[...] = pre_ref[:, 2 * span :].astype(LOW)


def prepare(pre, squares, gain_cols, cosine, sine, width, block):
    rows, total = pre.shape
    span = total // 3
    row_block = lambda cols: pl.BlockSpec((block, cols), lambda i: (i, 0))
    return pl.pallas_call(
        lambda *refs: prepare_kernel(width, *refs),
        grid=(rows // block,),
        in_specs=[
            row_block(total),
            pl.BlockSpec((2, block), lambda i: (0, i)),
            pl.BlockSpec((2, span), lambda i: (0, 0)),
            row_block(HDIM),
            row_block(HDIM),
        ],
        out_specs=[row_block(span)] * 3,
        out_shape=[jax.ShapeDtypeStruct((rows, span), LOW)] * 3,
        compiler_params=params(),
        cost_estimate=pl.CostEstimate(
            flops=10 * rows * total, bytes_accessed=6 * rows * total, transcendentals=0
        ),
    )(pre, squares, gain_cols, cosine, sine)


def visible(group, which, keys, queries):
    line = lax.broadcasted_iota(jnp.int32, (keys, queries), 0)
    key_place = ((line // queries) ^ group) * queries + line % queries
    query_place = (which ^ group) * queries + lax.broadcasted_iota(
        jnp.int32, (keys, queries), 1
    )
    return query_place >= key_place


def dot_last(left, right):
    return lax.dot_general(left, right, (((1,), (1,)), ((), ())), preferred_element_type=WIDE)


def dot_first(left, right):
    return lax.dot_general(left, right, (((0,), (0,)), ((), ())), preferred_element_type=WIDE)


def attend_kernel(which, group_ref, q_ref, k_ref, v_ref, out_ref, log_ref):
    keys, queries = k_ref.shape[0], q_ref.shape[0]
    scores = dot_last(k_ref[...], q_ref[...]) * HDIM ** (-0.5)
    scores = jnp.where(visible(group_ref[0], which, keys, queries), scores, MASKED)
    maximum = jnp.max(scores, axis=0, keepdims=True)
    weights = jnp.exp(scores - maximum)
    total = jnp.sum(weights, axis=0, keepdims=True)
    attn_low = (weights * (1.0 / total)).astype(LOW)
    out_ref[...] = dot_first(v_ref[...], attn_low).T.astype(LOW)
    log_ref[...] = (maximum + jnp.log(total))[None]


def attend_block(which, group, queries, keys, values, block):
    rows, span = queries.shape
    heads = span // HDIM
    whole = pl.BlockSpec((rows, HDIM), lambda h, g: (0, h))
    return pl.pallas_call(
        lambda *refs: attend_kernel(which, *refs),
        grid_spec=pltpu.PrefetchScalarGridSpec(
            num_scalar_prefetch=1,
            grid=(heads,),
            in_specs=[pl.BlockSpec((block, HDIM), lambda h, g: (which, h)), whole, whole],
            out_specs=[
                pl.BlockSpec((block, HDIM), lambda h, g: (0, h)),
                pl.BlockSpec((1, 1, block), lambda h, g: (h, 0, 0)),
            ],
        ),
        out_shape=[
            jax.ShapeDtypeStruct((block, span), LOW),
            jax.ShapeDtypeStruct((heads, 1, block), WIDE),
        ],
        compiler_params=params(),
        cost_estimate=pl.CostEstimate(
            flops=4 * block * rows * span,
            bytes_accessed=4 * rows * span,
            transcendentals=block * rows * heads,
        ),
    )(group, queries, keys, values)


def attend_back_kernel(which, first, group_ref, q_ref, k_ref, v_ref, grad_ref, log_ref, *refs):
    keys, queries = k_ref.shape[0], q_ref.shape[0]
    grad_q_ref, grad_k_ref, grad_v_ref = refs[-3:]
    scores = dot_last(k_ref[...], q_ref[...]) * HDIM ** (-0.5)
    probs = jnp.exp(scores - log_ref[0])
    probs = jnp.where(visible(group_ref[0], which, keys, queries), probs, 0.0)
    grad_probs = dot_last(v_ref[...], grad_ref[...])
    delta = jnp.sum(probs * grad_probs, axis=0, keepdims=True)
    grad_scores = (probs * (grad_probs - delta)).astype(LOW)
    grad_q_ref[...] = (dot_first(k_ref[...], grad_scores).T * HDIM ** (-0.5)).astype(LOW)
    key_part = plain(grad_scores, q_ref[...]) * HDIM ** (-0.5)
    value_part = plain(probs.astype(LOW), grad_ref[...])
    grad_k_ref[...] = key_part if first else refs[0][...] + key_part
    grad_v_ref[...] = value_part if first else refs[1][...] + value_part


def attend_block_back(which, group, queries, keys, values, grad, logs, sums, block):
    rows, span = queries.shape
    heads = span // HDIM
    whole = pl.BlockSpec((rows, HDIM), lambda h, g: (0, h))
    own = pl.BlockSpec((block, HDIM), lambda h, g: (0, h))
    carried = [] if sums is None else list(sums)
    return pl.pallas_call(
        lambda *refs: attend_back_kernel(which, sums is None, *refs),
        grid_spec=pltpu.PrefetchScalarGridSpec(
            num_scalar_prefetch=1,
            grid=(heads,),
            in_specs=[
                pl.BlockSpec((block, HDIM), lambda h, g: (which, h)),
                whole,
                whole,
                own,
                pl.BlockSpec((1, 1, block), lambda h, g: (h, 0, 0)),
            ]
            + [whole] * len(carried),
            out_specs=[own, whole, whole],
        ),
        out_shape=[
            jax.ShapeDtypeStruct((block, span), LOW),
            jax.ShapeDtypeStruct((rows, span), WIDE),
            jax.ShapeDtypeStruct((rows, span), WIDE),
        ],
        compiler_params=params(),
        cost_estimate=pl.CostEstimate(
            flops=10 * block * rows * span,
            bytes_accessed=20 * rows * span,
            transcendentals=block * rows * heads,
        ),
    )(group, queries, keys, values, grad, logs, *carried)


def turned_back(which, first, grads, cosine, sine):
    values = grads[which][:, first : first + HDIM].astype(WIDE)
    return turn(values, cosine, -sine)


def norm_sums_kernel(
    width, gq_ref, gk_ref, pre_ref, squares_ref, gain_ref, cos_ref, sin_ref, total_ref, col_ref
):
    span = gq_ref.shape[1]
    cosine, sine = cos_ref[...], sin_ref[...]
    factors = norm_factors(squares_ref, width)

    @pl.when(pl.program_id(0) == 0)
    def _():
        col_ref[...] = jnp.zeros_like(col_ref)

    for which in range(2):
        total = jnp.zeros(cosine.shape, WIDE)
        for first in range(0, span, HDIM):
            grad = turned_back(which, first, (gq_ref, gk_ref), cosine, sine)
            cols = slice(which * span + first, which * span + first + HDIM)
            product = grad * pre_ref[:, cols]
            total = total + product * gain_ref[which : which + 1, first : first + HDIM]
            col_ref[which : which + 1, first : first + HDIM] += jnp.sum(
                product * factors[which], axis=0, keepdims=True
            )
        total_ref[which : which + 1, :] = jnp.sum(total.T, axis=0, keepdims=True)


def norm_grads_kernel(
    width,
    gq_ref,
    gk_ref,
    gv_ref,
    pre_ref,
    squares_ref,
    total_ref,
    gain_ref,
    cos_ref,
    sin_ref,
    out_ref,
):
    span = gq_ref.shape[1]
    cosine, sine = cos_ref[...], sin_ref[...]
    factors = norm_factors(squares_ref, width)
    for which in range(2):
        factor = factors[which]
        mean = as_column(total_ref[which : which + 1] / width, HDIM)
        pull = factor * factor * factor * mean
        for first in range(0, span, HDIM):
            grad = turned_back(which, first, (gq_ref, gk_ref), cosine, sine)
            cols = slice(which * span + first, which * span + first + HDIM)
            scaled = grad * gain_ref[which : which + 1, first : first + HDIM]
            out_ref[:, cols] = (factor * scaled - pre_ref[:, cols] * pull).astype(LOW)
    out_ref[:, 2 * span :] = gv_ref[...].astype(LOW)


def norm_call(body, operands, kinds, outs, width, block):
    def spec(shape, kind):
        if kind == "rows":
            return pl.BlockSpec((block, shape[1]), lambda i: (i, 0))
        if kind == "line":
            return pl.BlockSpec((shape[0], block), lambda i: (0, i))
        return pl.BlockSpec(shape, lambda i: (0, 0))

    size = sum(o.size * o.dtype.itemsize for o in operands)
    return pl.pallas_call(
        lambda *refs: body(width, *refs),
        grid=(operands[0].shape[0] // block,),
        in_specs=[spec(o.shape, kind) for o, kind in zip(operands, kinds)],
        out_specs=[spec(shape, kind) for shape, _, kind in outs],
        out_shape=[jax.ShapeDtypeStruct(shape, dtype) for shape, dtype, _ in outs],
        compiler_params=params(),
        cost_estimate=pl.CostEstimate(flops=4 * size, bytes_accessed=size, transcendentals=0),
    )(*operands)


def silu_parts(gate_act):
    sigmoid_value = jax.nn.sigmoid(gate_act)
    return (gate_act * sigmoid_value, sigmoid_value)


def expert_hidden(rows, weights):
    gate_act = plain(rows, weights[0])
    up_act = plain(rows, weights[1])
    return (gate_act, up_act, (silu_parts(gate_act)[0] * up_act).astype(LOW))


def expert_produce(hidden_act, weights):
    return contract_last(hidden_act, weights[2]).astype(LOW)


def expert_forward(rows, weights):
    kept = expert_hidden(rows, weights)
    return (expert_produce(kept[2], weights), kept)


def expert_backward(grad_rows, kept, weights):
    gate_weight, up_weight, down_weight = weights
    gate_act, up_act, hidden_act = kept
    grad_hidden = plain(grad_rows, down_weight)
    activated, sigmoid_value = silu_parts(gate_act)
    grad_gate_act = (
        grad_hidden * up_act * sigmoid_value * (1.0 + gate_act * (1.0 - sigmoid_value))
    ).astype(LOW)
    grad_up_act = (grad_hidden * activated).astype(LOW)
    grad_route = contract_last(grad_gate_act, gate_weight) + contract_last(grad_up_act, up_weight)
    return (grad_route, grad_gate_act, grad_up_act)


def weight_total(left, right):
    return contract_first(left, right).astype(LOW)


def columns_of(values, tensor):
    half = values.shape[1] // 2
    return lax.dynamic_slice_in_dim(values, tensor * half, half, 1)


def their_grad(left, right):
    return contract_first(left, columns_of(right, 1 - lax.axis_index("tensor"))).astype(LOW)


def my_grad(left, right):
    return contract_first(left, columns_of(right, lax.axis_index("tensor")))


def owned_grad(total):
    return lax.psum_scatter(total, "tensor", scatter_dimension=1, tiled=True)


def halves(values):
    half = values.shape[0] // 2
    return (values[:half], values[half:])


def whole_weight(held):
    return lax.all_gather(held, "tensor", axis=1, tiled=True)


def softmax_rows(logits):
    weights = jnp.exp(logits - jnp.max(logits, axis=-1, keepdims=True))
    return weights / jnp.sum(weights, axis=-1, keepdims=True)


def pick_rows(picks, other_picks, blocks):
    pick = jnp.concatenate([picks, other_picks], axis=1)
    chosen = jnp.einsum("bst,btd->bsd", pick, blocks, preferred_element_type=jnp.float32)
    chosen = chosen.astype(LOW)
    capacity, width = picks.shape[1], blocks.shape[2]
    kept = chosen[:, :capacity].reshape(-1, width)
    arrived = hop(chosen[:, capacity:].reshape(-1, width), 1)
    return jnp.concatenate([kept, arrived], axis=0)


def slot_picks(ids, expert, capacity):
    routed = jnp.any(ids == expert, axis=1)
    tokens = ids.shape[2]
    line = jnp.arange(tokens, dtype=jnp.int32)
    earlier = (line[:, None] < line[None, :]).astype(LOW)
    position = plain(routed.astype(LOW), earlier).astype(jnp.int32)
    position = jnp.where(routed, position, -1)
    slots = jnp.arange(capacity, dtype=jnp.int32)
    return (position[:, None, :] == slots[None, :, None]).astype(LOW)


def chip_parts(rows, picks, other_picks):
    half = rows.shape[0] // 2
    return combine(rows[:half], hop(rows[half:], 1), picks, other_picks)


def combine(kept, arrived, picks, other_picks):
    shape = picks.shape[:2] + kept.shape[1:]
    both = jnp.concatenate([kept.reshape(shape), arrived.reshape(shape)], axis=1)
    pick = jnp.concatenate([picks, other_picks], axis=1)
    parts = jnp.einsum("bst,bsd->btd", pick, both, preferred_element_type=jnp.float32)
    return parts.astype(LOW)


def sum_chips(parts):
    return jnp.sum(over_chips(parts).astype(WIDE), axis=0)


def experts_by_blocks(
    low_second, cot_near, cotangent, all_ids, router, gate_weight, w_up, w_down, capacity
):
    shard, context = lax.axis_index("shard"), lax.axis_index("context")
    contexts = lax.axis_size("context")
    expert = shard * contexts + context
    other_expert = (shard ^ 1) * contexts + context
    token_count = low_second.shape[0]
    chips = lax.axis_size("shard") // 2
    same_core = 2 * jnp.arange(chips, dtype=jnp.int32) + (shard & 1)
    picks = []
    for turn in range(2):
        ids = jnp.take(all_ids, same_core * contexts + (context ^ turn), axis=0)
        far_ids = jnp.take(all_ids, (same_core ^ 1) * contexts + (context ^ turn), axis=0)
        picks.append(
            (
                slot_picks(ids, expert, capacity),
                slot_picks(ids, other_expert, capacity),
                slot_picks(far_ids, expert, capacity),
            )
        )

    def arrive(turn, rows):
        probs = softmax_rows(plain(rows, router))
        mine = jnp.arange(probs.shape[1], dtype=jnp.int32)[None, :] == expert
        return jnp.sum(jnp.where(mine, probs, 0.0), axis=1, keepdims=True)

    def leave(turn, produced, cot_rows, gate):
        cot_wide = cot_rows.astype(WIDE)
        produced_wide = produced.astype(WIDE)
        slot_grad = jnp.sum(produced_wide * cot_wide, axis=1)
        all_picks = jnp.concatenate([picks[turn][0], picks[turn][2]], axis=0).astype(WIDE)
        gate_grad = jnp.sum(all_picks * slot_grad.reshape(2 * chips, capacity)[:, :, None], axis=1)
        return (gate_grad, (gate * cot_wide).astype(LOW), (gate * produced_wide).astype(LOW))

    up_weight = whole_weight(w_up)
    near_chunk, across, w_down, cot_near, cotangent = sync(
        gather_chips(low_second), swap(low_second, "context"), w_down, cot_near, cotangent
    )
    cot_across = swap(cotangent, "context")
    near_rows = pick_rows(*picks[0][:2], near_chunk)
    down_weight = whole_weight(w_down)
    weights = (gate_weight, up_weight, down_weight)
    near_kept = expert_hidden(near_rows, weights)
    near_hidden, far_chunk, cot_across = sync(near_kept[2], gather_chips(across), cot_across)
    near_kept = near_kept[:2] + (near_hidden,)
    cot_far = gather_chips(cot_across)
    far_rows = pick_rows(*picks[1][:2], far_chunk)
    far_rows, down_weight = sync(far_rows, down_weight)
    weights = (gate_weight, up_weight, down_weight)
    far_kept = expert_hidden(far_rows, weights)
    near_cot, far_cot = pick_rows(*picks[0][:2], cot_near), pick_rows(*picks[1][:2], cot_far)
    gate = arrive(0, near_rows)
    produced = expert_produce(near_hidden, weights)
    near_gate_grad, near_grad_rows, weighted = leave(0, produced, near_cot, gate)
    mixture_parts = chip_parts(weighted, *picks[0][:2])
    gate = arrive(1, far_rows)
    produced = expert_produce(far_kept[2], weights)
    far_gate_grad, far_grad_rows, far_weighted = leave(1, produced, far_cot, gate)
    rest_parts = chip_parts(far_weighted, *picks[1][:2])
    lines = jnp.stack([near_gate_grad, far_gate_grad], axis=1)
    lines = jnp.where(context == 0, lines, lines[:, ::-1])
    mine, far = lines[:chips], lines[chips:]
    low_core = (shard & 1) == 0
    lines = jnp.stack([jnp.where(low_core, mine, far), jnp.where(low_core, far, mine)], axis=1)
    lines = lines.reshape(-1, token_count)
    by_expert = lax.all_to_all(lines, ("shard", "context"), split_axis=0, concat_axis=0, tiled=True)

    def both(near, far):
        return jnp.concatenate([near, far], axis=0)

    far_route, far_gate_act, far_up_act = expert_backward(far_grad_rows, far_kept, weights)
    far_route, near_grad_rows, far_grad_rows = sync(far_route, near_grad_rows, far_grad_rows)
    down_pair = (both(near_grad_rows, far_grad_rows), both(near_kept[2], far_kept[2]))
    down_total = weight_total(*down_pair)
    far_parts = chip_parts(far_route.astype(LOW), *picks[1][:2])
    near_grad_rows, far_parts, by_expert, down_total = sync(
        near_grad_rows, far_parts, by_expert, down_total
    )
    down_grad = owned_grad(down_total)
    near_route, near_gate_act, near_up_act = expert_backward(near_grad_rows, near_kept, weights)
    near_route = near_route.astype(LOW)
    near_half = near_route.shape[0] // 2
    near_swapped = hop(near_route[near_half:], 1)
    near_route, near_gate_act = sync(near_route, near_gate_act)
    all_rows = both(near_rows, far_rows)
    near_swapped, far_grad, near_up_act, gate_total = sync(
        near_swapped,
        sum_chips(far_parts).astype(LOW),
        near_up_act,
        weight_total(all_rows, both(near_gate_act, far_gate_act)),
    )
    gate_grad = owned_grad(gate_total)
    near_parts = combine(near_route[:near_half], near_swapped, *picks[0][:2])
    far_arrived = swap(far_grad, "context")
    far_arrived, mixture_parts, rest_parts = sync(far_arrived, mixture_parts, rest_parts)
    grad, mixture_parts, rest_parts, down_grad, far_up_act = sync(
        sum_chips(near_parts) + far_arrived.astype(WIDE),
        mixture_parts,
        rest_parts,
        down_grad,
        far_up_act,
    )
    up_pair = (all_rows, both(near_up_act, far_up_act))
    later = (mixture_parts, rest_parts, gate_grad, down_grad, up_pair)
    return (grad, by_expert.T, later)


def move_slots(buffer):
    return lax.all_to_all(buffer, ("shard", "context"), split_axis=0, concat_axis=0, tiled=True)


def experts_by_slots(low_second, cotangent, expert_ids, router_probs, weights, capacity):
    row_count, model_width = low_second.shape
    expert_count = router_probs.shape[1]
    top_count = expert_ids.shape[1]
    choose = expert_ids[:, :, None] == jnp.arange(expert_count, dtype=jnp.int32)[None, None, :]
    gate_probs = jnp.sum(jnp.where(choose, router_probs[:, None, :], 0.0), axis=2)
    route_total = row_count * top_count
    flat_ids = expert_ids.reshape(-1)
    onehot = (flat_ids[:, None] == jnp.arange(expert_count, dtype=jnp.int32)[None, :]).astype(
        jnp.int32
    )
    before = jnp.cumsum(onehot, axis=0) - onehot
    route_slot = flat_ids * capacity + jnp.sum(before * onehot, axis=1)
    route_of_slot = (
        jnp.full((expert_count * capacity,), route_total, jnp.int32)
        .at[route_slot]
        .set(jnp.arange(route_total, dtype=jnp.int32))
    )
    filled = route_of_slot < route_total
    route_clipped = jnp.minimum(route_of_slot, route_total - 1)
    token_of_slot = route_clipped // top_count
    slot_shape = (expert_count, capacity, model_width)
    flat_shape = (expert_count * capacity, model_width)
    sending = jnp.where(filled[:, None], low_second[token_of_slot], jnp.zeros((), LOW))
    rows = move_slots(sending.reshape(slot_shape)).reshape(flat_shape)
    produced, kept = expert_forward(rows, weights)
    returned = move_slots(produced.reshape(slot_shape)).reshape(flat_shape)
    chosen = returned[route_slot].reshape(row_count, top_count, model_width).astype(WIDE)
    mixture = jnp.sum(gate_probs[:, :, None] * chosen, axis=1)
    grad_top = cotangent.astype(WIDE)
    grad_gates = jnp.sum(chosen * grad_top[:, None, :], axis=2)
    slot_gate = jnp.where(filled, gate_probs.reshape(-1)[route_clipped], 0.0)
    sending_grad = (slot_gate[:, None] * grad_top[token_of_slot]).astype(LOW)
    grad_rows = move_slots(sending_grad.reshape(slot_shape)).reshape(flat_shape)
    grad_route, grad_gate_act, grad_up_act = expert_backward(grad_rows, kept, weights)
    returned_grad = move_slots(grad_route.astype(LOW).reshape(slot_shape)).reshape(flat_shape)
    grad = jnp.sum(
        returned_grad[route_slot].reshape(row_count, top_count, model_width).astype(WIDE), axis=1
    )
    by_expert = jnp.sum(jnp.where(choose, grad_gates[:, :, None], 0.0), axis=1)
    pairs = [(rows, grad_gate_act), (rows, grad_up_act), (grad_rows, kept[2])]
    grads = tuple(owned_grad(weight_total(*pair)) for pair in pairs)
    return (grad, by_expert, mixture, grads)


def local(
    hidden_in,
    cotangent,
    w_query,
    w_key,
    w_value,
    w_out,
    w_router,
    norm_first,
    norm_second,
    query_gain,
    key_gain,
    w_gate,
    w_up,
    w_down,
    expert_ids,
):
    group_index = lax.axis_index(("context", "tensor"))
    row_count, model_width = hidden_in.shape
    column_span = w_query.shape[1]
    expert_count = w_router.shape[1]
    top_count = expert_ids.shape[1]
    capacity = max(2, row_count * top_count * 5 // (4 * expert_count))
    by_blocks = 2 * capacity >= row_count
    device_count = model_width // norm_first.shape[0]

    router_rows = w_router.shape[0]
    small = gather_small(
        jnp.concatenate(
            [
                w_router.reshape(-1),
                norm_first,
                norm_second,
                query_gain,
                key_gain,
                expert_ids.T.reshape(-1).astype(LOW),
            ],
            axis=0,
        )
    )
    hidden_blocks = gather_group(hidden_in)
    hidden_blocks[3], gate_early = sync(hidden_blocks[3], w_gate[0])
    gate_weight = whole_weight(gate_early)
    packed = lax.all_gather(
        jnp.concatenate([w_query, w_key, w_value, w_out], axis=1), "shard", axis=0, tiled=True
    )
    router_size = router_rows * expert_count
    router_full = small[:, :router_size].reshape(model_width, expert_count)
    gains = [
        small[:, router_size + i * router_rows : router_size + (i + 1) * router_rows]
        .reshape(model_width)
        .astype(WIDE)
        for i in range(4)
    ]
    gain_first, gain_second, gain_query, gain_key = gains
    if by_blocks:
        tensors = lax.axis_size("tensor")
        all_ids = small[:, router_size + 4 * router_rows :].astype(jnp.int32)
        all_ids = all_ids.reshape(-1, tensors, top_count, row_count)
        all_ids = lax.dynamic_index_in_dim(all_ids, lax.axis_index("tensor"), 1, False)

    qkv_cols = packed[:, : 3 * column_span]
    out_cols = packed[:, 3 * column_span :]
    inputs = hidden_in.astype(WIDE)
    factor_first = rms_scale(inputs, gain_first)[1]
    low_blocks, pre_blocks = [], []
    for block in hidden_blocks:
        low_block = rms_scale(block.astype(WIDE), gain_first)[0].astype(LOW)
        low_blocks.append(low_block)
        pre_blocks.append(plain(low_block, qkv_cols))
    low_group = jnp.concatenate(low_blocks, axis=0)
    pre = jnp.concatenate(pre_blocks, axis=0)
    group_rows = low_group.shape[0]
    line = jnp.arange(group_rows, dtype=jnp.int32)
    place = ((line // row_count) ^ group_index) * row_count + line % row_count
    cosine, sine = rope_tables(place)
    gain_cols = jnp.stack(
        [
            lax.dynamic_slice_in_dim(gain, group_index * column_span, column_span, 0)
            for gain in (gain_query, gain_key)
        ]
    )

    def over_group(stacked):
        stacked = stacked.reshape(2, 4, -1)
        stacked = stacked + swap(stacked, "tensor")[:, jnp.array([1, 0, 3, 2])]
        stacked = stacked + swap(stacked, "context")[:, jnp.array([2, 3, 0, 1])]
        return stacked.reshape(2, -1)

    own_squares, early_cot = sync(
        jnp.stack(
            [
                jnp.sum(jnp.square(pre[:, i * column_span : (i + 1) * column_span]), axis=1)
                for i in range(2)
            ]
        ),
        cotangent,
    )
    if by_blocks:
        cot_near = gather_chips(early_cot)
    squares = over_group(own_squares)
    query_heads, key_heads, value_heads = prepare(
        pre, squares, gain_cols, cosine, sine, model_width, row_count
    )
    group = group_index[None].astype(jnp.int32)
    blocks, logs = [None] * 4, [None] * 4
    for k in (3, 2, 1, 0):
        blocks[k], logs[k] = attend_block(
            k, group, query_heads, key_heads, value_heads, row_count
        )
    parts = [contract_last(block, out_cols) for block in blocks]
    far_part, gate_weight = sync(parts[3].astype(LOW), gate_weight)
    far = swap(far_part, "tensor")
    far, near_part, part = sync(far, parts[1].astype(LOW), parts[2])
    across = swap((part + far.astype(WIDE)).astype(LOW), "context")
    near = swap(near_part, "tensor")
    if by_blocks:
        across, cot_near = sync(across, cot_near)
    middle = inputs + parts[0] + near.astype(WIDE) + across.astype(WIDE)
    normed_second, factor_second = rms_scale(middle, gain_second)
    low_second = normed_second.astype(LOW)
    router_probs = softmax_rows(plain(low_second, router_full))
    low_second, late_up, late_down = sync(low_second, w_up[0], w_down[0])
    if by_blocks:
        grad_from_experts, grad_router_probs, later = experts_by_blocks(
            low_second,
            cot_near,
            cotangent,
            all_ids,
            router_full,
            gate_weight,
            late_up,
            late_down,
            capacity,
        )
        mixture_parts, rest_parts, gate_grad, down_grad, up_pair = later
    else:
        weights = (gate_weight, whole_weight(late_up), whole_weight(late_down))
        grad_from_experts, grad_router_probs, mixture, expert_grads = experts_by_slots(
            low_second, cotangent, expert_ids, router_probs, weights, capacity
        )
    grad_logits = (
        router_probs
        * (grad_router_probs - jnp.sum(router_probs * grad_router_probs, axis=1, keepdims=True))
    ).astype(LOW)
    grad_router_weight = contract_first(low_second, grad_logits)
    grad_second = grad_from_experts + contract_last(grad_logits, router_full)
    grad_normed_second, grad_gain_second = rms_back(middle, factor_second, gain_second, grad_second)
    grad_middle = cotangent.astype(WIDE) + grad_normed_second
    grad_branch = grad_middle.astype(LOW)
    near_piece, across = swap(grad_branch, "tensor"), swap(grad_branch, "context")

    def piece_back(k, piece, sums):
        grad_queries, *sums = attend_block_back(
            k,
            group,
            query_heads,
            key_heads,
            value_heads,
            plain(piece, out_cols).astype(LOW),
            logs[k],
            sums,
            row_count,
        )
        return (grad_queries, tuple(sums))

    own_query, own_sums = piece_back(0, grad_branch, None)
    if by_blocks:
        rest = sum_chips(rest_parts).astype(LOW)
    if by_blocks:
        across, own_sums, rest, gate_grad, up_mine, up_theirs = sync(
            across, tuple(own_sums), rest, gate_grad, my_grad(*up_pair), their_grad(*up_pair)
        )
        up_halves = halves(up_theirs)
        others = lax.all_gather(rest, "context", axis=0, tiled=False)
    last = swap(across, "tensor")
    near_query, near_sums = piece_back(1, near_piece, own_sums)
    across_query, across_sums = piece_back(2, across, near_sums)
    last, across_sums = sync(last, across_sums)
    if by_blocks:
        last, up_early, mixture_parts = sync(last, up_halves[0], mixture_parts)
        mixture = sum_chips(mixture_parts)
    pieces = [grad_branch, near_piece, across, last]
    last_query, sums = piece_back(3, last, across_sums)
    grad_queries = [own_query, near_query, across_query, last_query]
    grad_query_heads = jnp.concatenate(grad_queries, axis=0)
    out_total = contract_first(pieces[0], blocks[0])
    for k in range(1, 4):
        out_total = out_total + contract_first(pieces[k], blocks[k])
    out_total = out_total.astype(LOW)
    totals, gain_grads = norm_call(
        norm_sums_kernel,
        (grad_query_heads, sums[0], pre, squares, gain_cols, cosine, sine),
        ("rows", "rows", "rows", "line", "whole", "rows", "rows"),
        (((2, group_rows), WIDE, "line"), ((2, column_span), WIDE, "whole")),
        model_width,
        row_count,
    )
    if by_blocks:
        totals, up_first = sync(totals, swap(up_early, "tensor"))
    totals = over_group(totals)
    if by_blocks:
        totals, up_late = sync(totals, up_halves[1])
    (grad_pre,) = norm_call(
        norm_grads_kernel,
        (grad_query_heads, *sums, pre, squares, totals, gain_cols, cosine, sine),
        ("rows", "rows", "rows", "rows", "line", "line", "whole", "rows", "rows"),
        (((group_rows, 3 * column_span), LOW, "rows"),),
        model_width,
        row_count,
    )

    def block_of(values, k):
        return values[k * row_count : (k + 1) * row_count]

    far_part = contract_last(block_of(grad_pre, 3), qkv_cols).astype(LOW)
    if by_blocks:
        far_part, grad_pre, out_total, mixture = sync(far_part, grad_pre, out_total, mixture)
    out_dealt = lax.all_to_all(out_total, "shard", split_axis=0, concat_axis=0, tiled=True)
    far = swap(far_part, "tensor")
    head_total = contract_first(low_group, grad_pre).astype(LOW)
    parts = [contract_last(block_of(grad_pre, k), qkv_cols) for k in range(3)]
    far, head_total, near_part, out_dealt, *parts = sync(
        far, head_total, parts[1].astype(LOW), out_dealt, parts[0], parts[2]
    )
    if by_blocks:
        other = lax.dynamic_index_in_dim(others, lax.axis_index("context") ^ 1, 0, False)
        mixture = mixture + other.astype(WIDE)
    block_output = (middle + mixture).astype(LOW)
    across = swap((parts[1] + far.astype(WIDE)).astype(LOW), "context")
    near = swap(near_part, "tensor")
    head_grads = lax.psum_scatter(head_total, "shard", scatter_dimension=0, tiled=True).astype(WIDE)
    if by_blocks:
        near, gate_grad, down_grad, up_late = sync(near, gate_grad, down_grad, up_late)
        up_second = swap(up_late, "tensor")
    out_grad = jnp.sum(
        out_dealt.reshape((lax.axis_size("shard"),) + w_out.shape).astype(WIDE), axis=0
    )
    grad_first = parts[0] + near.astype(WIDE) + across.astype(WIDE)
    grad_normed_first, grad_gain_first = rms_back(inputs, factor_first, gain_first, grad_first)
    grad_input = grad_middle + grad_normed_first
    zero_gain = jnp.zeros((2, model_width), WIDE)
    grad_gains = lax.dynamic_update_slice(zero_gain, gain_grads, (0, group_index * column_span))
    by_device = [
        one.reshape(device_count, -1)
        for one in (grad_router_weight, grad_gain_first, grad_gain_second, grad_gains[0], grad_gains[1])
    ]
    small_rows = jnp.concatenate(by_device, axis=1)
    if by_blocks:
        small_rows, up_second = sync(small_rows, up_second)
        up_arrived = jnp.concatenate([up_first, up_second], axis=0)
        expert_grads = (gate_grad, up_mine + up_arrived.astype(WIDE), down_grad)
    small_grads = scatter_small(small_rows)
    router_grad = small_grads[:router_size].reshape(router_rows, expert_count)
    gain_totals = small_grads[router_size:].reshape(4, router_rows)
    return (
        block_output,
        grad_input,
        head_grads[:, :column_span],
        head_grads[:, column_span : 2 * column_span],
        head_grads[:, 2 * column_span : 3 * column_span],
        out_grad,
        router_grad,
        *(gain_totals[i] for i in range(4)),
        *(grad.astype(WIDE)[None] for grad in expert_grads),
    )


def solution(mesh):
    rows = P(("shard", "context", "tensor"), None)
    columns = P("shard", ("context", "tensor"))
    vector = P(("shard", "context", "tensor"))
    expert = P(("shard", "context"), None, "tensor")
    return jax.shard_map(
        local,
        mesh=mesh,
        in_specs=(
            (rows, rows)
            + (columns,) * 4
            + (rows,)
            + (vector,) * 4
            + (expert,) * 3
            + (rows,)
        ),
        out_specs=((rows, rows) + (columns,) * 4 + (rows,) + (vector,) * 4 + (expert,) * 3),
        check_vma=False,
    )
```
